32 devices in a mesh: leaf: 8 (over z, core), row: 4 (over y, x).
Axes of the slice: x: 2, y: 2, z: 4, core: 2. Of those that a mesh axis runs over, the one named last changes fastest.
Arguments:
- inputs: bfloat16 [8, 1024, 2048], P('leaf', 'row'), may hold values from -6 to 6
- cotangent: bfloat16 [8, 1024, 2048], P('leaf', 'row'), may hold values from -6 to 6
- seg_lengths: int32 [8, 13], P('leaf'), may hold values from 1 to 256, 1024 in all within a row
- seg_parents: int32 [8, 13], P('leaf'), may hold values from 0 to 4, as said below
- w_query: float32 [2048, 2048], P(('leaf', 'row')), may hold values from -0.125 to 0.125
- w_key: float32 [2048, 2048], P(('leaf', 'row')), may hold values from -0.125 to 0.125
- w_value: float32 [2048, 2048], P(('leaf', 'row')), may hold values from -0.125 to 0.125
- w_output: float32 [2048, 2048], P(('leaf', 'row')), may hold values from -0.125 to 0.125
- gain_query: float32 [2048], P(('leaf', 'row')), may hold values from 0.1 to 1.9
- gain_key: float32 [2048], P(('leaf', 'row')), may hold values from 0.1 to 1.9
- gain_attn: float32 [2048], P(('leaf', 'row')), may hold values from 0.1 to 1.9
- w_gate: float32 [2048, 8192], P(('leaf', 'row')), may hold values from -0.125 to 0.125
- w_up: float32 [2048, 8192], P(('leaf', 'row')), may hold values from -0.125 to 0.125
- w_down: float32 [2048, 8192], P(('leaf', 'row')), may hold values from -0.0625 to 0.0625
- gain_mlp: float32 [2048], P(('leaf', 'row')), may hold values from 0.1 to 1.9
Outputs:
- outputs: bfloat16 [8, 1024, 2048], P('leaf', 'row')
- grad_inputs: bfloat16 [8, 1024, 2048], P('leaf', 'row')
- grad_query: float32 [2048, 2048], P(('leaf', 'row'))
- grad_key: float32 [2048, 2048], P(('leaf', 'row'))
- grad_value: float32 [2048, 2048], P(('leaf', 'row'))
- grad_output: float32 [2048, 2048], P(('leaf', 'row'))
- grad_gain_query: float32 [2048], P(('leaf', 'row'))
- grad_gain_key: float32 [2048], P(('leaf', 'row'))
- grad_gain_attn: float32 [2048], P(('leaf', 'row'))
- grad_gate: float32 [2048, 8192], P(('leaf', 'row'))
- grad_up: float32 [2048, 8192], P(('leaf', 'row'))
- grad_down: float32 [2048, 8192], P(('leaf', 'row'))
- grad_gain_mlp: float32 [2048], P(('leaf', 'row'))
The draws below stay inside these ranges and needn't reach their ends.
Inputs may be any that keep to these rules, and one draw needn't show every extreme that they name: `seg_lengths`: each tree's lengths sum to 1024; in every tree the longest segment has exactly 256 tokens. `seg_parents`: segment 0 of a tree is its root and its own parent; segments 1 to 4 have parent 0; every later segment's parent is one of segments 1 to 4.
All inputs are finite; a program needn't handle non-finite values.
Results may differ from the reference program's by a relative error of at most 0.018.
Values may be sent and summed in bfloat16 or wider, within the bound.
A program may use at most 704 MiB of HBM per device.

```python
import math
import jax
import jax.numpy as jnp
import numpy as np
from jax import lax

D = 2048
HEADS = 16
HEAD_DIM = 128
FF = 8192
BRANCHES = 4
TWIGS = 2
TREE_LEN = 1024
NSEG = 13
LONGEST = 256
TREES = 8


def draw_seg_parents(key, part):
    leaf_parents = jax.random.randint(key, (TREES, BRANCHES * TWIGS), 1, BRANCHES + 1, dtype=jnp.int32)
    return jnp.concatenate([jnp.zeros((TREES, 1 + BRANCHES), jnp.int32), leaf_parents], axis=1)


def block_levels(own_key, shape, cuts, low, top_value):
    def one(dim, parts):
        draws = jax.random.uniform(jax.random.fold_in(jax.random.fold_in(own_key, 6), dim), (parts,), jnp.float32, low / len(cuts), top_value / len(cuts))
        return jnp.repeat(jnp.exp(draws), shape[dim] // parts).reshape((-1,) + (1,) * (len(shape) - dim - 1))

    loudness = one(*cuts[0])
    for cut in cuts[1:]:
        loudness = loudness * one(*cut)
    return loudness


def length_profile(amount, total, limit, skew):
    portions = [(1 << 20) // math.isqrt(rank ** skew) + 1 for rank in range(2, amount + 1)]
    surplus, given = total - limit - (amount - 1), [1] * (amount - 1)
    while surplus > 0:
        movable = [i for i in range(amount - 1) if given[i] < limit]
        mass, left = sum([portions[i] for i in movable]), surplus
        for i in movable:
            more = min(limit - given[i], max(1, left * portions[i] // mass), surplus)
            given[i] = given[i] + more
            surplus = surplus - more
    return np.array([limit] + given)


def ragged_sizes(stream_key, count, total, most, skew):
    if count == 2:
        one = jax.random.randint(stream_key, (), max(1, total - most), min(most, total - 1) + 1)
        return jnp.stack([one, total - one])
    tallies = jnp.asarray(length_profile(count, total, most, skew), jnp.int32)
    pairs = (count - 1) // 2
    giver, sink = tallies[1:1 + 2 * pairs:2], tallies[2:2 + 2 * pairs:2]
    room = jnp.minimum(giver - 1, most - sink)
    shifted = jax.random.randint(jax.random.fold_in(stream_key, 1), (pairs,), 0, 1 << 20) % (room + 1)
    tallies = tallies.at[1:1 + 2 * pairs:2].set(giver - shifted).at[2:2 + 2 * pairs:2].set(sink + shifted)
    return tallies[jax.random.permutation(jax.random.fold_in(stream_key, 2), count)]


def bell_draw(stream_key, shape, spread, reach, pieces=(), kind=jnp.bfloat16):
    values = spread * jax.random.normal(stream_key, shape, jnp.float32)
    if pieces:
        values = values * block_levels(stream_key, shape, pieces, -0.22, 0.18)
    return jnp.clip(values, -reach, reach).astype(kind)


def setup_inputs(seed: int = 0) -> dict:
    key_list = jax.random.split(jax.random.key(seed), 16)
    return {
        "inputs": bell_draw(key_list[0], (TREES, TREE_LEN, D), 1.0, 6.0, ((0, 8), (1, 4))),
        "cotangent": bell_draw(key_list[1], (TREES, TREE_LEN, D), 1.0, 6.0, ((0, 8), (1, 4))),
        "seg_lengths": jax.vmap(lambda own: ragged_sizes(own, NSEG, TREE_LEN, LONGEST, 2))(jax.random.split(key_list[2], TREES)).reshape((TREES, NSEG)).astype(jnp.int32),
        "seg_parents": draw_seg_parents(jax.random.fold_in(key_list[15], 71), 0),
        "w_query": bell_draw(key_list[4], (D, D), D ** -0.5, 0.125, ((0, 32),), jnp.float32),
        "w_key": bell_draw(key_list[5], (D, D), D ** -0.5, 0.125, ((0, 32),), jnp.float32),
        "w_value": bell_draw(key_list[6], (D, D), D ** -0.5, 0.125, ((0, 32),), jnp.float32),
        "w_output": bell_draw(key_list[7], (D, D), D ** -0.5, 0.125, ((0, 32),), jnp.float32),
        "gain_query": jnp.clip(1.0 + 0.18 * jax.random.normal(key_list[8], (D,), jnp.float32), 0.1, 1.9),
        "gain_key": jnp.clip(1.0 + 0.18 * jax.random.normal(key_list[9], (D,), jnp.float32), 0.1, 1.9),
        "gain_attn": jnp.clip(1.0 + 0.18 * jax.random.normal(key_list[10], (D,), jnp.float32), 0.1, 1.9),
        "w_gate": bell_draw(key_list[11], (D, FF), D ** -0.5, 0.125, ((0, 32),), jnp.float32),
        "w_up": bell_draw(key_list[12], (D, FF), D ** -0.5, 0.125, ((0, 32),), jnp.float32),
        "w_down": bell_draw(key_list[13], (D, FF), FF ** -0.5, 0.0625, ((0, 32),), jnp.float32),
        "gain_mlp": jnp.clip(1.0 + 0.18 * jax.random.normal(key_list[14], (D,), jnp.float32), 0.1, 1.9),
    }


epsilon = 1e-06
rope_theta = 500000.0
masked_fill = -1e+30
highest = lax.Precision.HIGHEST

@jax.custom_vjp
def low(v):
    return lax.optimization_barrier(v.astype(jnp.bfloat16)).astype(jnp.float32)

@jax.custom_vjp
def low_back(v):
    return v

def low_keep(v):
    return (low(v), None)

def low_pass(kept, grad):
    return (grad,)

def back_keep(v):
    return (v, None)

def back_low(kept, grad):
    return (low(grad),)
low.defvjp(low_keep, low_pass)
low_back.defvjp(back_keep, back_low)

def matmul(left, right):
    return jnp.dot(left, right, precision=highest)

def normalize(vector, gain_row):
    scaled = lax.rsqrt(lax.optimization_barrier(jnp.mean(vector * vector, axis=-1, keepdims=True)) + epsilon)
    return vector * scaled * gain_row

def rotate(vector, cos_part, sin_part):
    half_dim = HEAD_DIM // 2
    by_head = vector.reshape(vector.shape[0], HEADS, HEAD_DIM)
    first_half = by_head[..., :half_dim]
    second_half = by_head[..., half_dim:]
    cos_wide = cos_part[:, None, :]
    sin_wide = sin_part[:, None, :]
    turned = jnp.concatenate([first_half * cos_wide - second_half * sin_wide, second_half * cos_wide + first_half * sin_wide], axis=-1)
    return turned.reshape(vector.shape)

def tree_tables(length_row, parent_row, total):
    seg_count = parent_row.shape[0]
    segment_ids = jnp.arange(seg_count, dtype=jnp.int32)
    ends = jnp.cumsum(length_row).astype(jnp.int32)
    offsets = (ends - length_row).astype(jnp.int32)
    all_rows = jnp.arange(total, dtype=jnp.int32)
    segment_all = (lax.optimization_barrier(jnp.sum((all_rows[:, None] >= offsets[None, :]).astype(jnp.int32), axis=1)) - 1).astype(jnp.int32)
    reached = ((parent_row[:, None] == segment_ids[None, :]) | (segment_ids[:, None] == segment_ids[None, :])).astype(jnp.float32)
    for _ in range(4):
        reached = jnp.minimum(lax.optimization_barrier(jnp.sum(reached[:, :, None] * reached[None, :, :], axis=1)), 1.0)
    strict = reached - jnp.eye(seg_count, dtype=jnp.float32)
    path_start = lax.optimization_barrier(jnp.sum(strict * length_row.astype(jnp.float32)[None, :], axis=1))
    position = all_rows.astype(jnp.float32) - offsets.astype(jnp.float32)[segment_all] + path_start[segment_all]
    seen = reached[segment_all][:, segment_all]
    allowed = (seen > 0.5) & (all_rows[None, :] <= all_rows[:, None])
    frequency = jnp.exp(jnp.arange(HEAD_DIM // 2, dtype=jnp.float32) * (-2.0 * math.log(rope_theta) / HEAD_DIM))
    angles = position[:, None] * frequency[None, :]
    return (allowed, jnp.cos(angles), jnp.sin(angles))

def tree_forward(tokens, weights, allowed, cos_part, sin_part):
    query_mat, key_mat, value_mat, output_mat, query_gain, key_gain, attn_gain, gate_mat, up_mat, down_mat, mlp_gain = weights
    row_count = tokens.shape[0]
    block_rows = min(512, row_count)
    query_pre = low_back(matmul(tokens, query_mat))
    key_pre = low_back(matmul(tokens, key_mat))
    value_low = low(low_back(matmul(tokens, value_mat)))
    query_low = low(rotate(normalize(query_pre, query_gain), cos_part, sin_part))
    key_low = low(rotate(normalize(key_pre, key_gain), cos_part, sin_part))
    head_query = query_low.reshape(row_count // block_rows, block_rows, HEADS, HEAD_DIM)
    head_key = key_low.reshape(row_count, HEADS, HEAD_DIM)
    head_value = value_low.reshape(row_count, HEADS, HEAD_DIM)
    mask_blocks = allowed.reshape(row_count // block_rows, block_rows, row_count)
    scale = 1.0 / math.sqrt(HEAD_DIM)

    def attend(items):
        query_block, mask_block = items
        scores = low_back(jnp.einsum('qhd,khd->hqk', query_block, head_key, precision=highest) * scale)
        scores = jnp.where(mask_block[None], scores, masked_fill)
        log_total = jax.nn.logsumexp(scores, axis=-1, keepdims=True)
        attn_probs = low(jnp.where(mask_block[None], jnp.exp(scores - log_total), 0.0))
        return jnp.einsum('hqk,khd->qhd', attn_probs, head_value, precision=highest)
    context = lax.map(jax.checkpoint(attend), (head_query, mask_blocks)).reshape(row_count, HEADS * HEAD_DIM)
    context = low(low_back(context))
    attn_pre = low_back(matmul(context, output_mat))
    hidden = tokens + normalize(attn_pre, attn_gain)
    hidden_low = low(hidden)
    gate_pre = low_back(matmul(hidden_low, gate_mat))
    up_pre = low_back(matmul(hidden_low, up_mat))
    activated = low(jax.nn.silu(gate_pre) * up_pre)
    mlp_pre = low_back(jnp.dot(activated, down_mat.T, precision=highest))
    return hidden + normalize(mlp_pre, mlp_gain)

def reference(inputs, cotangent, seg_lengths, seg_parents, w_query, w_key, w_value, w_output, gain_query, gain_key, gain_attn, w_gate, w_up, w_down, gain_mlp):
    allowed, cos_table, sin_table = jax.vmap(lambda length_row, parent_row: tree_tables(length_row, parent_row, TREE_LEN))(seg_lengths, seg_parents)
    masters = (w_query, w_key, w_value, w_output, gain_query, gain_key, gain_attn, w_gate, w_up, w_down, gain_mlp)

    def forward(tokens, *params):
        weights = tuple((low(param) for param in params))

        def one_tree(items):
            return tree_forward(items[0], weights, items[1], items[2], items[3])
        return lax.map(jax.checkpoint(one_tree), (tokens, allowed, cos_table, sin_table))
    result, pullback = jax.vjp(forward, inputs.astype(jnp.float32), *masters)
    gradients = pullback(cotangent.astype(jnp.float32))
    return (result.astype(jnp.bfloat16), gradients[0].astype(jnp.bfloat16), gradients[1], gradients[2], gradients[3], gradients[4], gradients[5], gradients[6], gradients[7], gradients[8], gradients[9], gradients[10], gradients[11])
```

```python
import functools
import math

import jax
import jax.numpy as jnp
from jax import lax
from jax.experimental import pallas as pl
from jax.experimental.pallas import tpu as pltpu
from jax.sharding import PartitionSpec as P

HEAD_DIM = 128

epsilon = 1e-06
rope_theta = 500000.0
masked_fill = -1e30
bf16 = jnp.bfloat16
f32 = jnp.float32
NN = (((1,), (0,)), ((), ()))
NT = (((1,), (1,)), ((), ()))
TN = (((0,), (0,)), ((), ()))


def dot(left, right, dims, kind=f32):
    return lax.dot_general(left, right, dims, preferred_element_type=f32).astype(kind)


def swap(piece, hop):
    count = lax.axis_size("row")
    return lax.ppermute(piece, "row", [(i, i ^ hop) for i in range(count)])


def gather_rows(rows):
    count, me = lax.axis_size("row"), lax.axis_index("row")
    size = rows.shape[0]
    whole = jnp.zeros((count * size,) + rows.shape[1:], rows.dtype)
    for hop in range(count):
        piece = swap(rows, hop) if hop else rows
        whole = lax.dynamic_update_slice_in_dim(whole, piece, (me ^ hop) * size, 0)
    return whole


def scatter_rows(partial):
    count, me = lax.axis_size("row"), lax.axis_index("row")
    size = partial.shape[0] // count
    total = lax.dynamic_slice_in_dim(partial, me * size, size, 0).astype(f32)
    for hop in range(1, count):
        piece = lax.dynamic_slice_in_dim(partial, (me ^ hop) * size, size, 0)
        total = total + swap(piece, hop).astype(f32)
    return total


def tie(value, *others):
    return lax.optimization_barrier((value,) + others)[0]


def columns_in(*weights):
    count, me = lax.axis_size("row"), lax.axis_index("row")
    size, wide = weights[0].shape[0], weights[0].shape[1] // count
    whole = jnp.zeros((count * size, wide * len(weights)), bf16)
    for hop in range(count):
        piece = jnp.concatenate(
            [lax.dynamic_slice_in_dim(w, (me ^ hop) * wide, wide, 1).astype(bf16) for w in weights], axis=1
        )
        if hop:
            piece = swap(piece, hop)
        whole = lax.dynamic_update_slice_in_dim(whole, piece, (me ^ hop) * size, 0)
    return whole


def columns_out(block):
    count, me = lax.axis_size("row"), lax.axis_index("row")
    size, wide = block.shape[0] // count, block.shape[1]
    whole = jnp.zeros((size, wide * count), f32)
    for hop in range(count):
        piece = lax.dynamic_slice_in_dim(block, (me ^ hop) * size, size, 0)
        if hop:
            piece = swap(piece, hop)
        whole = lax.dynamic_update_slice_in_dim(whole, piece.astype(f32), (me ^ hop) * wide, 1)
    return whole


def sum_rows(small):
    count = lax.axis_size("row")
    total = small
    for hop in range(1, count):
        total = total + swap(small, hop)
    return total


def norm_back(grad_out, unit_rows, scaled, gain_row):
    weighted = grad_out * gain_row
    inner = jnp.mean(weighted * unit_rows, axis=-1, keepdims=True)
    return (scaled * (weighted - unit_rows * inner), jnp.sum(grad_out * unit_rows, axis=0))


def rotate(vector, cos_part, sin_part):
    half_dim = HEAD_DIM // 2
    by_head = vector.reshape(vector.shape[0], vector.shape[1] // HEAD_DIM, HEAD_DIM)
    swapped = jnp.concatenate([by_head[..., half_dim:], by_head[..., :half_dim]], axis=-1)
    turned = by_head * cos_part[:, None, :] + swapped * sin_part[:, None, :]
    return turned.reshape(vector.shape)


def tree_tables(length_row, parent_row, total):
    seg_count = parent_row.shape[0]
    segment_ids = jnp.arange(seg_count, dtype=jnp.int32)
    ends = jnp.cumsum(length_row)
    offsets = ends - length_row
    all_rows = jnp.arange(total, dtype=jnp.int32)
    owned_from = (all_rows[:, None] >= offsets[None, :]).astype(f32)
    onehot_all = owned_from - jnp.concatenate(
        [owned_from[:, 1:], jnp.zeros((total, 1), f32)], axis=1
    )
    reached = (
        (parent_row[:, None] == segment_ids[None, :])
        | (segment_ids[:, None] == segment_ids[None, :])
    ).astype(f32)
    for _ in range(2):
        reached = jnp.minimum(jnp.sum(reached[:, :, None] * reached[None, :, :], axis=1), 1.0)
    strict = reached - jnp.eye(seg_count, dtype=f32)
    path_start = jnp.sum(strict * length_row.astype(f32)[None, :], axis=1)
    position = all_rows.astype(f32) + jnp.sum(
        onehot_all * (path_start - offsets.astype(f32))[None, :], axis=1
    )
    onehot_low = onehot_all.astype(bf16)
    row_reach = dot(onehot_low, reached.astype(bf16), NN, bf16)
    seen = dot(onehot_low, row_reach, NT)
    allowed = (seen > 0.5) & (all_rows[:, None] <= all_rows[None, :])
    bias = jnp.where(allowed, 0.0, masked_fill).astype(bf16)
    frequency = jnp.exp(
        jnp.arange(HEAD_DIM // 2, dtype=f32) * (-2.0 * math.log(rope_theta) / HEAD_DIM)
    )
    angles = position[:, None] * frequency[None, :]
    cos_half, sin_half = jnp.cos(angles), jnp.sin(angles)
    cos_wide = jnp.concatenate([cos_half, cos_half], axis=1)
    sin_wide = jnp.concatenate([-sin_half, sin_half], axis=1)
    return (bias, cos_wide, sin_wide)


def attend_kernel(block, scale, query_ref, key_ref, value_ref, bias_ref, context_ref, lse_ref):
    total = key_ref.shape[0]
    for first in range(0, total, block):
        last = first + block
        scores = dot(key_ref[:last], query_ref[first:last], NT) * scale
        scores = scores + bias_ref[:last, first:last].astype(f32)
        top = jnp.max(scores, axis=0, keepdims=True)
        probs = jnp.exp(scores - top)
        mass = jnp.sum(probs, axis=0, keepdims=True)
        probs_low = (probs * (1.0 / mass)).astype(bf16)
        turned = dot(value_ref[:last], probs_low, TN)
        context_ref[first:last, :] = turned.T.astype(bf16)
        lse_ref[:, first:last] = jnp.broadcast_to(top + jnp.log(mass), (8, block))


def attend(query, key, value, bias):
    total, width = query.shape
    heads = width // HEAD_DIM
    part = pl.BlockSpec((total, HEAD_DIM), lambda h: (0, h))
    return pl.pallas_call(
        functools.partial(attend_kernel, 256, 1.0 / math.sqrt(HEAD_DIM)),
        grid=(heads,),
        in_specs=[part, part, part, pl.BlockSpec((total, total), lambda h: (0, 0))],
        out_specs=[part, pl.BlockSpec((8, total), lambda h: (h, 0))],
        out_shape=[
            jax.ShapeDtypeStruct((total, width), bf16),
            jax.ShapeDtypeStruct((8 * heads, total), f32),
        ],
        compiler_params=pltpu.CompilerParams(vmem_limit_bytes=48 * 2**20),
        cost_estimate=pl.CostEstimate(
            flops=4 * total * total * width, bytes_accessed=10 * total * width, transcendentals=total * total * heads
        ),
    )(query, key, value, bias)


def attend_back_kernel(
    block,
    scale,
    query_ref,
    key_ref,
    value_ref,
    bias_ref,
    lse_ref,
    grad_ref,
    grad_query_ref,
    grad_key_ref,
    grad_value_ref,
):
    total = key_ref.shape[0]
    grad_key_ref[...] = jnp.zeros_like(grad_key_ref)
    grad_value_ref[...] = jnp.zeros_like(grad_value_ref)
    for first in range(0, total, block):
        last = first + block
        scores = dot(key_ref[:last], query_ref[first:last], NT) * scale
        scores = scores + bias_ref[:last, first:last].astype(f32)
        probs = jnp.exp(scores - lse_ref[0:1, first:last])
        grad_probs = dot(value_ref[:last], grad_ref[first:last], NT)
        inner = jnp.sum(probs * grad_probs, axis=0, keepdims=True)
        grad_scores = (probs * (grad_probs - inner)).astype(bf16)
        turned = dot(key_ref[:last], grad_scores, TN)
        grad_query_ref[first:last, :] = turned.T * scale
        grad_key_ref[:last, :] += dot(grad_scores, query_ref[first:last], NN) * scale
        grad_value_ref[:last, :] += dot(probs.astype(bf16), grad_ref[first:last], NN)


def attend_back(query, key, value, bias, lse, grad_context):
    total, width = query.shape
    heads = width // HEAD_DIM
    part = pl.BlockSpec((total, HEAD_DIM), lambda h: (0, h))
    return pl.pallas_call(
        functools.partial(attend_back_kernel, 256, 1.0 / math.sqrt(HEAD_DIM)),
        grid=(heads,),
        in_specs=[
            part,
            part,
            part,
            pl.BlockSpec((total, total), lambda h: (0, 0)),
            pl.BlockSpec((8, total), lambda h: (h, 0)),
            part,
        ],
        out_specs=[part, part, part],
        out_shape=[jax.ShapeDtypeStruct((total, width), f32)] * 3,
        compiler_params=pltpu.CompilerParams(vmem_limit_bytes=56 * 2**20),
        cost_estimate=pl.CostEstimate(
            flops=10 * total * total * width, bytes_accessed=24 * total * width, transcendentals=total * total * heads
        ),
    )(query, key, value, bias, lse, grad_context)


def body(
    inputs,
    cotangent,
    seg_lengths,
    seg_parents,
    w_query,
    w_key,
    w_value,
    w_output,
    gain_query,
    gain_key,
    gain_attn,
    w_gate,
    w_up,
    w_down,
    gain_mlp,
):
    trees, rows_dev, width = inputs.shape
    count, leaves, me = lax.axis_size("row"), lax.axis_size("leaf"), lax.axis_index("row")
    tree_len = rows_dev * count
    part = width // count
    own = w_query.shape[0]
    units = w_gate.shape[1] // count
    tokens = inputs.reshape(rows_dev, width)

    def leaf_gather(block):
        return lax.all_gather(block, "leaf", axis=0, tiled=True)

    def leaf_scatter(block):
        return lax.psum_scatter(block, "leaf", scatter_dimension=0, tiled=True)

    qkv_block = columns_in(w_query, w_key, w_value)
    gains_own = jnp.stack([gain_query, gain_key, gain_attn, gain_mlp]).astype(bf16).reshape(1, 4 * own)
    gains_leaf = gather_rows(gains_own).reshape(own, 4 * count)
    qkv_mat = leaf_gather(qkv_block)
    all_tokens = gather_rows(tie(tokens, qkv_block))
    output_block = jnp.concatenate(
        [w_output.astype(bf16), gains_leaf, jnp.zeros((own, HEAD_DIM - 4 * count), bf16)], axis=1
    )
    output_block = tie(output_block, qkv_block)
    output_rows = leaf_gather(output_block)
    gains_all = output_rows[:, width : width + 4 * count].reshape(leaves, count, 4, own)
    gains_all = jnp.moveaxis(gains_all, 2, 0).reshape(4, width).astype(f32)
    output_rows = output_rows[:, :width].reshape(count, leaves // count, own, width)
    output_mat = jnp.zeros((leaves // count, count, own, width), bf16)
    for hop in range(count):
        piece = lax.dynamic_index_in_dim(output_rows, me ^ hop, 0, keepdims=False)
        if hop:
            piece = swap(piece, hop)
        output_mat = lax.dynamic_update_index_in_dim(output_mat, piece, me ^ hop, 1)
    output_mat = output_mat.reshape(part, width)
    gate_block = columns_in(tie(w_gate, output_block))
    up_block = columns_in(tie(w_up, gate_block))
    down_block = columns_in(tie(w_down, up_block))
    gate_mat = leaf_gather(gate_block)
    up_mat = leaf_gather(up_block)
    down_mat = leaf_gather(down_block)

    bias, cos_wide, sin_wide = tree_tables(seg_lengths[0], seg_parents[0], tree_len)

    query_pre = dot(all_tokens, qkv_mat[:, :part], NN)
    key_pre = dot(all_tokens, qkv_mat[:, part : 2 * part], NN)
    value = dot(all_tokens, qkv_mat[:, 2 * part :], NN, bf16)
    squares = sum_rows(jnp.stack([jnp.sum(query_pre * query_pre, axis=1), jnp.sum(key_pre * key_pre, axis=1)]))
    scales = lax.rsqrt(squares / width + epsilon)
    query_scale, key_scale = scales[0][:, None], scales[1][:, None]
    query_gain = lax.dynamic_slice_in_dim(gains_all[0], me * part, part)
    key_gain = lax.dynamic_slice_in_dim(gains_all[1], me * part, part)
    attn_gain, mlp_gain = gains_all[2], gains_all[3]
    query_unit = query_pre * query_scale
    key_unit = key_pre * key_scale
    query = rotate(query_unit * query_gain, cos_wide, sin_wide).astype(bf16)
    key = rotate(key_unit * key_gain, cos_wide, sin_wide).astype(bf16)
    context, lse = attend(query, key, value, bias)
    attn_pre = scatter_rows(dot(context, output_mat, NN, bf16))
    attn_scale = lax.rsqrt(jnp.mean(attn_pre * attn_pre, axis=-1, keepdims=True) + epsilon)
    attn_unit = attn_pre * attn_scale
    hidden = tokens.astype(f32) + attn_unit * attn_gain
    hidden_all = gather_rows(hidden.astype(bf16))

    gate_pre = dot(hidden_all, gate_mat, NN)
    up_pre = dot(hidden_all, up_mat, NN)
    sigmoid_gate = jax.nn.sigmoid(gate_pre)
    activated = (gate_pre * sigmoid_gate * up_pre).astype(bf16)
    mlp_pre = scatter_rows(dot(activated, down_mat, NT, bf16))
    mlp_scale = lax.rsqrt(jnp.mean(mlp_pre * mlp_pre, axis=-1, keepdims=True) + epsilon)
    mlp_unit = mlp_pre * mlp_scale
    outputs = (hidden + mlp_unit * mlp_gain).astype(bf16).reshape(inputs.shape)

    grad_final = cotangent.reshape(rows_dev, width).astype(f32)
    grad_mlp, grad_mlp_gain = norm_back(grad_final, mlp_unit, mlp_scale, mlp_gain)
    grad_mlp_all = gather_rows(grad_mlp.astype(bf16))
    grad_act = dot(grad_mlp_all, down_mat, NN)
    down_sum = dot(grad_mlp_all, activated, TN, bf16)
    down_shard = leaf_scatter(down_sum)
    grad_act = tie(grad_act, down_sum)
    grad_gate = (grad_act * up_pre * sigmoid_gate * (1.0 + gate_pre * (1.0 - sigmoid_gate))).astype(bf16)
    grad_up = (grad_act * gate_pre * sigmoid_gate).astype(bf16)
    grad_hidden_part = dot(grad_gate, gate_mat, NT) + dot(grad_up, up_mat, NT)
    grad_hidden = grad_final + scatter_rows(grad_hidden_part.astype(bf16))
    gate_sum = dot(hidden_all, tie(grad_gate, grad_hidden_part), TN, bf16)
    up_sum = dot(hidden_all, tie(grad_up, gate_sum), TN, bf16)
    gate_sum = tie(gate_sum, down_shard, up_sum, grad_hidden)
    gate_shard = leaf_scatter(gate_sum)
    grad_hidden = tie(grad_hidden, gate_sum)

    grad_attn, grad_attn_gain = norm_back(grad_hidden, attn_unit, attn_scale, attn_gain)
    grad_attn_all = gather_rows(grad_attn.astype(bf16))
    grad_context = dot(grad_attn_all, output_mat, NT, bf16)
    grad_query, grad_key, grad_value = attend_back(query, key, value, bias, lse, grad_context)
    grad_query, grad_key, grad_value, up_sum = lax.optimization_barrier(
        (grad_query, grad_key, grad_value, tie(up_sum, gate_shard))
    )
    up_shard = leaf_scatter(up_sum)
    grad_value_low = grad_value.astype(bf16)
    grad_query = rotate(grad_query, cos_wide, -sin_wide)
    grad_key = rotate(grad_key, cos_wide, -sin_wide)
    inner = sum_rows(
        jnp.stack(
            [
                jnp.sum(grad_query * query_gain * query_unit, axis=1),
                jnp.sum(grad_key * key_gain * key_unit, axis=1),
            ]
        )
    ) / width
    grad_query_gain = jnp.sum(grad_query * query_unit, axis=0)
    grad_key_gain = jnp.sum(grad_key * key_unit, axis=0)
    grad_query_low = (query_scale * (grad_query * query_gain - query_unit * inner[0][:, None])).astype(bf16)
    grad_key_low = (key_scale * (grad_key * key_gain - key_unit * inner[1][:, None])).astype(bf16)
    grad_qkv = jnp.concatenate([grad_query_low, grad_key_low, grad_value_low], axis=1)
    grad_tokens = grad_hidden + scatter_rows(dot(grad_qkv, qkv_mat, NT, bf16))
    grad_inputs = grad_tokens.astype(bf16).reshape(inputs.shape)

    output_part = dot(context, grad_attn_all, TN, bf16).reshape(leaves // count, count, own, width)
    output_turned = jnp.zeros((count, leaves // count, own, width), bf16)
    for hop in range(count):
        piece = lax.dynamic_index_in_dim(output_part, me ^ hop, 1, keepdims=False)
        if hop:
            piece = swap(piece, hop)
        output_turned = lax.dynamic_update_index_in_dim(output_turned, piece, me ^ hop, 0)
    qkv_sum = dot(all_tokens, grad_qkv, TN, bf16)
    output_shard = leaf_scatter(tie(output_turned.reshape(leaves * own, width), up_shard, qkv_sum))
    qkv_shard = leaf_scatter(tie(qkv_sum, output_shard))
    grad_output = output_shard.astype(f32)

    wide_part = jnp.stack([grad_attn_gain, grad_mlp_gain]).reshape(2, leaves, count, own)
    narrow_part = jnp.stack([grad_query_gain, grad_key_gain]).reshape(2, leaves // count, count, own)
    wide_sum = jnp.zeros((2, leaves, own), f32)
    narrow_all = jnp.zeros((2, leaves, own), f32)
    for hop in range(count):
        piece = lax.dynamic_index_in_dim(jnp.concatenate([wide_part, narrow_part], axis=1), me ^ hop, 2, keepdims=False)
        if hop:
            piece = swap(piece, hop)
        wide_sum = wide_sum + piece[:, :leaves]
        narrow_all = lax.dynamic_update_slice_in_dim(
            narrow_all, piece[:, leaves:], (me ^ hop) * (leaves // count), 1
        )
    grad_gains = jnp.concatenate([narrow_all, wide_sum], axis=0)
    stride = 1
    while stride < leaves:
        grad_gains = grad_gains + lax.ppermute(
            grad_gains, "leaf", [(i, i ^ stride) for i in range(leaves)]
        )
        stride *= 2
    grad_gains = lax.dynamic_index_in_dim(grad_gains, lax.axis_index("leaf"), 1, keepdims=False)
    return (
        outputs,
        grad_inputs,
        columns_out(qkv_shard[:, :part]),
        columns_out(qkv_shard[:, part : 2 * part]),
        columns_out(qkv_shard[:, 2 * part :]),
        grad_output,
        grad_gains[0],
        grad_gains[1],
        grad_gains[2],
        columns_out(gate_shard),
        columns_out(up_shard),
        columns_out(down_shard),
        grad_gains[3],
    )


def solution(mesh):
    both = ("leaf", "row")
    token_spec, tree_spec, matrix_spec, gain_spec = P("leaf", "row", None), P("leaf", None), P(both, None), P(both)
    return jax.shard_map(
        body,
        mesh=mesh,
        in_specs=(token_spec,) * 2 + (tree_spec,) * 2 + (matrix_spec,) * 4 + (gain_spec,) * 3 + (matrix_spec,) * 3 + (gain_spec,),
        out_specs=(token_spec,) * 2 + (matrix_spec,) * 4 + (gain_spec,) * 3 + (matrix_spec,) * 3 + (gain_spec,),
        check_vma=False,
    )
```

```python
import functools
import math

import jax
import jax.numpy as jnp
from jax import lax
from jax.experimental import pallas as pl
from jax.experimental.pallas import tpu as pltpu
from jax.sharding import PartitionSpec as P

HEAD_DIM = 128
MESH = pl.DeviceIdType.MESH

epsilon = 1e-06
rope_theta = 500000.0
masked_fill = -1e30
bf16 = jnp.bfloat16
f32 = jnp.float32
NN = (((1,), (0,)), ((), ()))
NT = (((1,), (1,)), ((), ()))
TN = (((0,), (0,)), ((), ()))


def dot(left, right, dims, kind=f32):
    return lax.dot_general(left, right, dims, preferred_element_type=f32).astype(kind)


def swap(piece, hop):
    count = lax.axis_size("row")
    return lax.ppermute(piece, "row", [(i, i ^ hop) for i in range(count)])


def gather_rows(rows, *meanwhile):
    count, me = lax.axis_size("row"), lax.axis_index("row")
    size = rows.shape[0]
    whole = jnp.zeros((count * size,) + rows.shape[1:], rows.dtype)
    for hop in range(1, count):
        whole = lax.dynamic_update_slice_in_dim(whole, swap(rows, hop), (me ^ hop) * size, 0)
    return lax.dynamic_update_slice_in_dim(whole, tie(rows, *meanwhile), me * size, 0)


def dot_scatter(lefts, rights, dims, *meanwhile):
    count, me = lax.axis_size("row"), lax.axis_index("row")
    size = lefts[0].shape[0] // count

    def rows_of(hop, lefts):
        parts = [lax.dynamic_slice_in_dim(left, (me ^ hop) * size, size, 0) for left in lefts]
        return sum(dot(part, right, dims) for part, right in zip(parts, rights))

    coming = [swap(rows_of(hop, lefts).astype(bf16), hop) for hop in reversed(range(1, count))]
    total = rows_of(0, [tie(left, *meanwhile) for left in lefts])
    for piece in coming:
        total = total + piece.astype(f32)
    return total


def tie(value, *others):
    return lax.optimization_barrier((value,) + others)[0]


def columns_in(*weights):
    count, me = lax.axis_size("row"), lax.axis_index("row")
    size, wide = weights[0].shape[0], weights[0].shape[1] // count
    whole = jnp.zeros((count * size, wide * len(weights)), bf16)
    for hop in range(count):
        piece = jnp.concatenate(
            [lax.dynamic_slice_in_dim(w, (me ^ hop) * wide, wide, 1).astype(bf16) for w in weights], axis=1
        )
        if hop:
            piece = swap(piece, hop)
        whole = lax.dynamic_update_slice_in_dim(whole, piece, (me ^ hop) * size, 0)
    return whole


def columns_out(block, many=1):
    count, me = lax.axis_size("row"), lax.axis_index("row")
    size, wide = block.shape[0] // count, block.shape[1] // many
    whole = [jnp.zeros((size, wide * count), f32)] * many
    for hop in range(count):
        piece = lax.dynamic_slice_in_dim(block, (me ^ hop) * size, size, 0)
        if hop:
            piece = swap(piece, hop)
        for i in range(many):
            own = piece[:, i * wide : (i + 1) * wide].astype(f32)
            whole[i] = lax.dynamic_update_slice_in_dim(whole[i], own, (me ^ hop) * wide, 1)
    return whole


def sum_rows(small):
    count = lax.axis_size("row")
    total = small
    for hop in range(1, count):
        total = total + swap(small, hop)
    return total


def norm_back(grad_out, unit_rows, scaled, gain_row):
    weighted = grad_out * gain_row
    inner = jnp.mean(weighted * unit_rows, axis=-1, keepdims=True)
    return (scaled * (weighted - unit_rows * inner), jnp.sum(grad_out * unit_rows, axis=0))


def tree_tables(length_row, parent_row, total):
    seg_count = parent_row.shape[0]
    segment_ids = jnp.arange(seg_count, dtype=jnp.int32)
    ends = jnp.cumsum(length_row)
    offsets = ends - length_row
    all_rows = jnp.arange(total, dtype=jnp.int32)
    owned_from = (all_rows[:, None] >= offsets[None, :]).astype(f32)
    onehot_all = owned_from - jnp.concatenate(
        [owned_from[:, 1:], jnp.zeros((total, 1), f32)], axis=1
    )
    reached = (
        (parent_row[:, None] == segment_ids[None, :])
        | (segment_ids[:, None] == segment_ids[None, :])
    ).astype(f32)
    for _ in range(2):
        reached = jnp.minimum(jnp.sum(reached[:, :, None] * reached[None, :, :], axis=1), 1.0)
    strict = reached - jnp.eye(seg_count, dtype=f32)
    path_start = jnp.sum(strict * length_row.astype(f32)[None, :], axis=1)
    position = all_rows.astype(f32) + jnp.sum(
        onehot_all * (path_start - offsets.astype(f32))[None, :], axis=1
    )
    onehot_low = onehot_all.astype(bf16)
    row_reach = dot(onehot_low, reached.astype(bf16), NN, bf16)
    seen = dot(onehot_low, row_reach, NT)
    allowed = (seen > 0.5) & (all_rows[:, None] <= all_rows[None, :])
    bias = jnp.where(allowed, 0.0, masked_fill).astype(bf16)
    frequency = jnp.exp(
        jnp.arange(HEAD_DIM // 2, dtype=f32) * (-2.0 * math.log(rope_theta) / HEAD_DIM)
    )
    angles = position[:, None] * frequency[None, :]
    cos_half, sin_half = jnp.cos(angles), jnp.sin(angles)
    cos_wide = jnp.concatenate([cos_half, cos_half], axis=1)
    sin_wide = jnp.concatenate([-sin_half, sin_half], axis=1)
    return (bias, cos_wide, sin_wide)


def turn(vector, cos_part, sin_part):
    return vector * cos_part + pltpu.roll(vector, HEAD_DIM // 2, 1) * sin_part


def project_kernel(tokens_ref, weights_ref, query_ref, key_ref, value_ref, squares_ref):
    part = query_ref.shape[1]
    tokens = tokens_ref[...]
    for i, out_ref in enumerate((query_ref, key_ref)):
        product = dot(tokens, weights_ref[:, i * part : (i + 1) * part], NN)
        out_ref[...] = product
        square = jnp.sum(product * product, axis=1, keepdims=True)
        squares_ref[i : i + 1, :] = jnp.broadcast_to(square, (square.shape[0], HEAD_DIM)).T[0:1]
    value_ref[...] = dot(tokens, weights_ref[:, 2 * part :], NN, bf16)


def project(tokens, weights, part):
    total, width = tokens.shape
    size = 256
    rows = pl.BlockSpec((size, part), lambda i: (i, 0))
    wide = jax.ShapeDtypeStruct((total, part), f32)
    return pl.pallas_call(
        project_kernel,
        grid=(total // size,),
        in_specs=[
            pl.BlockSpec((size, width), lambda i: (i, 0)),
            pl.BlockSpec((width, 3 * part), lambda i: (0, 0)),
        ],
        out_specs=[rows, rows, rows, pl.BlockSpec((2, size), lambda i: (0, i))],
        out_shape=[
            wide,
            wide,
            jax.ShapeDtypeStruct((total, part), bf16),
            jax.ShapeDtypeStruct((2, total), f32),
        ],
        compiler_params=pltpu.CompilerParams(vmem_limit_bytes=48 * 2**20),
        cost_estimate=pl.CostEstimate(
            flops=6 * total * width * part, bytes_accessed=2 * width * (total + 3 * part) + 10 * total * part, transcendentals=0
        ),
    )(tokens, weights)


def attend_kernel(
    block,
    scale,
    query_pre_ref,
    key_pre_ref,
    value_ref,
    scales_ref,
    gains_ref,
    cos_ref,
    sin_ref,
    bias_ref,
    query_ref,
    key_ref,
    context_ref,
    lse_ref,
):
    total = key_ref.shape[0]
    cos_part, sin_part = cos_ref[...], sin_ref[...]
    query_ref[...] = turn(query_pre_ref[...] * scales_ref[:, 0:1] * gains_ref[0:1], cos_part, sin_part).astype(bf16)
    key_ref[...] = turn(key_pre_ref[...] * scales_ref[:, 1:2] * gains_ref[1:2], cos_part, sin_part).astype(bf16)
    for first in range(0, total, block):
        last = first + block
        scores = dot(key_ref[:last], query_ref[first:last], NT) * scale
        scores = scores + bias_ref[:last, first:last].astype(f32)
        top = jnp.max(scores, axis=0, keepdims=True)
        probs = jnp.exp(scores - top)
        mass = jnp.sum(probs, axis=0, keepdims=True)
        probs_low = (probs * (1.0 / mass)).astype(bf16)
        turned = dot(value_ref[:last], probs_low, TN)
        context_ref[first:last, :] = turned.T.astype(bf16)
        lse_ref[:, first:last] = jnp.broadcast_to(top + jnp.log(mass), (8, block))


def head_specs(total):
    part = pl.BlockSpec((total, HEAD_DIM), lambda h: (0, h))
    whole = pl.BlockSpec((total, HEAD_DIM), lambda h: (0, 0))
    gains = pl.BlockSpec((2, HEAD_DIM), lambda h: (0, h))
    scales = pl.BlockSpec((total, 2), lambda h: (0, 0))
    bias = pl.BlockSpec((total, total), lambda h: (0, 0))
    lse = pl.BlockSpec((8, total), lambda h: (h, 0))
    return part, whole, gains, scales, bias, lse


def attend(query_pre, key_pre, value, scales, gains, cos_wide, sin_wide, bias):
    total, width = query_pre.shape
    heads = width // HEAD_DIM
    part, whole, gain, scale, square, lse = head_specs(total)
    low = jax.ShapeDtypeStruct((total, width), bf16)
    return pl.pallas_call(
        functools.partial(attend_kernel, 256, 1.0 / math.sqrt(HEAD_DIM)),
        grid=(heads,),
        in_specs=[part, part, part, scale, gain, whole, whole, square],
        out_specs=[part, part, part, lse],
        out_shape=[low, low, low, jax.ShapeDtypeStruct((8 * heads, total), f32)],
        compiler_params=pltpu.CompilerParams(vmem_limit_bytes=56 * 2**20),
        cost_estimate=pl.CostEstimate(
            flops=4 * total * total * width, bytes_accessed=16 * total * width, transcendentals=total * total * heads
        ),
    )(query_pre, key_pre, value, scales, gains, cos_wide, sin_wide, bias)


def attend_back_kernel(
    block,
    scale,
    query_ref,
    key_ref,
    value_ref,
    bias_ref,
    lse_ref,
    grad_ref,
    query_pre_ref,
    key_pre_ref,
    scales_ref,
    gains_ref,
    cos_ref,
    sin_ref,
    grad_query_ref,
    grad_key_ref,
    grad_value_ref,
    inner_query_ref,
    inner_key_ref,
    grad_gains_ref,
    key_sum,
    value_sum,
):
    total = key_ref.shape[0]

    @pl.when(pl.program_id(0) == 0)
    def _():
        inner_query_ref[...] = jnp.zeros_like(inner_query_ref)
        inner_key_ref[...] = jnp.zeros_like(inner_key_ref)

    key_sum[...] = jnp.zeros_like(key_sum)
    value_sum[...] = jnp.zeros_like(value_sum)
    for first in range(0, total, block):
        last = first + block
        scores = dot(key_ref[:last], query_ref[first:last], NT) * scale
        scores = scores + bias_ref[:last, first:last].astype(f32)
        probs = jnp.exp(scores - lse_ref[0:1, first:last])
        grad_probs = dot(value_ref[:last], grad_ref[first:last], NT)
        inner = jnp.sum(probs * grad_probs, axis=0, keepdims=True)
        grad_scores = (probs * (grad_probs - inner)).astype(bf16)
        turned = dot(key_ref[:last], grad_scores, TN)
        grad_query_ref[first:last, :] = turned.T
        key_sum[:last, :] += dot(grad_scores, query_ref[first:last], NN)
        value_sum[:last, :] += dot(probs.astype(bf16), grad_ref[first:last], NN)
    grad_value_ref[...] = value_sum[...].astype(bf16)
    cos_part, sin_part = cos_ref[...], -sin_ref[...]
    for row, (grad, out_ref, pre_ref, inner_ref) in enumerate(
        (
            (grad_query_ref[...], grad_query_ref, query_pre_ref, inner_query_ref),
            (key_sum[...], grad_key_ref, key_pre_ref, inner_key_ref),
        )
    ):
        grad = turn(grad * scale, cos_part, sin_part)
        by_unit = grad * (pre_ref[...] * scales_ref[:, row : row + 1])
        inner_ref[...] += by_unit * gains_ref[row : row + 1]
        grad_gains_ref[row : row + 1, :] = jnp.sum(by_unit, axis=0, keepdims=True)
        out_ref[...] = grad


def attend_back(query, key, value, bias, lse, grad_context, query_pre, key_pre, scales, gains, cos_wide, sin_wide):
    total, width = query.shape
    heads = width // HEAD_DIM
    part, whole, gain, scale, square, lse_spec = head_specs(total)
    wide = jax.ShapeDtypeStruct((total, width), f32)
    narrow = jax.ShapeDtypeStruct((total, HEAD_DIM), f32)
    return pl.pallas_call(
        functools.partial(attend_back_kernel, 256, 1.0 / math.sqrt(HEAD_DIM)),
        grid=(heads,),
        in_specs=[part, part, part, square, lse_spec, part, part, part, scale, gain, whole, whole],
        out_specs=[part, part, part, whole, whole, gain],
        out_shape=[
            wide,
            wide,
            jax.ShapeDtypeStruct((total, width), bf16),
            narrow,
            narrow,
            jax.ShapeDtypeStruct((2, width), f32),
        ],
        scratch_shapes=[pltpu.VMEM((total, HEAD_DIM), f32)] * 2,
        compiler_params=pltpu.CompilerParams(vmem_limit_bytes=58 * 2**20),
        cost_estimate=pl.CostEstimate(
            flops=10 * total * total * width, bytes_accessed=30 * total * width, transcendentals=total * total * heads
        ),
    )(query, key, value, bias, lse, grad_context, query_pre, key_pre, scales, gains, cos_wide, sin_wide)


def sums_kernel(tokens_ref, grads_ref, side_ref, out_ref):
    wide = grads_ref.shape[1]
    out_ref[:, :wide] = dot(tokens_ref[...], grads_ref[...], TN, bf16)
    out_ref[:, wide:] = side_ref[...]


def sums_beside(tokens, grads, side):
    total, rows = tokens.shape
    wide, extra = grads.shape[1], side.shape[1]
    size = 256
    return pl.pallas_call(
        sums_kernel,
        grid=(rows // size,),
        in_specs=[
            pl.BlockSpec((total, size), lambda i: (0, i)),
            pl.BlockSpec((total, wide), lambda i: (0, 0)),
            pl.BlockSpec((size, extra), lambda i: (i, 0)),
        ],
        out_specs=pl.BlockSpec((size, wide + extra), lambda i: (i, 0)),
        out_shape=jax.ShapeDtypeStruct((rows, wide + extra), bf16),
        compiler_params=pltpu.CompilerParams(vmem_limit_bytes=40 * 2**20),
        cost_estimate=pl.CostEstimate(
            flops=2 * total * rows * wide, bytes_accessed=2 * rows * (total + wide + 2 * extra), transcendentals=0
        ),
    )(tokens, grads, side)


def landed(ref, sem):
    pltpu.make_async_copy(ref, ref, sem).wait()


def line_order(z):
    far, inner = z // 2, ((z + 1) // 2) % 2
    blocks = []
    for end, middle in ((3, 0), (2, 2), (1, 3), (0, 1)):
        first = end + inner * (middle - end)
        blocks.append(first + far * (3 - 2 * first))
    near = 1 + far
    chips = [near + inner * (blocks[0] - near), blocks[1], blocks[2]]
    slots = [3 + inner * (-2 - far), 2 + inner * (far - 2), far + inner * (2 - far)]
    return far, inner, blocks, chips, slots


def other(index, hop):
    return (index, index + 1 - 2 * (index % 2), (index + 2) % 4, 3 - index)[hop]


def final_kernel(
    tokens_hbm,
    grads_hbm,
    weights_hbm,
    output_hbm,
    hidden_hbm,
    up_hbm,
    query_out,
    key_out,
    value_out,
    output_out,
    inputs_out,
    up_out,
    tokens,
    grads,
    weights,
    hidden,
    core_out,
    core_in,
    mine,
    line_in,
    side,
    side_in,
    side_mine,
    side_line_in,
    tokens_send,
    tokens_in,
    rows_send,
    rows_in,
    up_in,
    load_sem,
    row_send_sem,
    row_recv_sem,
    core_send_sem,
    core_recv_sem,
    line_send_sem,
    line_recv_sem,
):
    leaf, row = lax.axis_index("leaf"), lax.axis_index("row")
    z, core = leaf // 2, leaf % 2
    far, inner, blocks, chips, slots = line_order(z)
    wide, own = grads.shape[1], query_out.shape[0]
    part, size = wide // 3, mine.shape[1]
    rows = tokens_in.shape[1]
    hops = (3, 1, 2)

    loads = [
        pltpu.make_async_copy(tokens_hbm, tokens, load_sem.at[0]),
        pltpu.make_async_copy(grads_hbm, grads, load_sem.at[1]),
        pltpu.make_async_copy(weights_hbm.at[:, pl.ds(0, wide)], weights, load_sem.at[2]),
        pltpu.make_async_copy(hidden_hbm, hidden, load_sem.at[3]),
        pltpu.make_async_copy(output_hbm.at[:, row], side.at[pl.ds(2 * row, 2)], load_sem.at[4]),
    ]
    for load in loads:
        load.start()
    barrier = pltpu.get_barrier_semaphore()
    for hop in hops:
        pl.semaphore_signal(barrier, inc=1, device_id={"row": other(row, hop)}, device_id_type=MESH)
        pl.semaphore_signal(barrier, inc=1, device_id={"leaf": 2 * other(z, hop) + core}, device_id_type=MESH)
    pl.semaphore_signal(barrier, inc=1, device_id={"leaf": 2 * z + 1 - core}, device_id_type=MESH)
    pl.semaphore_wait(barrier, 7)

    sent = []

    def row_copy(source, target, kind, hop):
        copy = pltpu.make_async_remote_copy(
            source,
            target,
            row_send_sem.at[kind, hop - 1],
            row_recv_sem.at[kind, hop - 1],
            device_id={"row": other(row, hop)},
            device_id_type=MESH,
        )
        copy.start()
        sent.append(copy)

    def core_copy(source, target, kind, i):
        copy = pltpu.make_async_remote_copy(
            source,
            target,
            core_send_sem.at[kind, i],
            core_recv_sem.at[kind, i],
            device_id={"leaf": 2 * z + 1 - core},
            device_id_type=MESH,
        )
        copy.start()
        sent.append(copy)

    def line_copy(source, target, kind, i):
        return pltpu.make_async_remote_copy(
            source,
            target.at[slots[i]],
            line_send_sem.at[kind, i],
            line_recv_sem.at[kind, slots[i]],
            device_id={"leaf": 2 * chips[i] + core},
            device_id_type=MESH,
        )

    for hop in hops:
        row_copy(output_hbm.at[:, other(row, hop)], side.at[pl.ds(2 * row, 2)], 0, hop)

    loads[0].wait()
    loads[1].wait()

    def product(block):
        return dot(tokens[:, pl.ds(pl.multiple_of(block * size, size), size)], grads[...], TN)

    for i in range(4):
        core_out[i] = product(2 * blocks[i] + 1 - core).astype(bf16)
        core_copy(core_out.at[i], core_in.at[i], 0, i)

    def pair(i):
        mine[i] = (product(2 * blocks[i] + core) + core_in[i].astype(f32)).astype(bf16)

    for i in range(4):
        landed(core_in.at[i], core_recv_sem.at[0, i])
        pair(i)
        if i < 2:
            copy = line_copy(mine.at[i], line_in, 0, i)
            copy.start()
            sent.append(copy)
        if i == 2:
            last = line_copy(mine.at[2], line_in, 0, 2)
            sent.append(last)

            @pl.when(inner == 0)
            def _():
                last.start()

    loads[2].wait()

    def tokens_part(hop, store):
        lines = grads[pl.ds(pl.multiple_of((other(row, hop)) * rows, rows), rows), :]

        def step(j, carry):
            columns = pl.ds(pl.multiple_of(j * part, part), part)
            store(columns, dot(lines, weights[columns, :], NT))
            return carry

        lax.fori_loop(0, weights.shape[0] // part, step, 0)

    for hop in hops:

        def store(columns, values):
            tokens_send[hop - 1, :, columns] = values.astype(bf16)

        tokens_part(hop, store)
        row_copy(tokens_send.at[hop - 1], tokens_in.at[hop - 1], 1, hop)

    loads[4].wait()
    for hop in hops:
        landed(side.at[pl.ds(2 * (other(row, hop)), 2)], row_recv_sem.at[0, hop - 1])
    for i in range(4):
        core_copy(side.at[2 * blocks[i] + 1 - core], side_in.at[i], 1, i)

    for hop in hops:
        row_copy(up_hbm.at[pl.ds((other(row, hop)) * own, own)], up_in.at[row], 2, hop)
    keep = pltpu.make_async_copy(up_hbm.at[pl.ds(row * own, own)], up_in.at[row], load_sem.at[5])
    keep.start()

    @pl.when(inner == 1)
    def _():
        landed(line_in.at[3], line_recv_sem.at[0, 3])
        mine[2] = (mine[2].astype(f32) + line_in[3].astype(f32)).astype(bf16)
        last.start()

    for i in range(4):
        landed(side_in.at[i], core_recv_sem.at[1, i])
        side_mine[i] = (side[2 * blocks[i] + core].astype(f32) + side_in[i].astype(f32)).astype(bf16)
        if i < 2:
            copy = line_copy(side_mine.at[i], side_line_in, 1, i)
            copy.start()
            sent.append(copy)
        if i == 2:
            side_last = line_copy(side_mine.at[2], side_line_in, 1, 2)
            sent.append(side_last)

            @pl.when(inner == 0)
            def _():
                side_last.start()

    loads[3].wait()

    def own_store(columns, values):
        hidden[:, columns] += values

    tokens_part(0, own_store)

    def total(kind, came, kept):
        landed(came.at[2], line_recv_sem.at[kind, 2])
        kept[3] = (kept[3].astype(f32) + came[2].astype(f32)).astype(bf16)
        for slot in range(2):

            @pl.when(inner + (1 - far) * slot + far * (1 - slot) > 0)
            def _():
                landed(came.at[slot], line_recv_sem.at[kind, slot])
                kept[3] = (kept[3].astype(f32) + came[slot].astype(f32)).astype(bf16)

    @pl.when(inner == 1)
    def _():
        landed(side_line_in.at[3], line_recv_sem.at[1, 3])
        side_mine[2] = (side_mine[2].astype(f32) + side_line_in[3].astype(f32)).astype(bf16)
        side_last.start()

    for hop in hops:
        landed(tokens_in.at[hop - 1], row_recv_sem.at[1, hop - 1])
        hidden[...] += tokens_in[hop - 1].astype(f32)
    inputs_out[...] = hidden[...].astype(bf16)

    keep.wait()
    for hop in hops:
        landed(up_in.at[other(row, hop)], row_recv_sem.at[2, hop - 1])
    for source in range(4):
        up_out[:, source * up_in.shape[2] : (source + 1) * up_in.shape[2]] = up_in[source].astype(f32)

    total(0, line_in, mine)
    rows_send[...] = mine[3]
    for hop in hops:
        row_copy(rows_send.at[pl.ds((other(row, hop)) * own, own)], rows_in.at[hop - 1], 3, hop)

    def give(source, values):
        columns = pl.ds(pl.multiple_of(source * part, part), part)
        for i, out in enumerate((query_out, key_out, value_out)):
            out[:, columns] = values[:, i * part : (i + 1) * part].astype(f32)

    give(row, rows_send[pl.ds(pl.multiple_of(row * own, own), own), :])
    total(1, side_line_in, side_mine)
    output_out[...] = side_mine[3].astype(f32)
    for hop in hops:
        landed(rows_in.at[hop - 1], row_recv_sem.at[3, hop - 1])
        give(other(row, hop), rows_in[hop - 1])
    for copy in sent:
        copy.wait_send()


def finish(tokens, grads, weights, output_part, hidden, up_shard):
    total, width = tokens.shape
    wide = grads.shape[1]
    own = output_part.shape[2]
    size, rows, units = 4 * own, hidden.shape[0], up_shard.shape[1]
    matrix = jax.ShapeDtypeStruct((own, width), f32)
    dma = pltpu.SemaphoreType.DMA
    return pl.pallas_call(
        final_kernel,
        in_specs=[pl.BlockSpec(memory_space=pl.ANY)] * 6,
        out_specs=[pl.BlockSpec(memory_space=pltpu.VMEM)] * 6,
        out_shape=[
            matrix,
            matrix,
            matrix,
            matrix,
            jax.ShapeDtypeStruct((rows, width), bf16),
            jax.ShapeDtypeStruct((own, 4 * units), f32),
        ],
        scratch_shapes=[
            pltpu.VMEM((total, width), bf16),
            pltpu.VMEM((total, wide), bf16),
            pltpu.VMEM((width, wide), bf16),
            pltpu.VMEM((rows, width), f32),
            pltpu.VMEM((4, size, wide), bf16),
            pltpu.VMEM((4, size, wide), bf16),
            pltpu.VMEM((4, size, wide), bf16),
            pltpu.VMEM((4, size, wide), bf16),
            pltpu.VMEM((8, own, width), bf16),
            pltpu.VMEM((4, own, width), bf16),
            pltpu.VMEM((4, own, width), bf16),
            pltpu.VMEM((4, own, width), bf16),
            pltpu.VMEM((3, rows, width), bf16),
            pltpu.VMEM((3, rows, width), bf16),
            pltpu.VMEM((size, wide), bf16),
            pltpu.VMEM((3, own, wide), bf16),
            pltpu.VMEM((4, own, units), bf16),
            dma((6,)),
            dma((4, 3)),
            dma((4, 3)),
            dma((2, 4)),
            dma((2, 4)),
            dma((2, 3)),
            dma((2, 4)),
        ],
        compiler_params=pltpu.CompilerParams(
            collective_id=1, has_side_effects=True, vmem_limit_bytes=60 * 2**20
        ),
        cost_estimate=pl.CostEstimate(
            flops=4 * total * width * wide, bytes_accessed=100 * 2**20, transcendentals=0
        ),
    )(tokens, grads, weights, output_part, hidden, up_shard)


def body(
    inputs,
    cotangent,
    seg_lengths,
    seg_parents,
    w_query,
    w_key,
    w_value,
    w_output,
    gain_query,
    gain_key,
    gain_attn,
    w_gate,
    w_up,
    w_down,
    gain_mlp,
):
    trees, rows_dev, width = inputs.shape
    count, leaves, me = lax.axis_size("row"), lax.axis_size("leaf"), lax.axis_index("row")
    tree_len = rows_dev * count
    part = width // count
    own = w_query.shape[0]
    group = count * own // 2
    units = w_gate.shape[1] // count
    tokens = inputs.reshape(rows_dev, width)

    def leaf_gather(block):
        return lax.all_gather(block, "leaf", axis=0, tiled=True)

    def leaf_scatter(block):
        return lax.psum_scatter(block, "leaf", scatter_dimension=0, tiled=True)

    qkv_block = columns_in(w_query, w_key, w_value)
    gains_own = jnp.stack([gain_query, gain_key, gain_attn, gain_mlp]).astype(bf16).reshape(1, 4 * own)
    gains_leaf = gather_rows(gains_own).reshape(count * own, 4)
    attn_block = jnp.concatenate(
        [
            qkv_block,
            w_output.astype(bf16).reshape(count * own, part),
            jnp.pad(gains_leaf, ((0, 0), (0, HEAD_DIM - 4))),
        ],
        axis=1,
    )
    attn_mat = leaf_gather(attn_block)
    qkv_mat = attn_mat[:, : 3 * part]
    output_rows = attn_mat[:, 3 * part : 4 * part].reshape(count, leaves // count, own, width)
    gains_all = attn_mat[:, 4 * part : 4 * part + 4].reshape(leaves, count, 4, own)
    gains_all = jnp.moveaxis(gains_all, 2, 0).reshape(4, width).astype(f32)
    gate_block = columns_in(tie(w_gate, qkv_block))
    up_block = columns_in(tie(w_up, qkv_block))
    down_block = columns_in(tie(w_down, qkv_block))
    all_tokens = gather_rows(tie(tokens, gate_block, up_block, down_block))
    bias, cos_wide, sin_wide = tree_tables(seg_lengths[0], seg_parents[0], tree_len)

    query_pre, key_pre, value, squares = project(all_tokens, attn_mat, part)
    gate_mat = leaf_gather(gate_block)
    up_mat = leaf_gather(up_block)
    down_halves = [leaf_gather(down_block[h * group : (h + 1) * group]) for h in range(2)]

    squares = sum_rows(squares)
    scales = lax.rsqrt(squares / width + epsilon)
    query_scale, key_scale = scales[0][:, None], scales[1][:, None]
    attn_gain, mlp_gain = gains_all[2], gains_all[3]
    head_gains = lax.dynamic_slice_in_dim(gains_all[:2], me * part, part, 1)
    output_rows = tie(output_rows, scales)
    output_mat = jnp.zeros((leaves // count, count, own, width), bf16)
    for hop in range(count):
        piece = lax.dynamic_index_in_dim(output_rows, me ^ hop, 0, keepdims=False)
        if hop:
            piece = swap(piece, hop)
        output_mat = lax.dynamic_update_index_in_dim(output_mat, piece, me ^ hop, 1)
    output_mat = output_mat.reshape(part, width)
    query, key, context, lse = attend(
        query_pre, key_pre, value, scales.T, head_gains, cos_wide, sin_wide, bias
    )
    attn_pre = dot_scatter([context], [output_mat], NN)
    attn_scale = lax.rsqrt(jnp.mean(attn_pre * attn_pre, axis=-1, keepdims=True) + epsilon)
    attn_unit = attn_pre * attn_scale
    hidden = tokens.astype(f32) + attn_unit * attn_gain
    hidden_all = gather_rows(hidden.astype(bf16))

    gate_pre = dot(hidden_all, gate_mat, NN)
    up_pre = dot(hidden_all, up_mat, NN)
    sigmoid_gate = jax.nn.sigmoid(gate_pre)
    activated = (gate_pre * sigmoid_gate * up_pre).astype(bf16)
    mlp_halves = [dot_scatter([activated], [down_halves[h]], NT) for h in range(2)]
    grad_final = cotangent.reshape(rows_dev, width).astype(f32)
    halves = range(2)

    def split(rows):
        rows = rows.reshape(rows.shape[:-1] + (leaves, 2, group))
        return [rows[..., h, :].reshape(rows.shape[:-3] + (width // 2,)) for h in halves]

    weighted = tie(split(grad_final * mlp_gain), hidden_all)
    square = sum(jnp.sum(m * m, axis=-1, keepdims=True) for m in mlp_halves) / width
    cross = sum(jnp.sum(m * w, axis=-1, keepdims=True) for m, w in zip(mlp_halves, weighted)) / width
    mlp_scale = lax.rsqrt(square + epsilon)
    grad_mlp = [
        (mlp_scale * (w - m * (mlp_scale * mlp_scale * cross))).astype(bf16) for m, w in zip(mlp_halves, weighted)
    ]
    grad_mlp_halves = [gather_rows(grad_mlp[h]) for h in halves]
    down_sums = [dot(grad_mlp_halves[h], activated, TN, bf16) for h in range(2)]
    down_shards = [leaf_scatter(down_sums[h]) for h in range(2)]
    grad_act = dot(tie(grad_mlp_halves[0], down_sums[0]), down_halves[0], NN)
    grad_act = grad_act + dot(tie(grad_mlp_halves[1], down_sums[1]), down_halves[1], NN)
    grad_gate = (grad_act * up_pre * sigmoid_gate * (1.0 + gate_pre * (1.0 - sigmoid_gate))).astype(bf16)
    grad_up = (grad_act * gate_pre * sigmoid_gate).astype(bf16)
    gate_sum = tie(dot(hidden_all, grad_gate, TN, bf16), *down_sums)
    grad_hidden = grad_final + dot_scatter([grad_gate, grad_up], [gate_mat, up_mat], NT, gate_sum)
    gate_shard = leaf_scatter(gate_sum)

    grad_attn, grad_attn_gain = norm_back(grad_hidden, attn_unit, attn_scale, attn_gain)
    grad_attn_low = grad_attn.astype(bf16)
    up_sum = dot(hidden_all, tie(grad_up, grad_attn_low), TN, bf16)
    grad_attn_all = gather_rows(tie(grad_attn_low, *down_shards), up_sum)
    grad_context = dot(grad_attn_all, output_mat, NT, bf16)
    up_shard = leaf_scatter(tie(up_sum, gate_sum))
    grad_context = tie(grad_context, gate_shard)
    grad_query, grad_key, grad_value, inner_query, inner_key, grad_head_gains = attend_back(
        query, key, value, bias, lse, grad_context, query_pre, key_pre, scales.T, head_gains, cos_wide, sin_wide
    )
    inner = sum_rows(jnp.stack([jnp.sum(inner_query, axis=1), jnp.sum(inner_key, axis=1)])) / width
    output_part = dot(context, tie(grad_attn_all, inner), TN, bf16).reshape(leaves // count, count, own, width)
    grad_query_low = (
        query_scale * (grad_query * head_gains[0] - query_pre * (query_scale * inner[0][:, None]))
    ).astype(bf16)
    grad_key_low = (
        key_scale * (grad_key * head_gains[1] - key_pre * (key_scale * inner[1][:, None]))
    ).astype(bf16)
    grad_qkv = jnp.concatenate([grad_query_low, grad_key_low, grad_value], axis=1)
    gate_out = columns_out(tie(gate_shard, inner))
    down_out = columns_out(tie(jnp.concatenate(down_shards), inner))
    mlp_unit = jnp.stack([m.reshape(rows_dev, leaves, group) for m in mlp_halves], axis=2).reshape(rows_dev, width)
    mlp_unit = mlp_unit * mlp_scale
    outputs = (hidden + mlp_unit * mlp_gain).astype(bf16).reshape(inputs.shape)
    grad_mlp_gain = jnp.sum(grad_final * mlp_unit, axis=0)

    wide_part = jnp.stack([grad_attn_gain, grad_mlp_gain]).reshape(2, leaves, count, own)
    narrow_part = grad_head_gains.reshape(2, leaves // count, count, own)
    wide_sum = jnp.zeros((2, leaves, own), f32)
    narrow_all = jnp.zeros((2, leaves, own), f32)
    for hop in range(count):
        piece = lax.dynamic_index_in_dim(jnp.concatenate([wide_part, narrow_part], axis=1), me ^ hop, 2, keepdims=False)
        if hop:
            piece = swap(piece, hop)
        wide_sum = wide_sum + piece[:, :leaves]
        narrow_all = lax.dynamic_update_slice_in_dim(
            narrow_all, piece[:, leaves:], (me ^ hop) * (leaves // count), 1
        )
    grad_gains = jnp.concatenate([narrow_all, wide_sum], axis=0)
    stride = 1
    while stride < leaves:
        grad_gains = grad_gains + lax.ppermute(
            grad_gains, "leaf", [(i, i ^ stride) for i in range(leaves)]
        )
        stride *= 2
    grad_gains = lax.dynamic_index_in_dim(grad_gains, lax.axis_index("leaf"), 1, keepdims=False)
    grad_qkv = tie(grad_qkv, gate_out, down_out, outputs, grad_gains)
    if leaves == 8 and count == 4:
        *grad_mats, grad_output, grad_tokens, up_out = finish(
            all_tokens, grad_qkv, attn_mat, output_part, grad_hidden, up_shard
        )
        grad_inputs, up_out = grad_tokens.reshape(inputs.shape), [up_out]
    else:
        output_turned = jnp.zeros((count, leaves // count, own, width), bf16)
        for hop in range(count):
            piece = lax.dynamic_index_in_dim(output_part, me ^ hop, 1, keepdims=False)
            if hop:
                piece = swap(piece, hop)
            output_turned = lax.dynamic_update_index_in_dim(output_turned, piece, me ^ hop, 0)
        attn_sum = sums_beside(all_tokens, grad_qkv, output_turned.reshape(leaves * count * own, part))
        grad_tokens = grad_hidden + dot_scatter([grad_qkv], [qkv_mat], NT)
        grad_inputs = grad_tokens.astype(bf16).reshape(inputs.shape)
        attn_shard = leaf_scatter(tie(attn_sum, up_shard))
        up_out = columns_out(up_shard)
        grad_mats = columns_out(attn_shard[:, : 3 * part], 3)
        grad_output = attn_shard[:, 3 * part :].reshape(own, width).astype(f32)
    return (
        outputs,
        grad_inputs,
        *grad_mats,
        grad_output,
        grad_gains[0],
        grad_gains[1],
        grad_gains[2],
        *gate_out,
        *up_out,
        *down_out,
        grad_gains[3],
    )


def solution(mesh):
    both = ("leaf", "row")
    token_spec, tree_spec, matrix_spec, gain_spec = P("leaf", "row", None), P("leaf", None), P(both, None), P(both)
    return jax.shard_map(
        body,
        mesh=mesh,
        in_specs=(token_spec,) * 2 + (tree_spec,) * 2 + (matrix_spec,) * 4 + (gain_spec,) * 3 + (matrix_spec,) * 3 + (gain_spec,),
        out_specs=(token_spec,) * 2 + (matrix_spec,) * 4 + (gain_spec,) * 3 + (matrix_spec,) * 3 + (gain_spec,),
        check_vma=False,
    )
```

```python
import functools
import math

import jax
import jax.numpy as jnp
from jax import lax
from jax.experimental import pallas as pl
from jax.experimental.pallas import tpu as pltpu
from jax.sharding import PartitionSpec as P

HEAD_DIM = 128
MESH = pl.DeviceIdType.MESH

epsilon = 1e-06
rope_theta = 500000.0
masked_fill = -1e30
bf16 = jnp.bfloat16
f32 = jnp.float32
NN = (((1,), (0,)), ((), ()))
NT = (((1,), (1,)), ((), ()))
TN = (((0,), (0,)), ((), ()))


def dot(left, right, dims, kind=f32):
    return lax.dot_general(left, right, dims, preferred_element_type=f32).astype(kind)


def swap(piece, hop):
    count = lax.axis_size("row")
    return lax.ppermute(piece, "row", [(i, i ^ hop) for i in range(count)])


def gather_rows(rows, *meanwhile):
    count, me = lax.axis_size("row"), lax.axis_index("row")
    size = rows.shape[0]
    whole = jnp.zeros((count * size,) + rows.shape[1:], rows.dtype)
    for hop in range(1, count):
        whole = lax.dynamic_update_slice_in_dim(whole, swap(rows, hop), (me ^ hop) * size, 0)
    return lax.dynamic_update_slice_in_dim(whole, tie(rows, *meanwhile), me * size, 0)


def dot_scatter(lefts, rights, dims, *meanwhile):
    count, me = lax.axis_size("row"), lax.axis_index("row")
    size = lefts[0].shape[0] // count

    def rows_of(hop, lefts):
        parts = [lax.dynamic_slice_in_dim(left, (me ^ hop) * size, size, 0) for left in lefts]
        return sum(dot(part, right, dims) for part, right in zip(parts, rights))

    coming = [swap(rows_of(hop, lefts).astype(bf16), hop) for hop in reversed(range(1, count))]
    total = rows_of(0, [tie(left, *meanwhile) for left in lefts])
    for piece in coming:
        total = total + piece.astype(f32)
    return total


def send_rows(partial):
    count, me = lax.axis_size("row"), lax.axis_index("row")
    size = partial.shape[0] // count
    return [
        swap(lax.dynamic_slice_in_dim(partial, (me ^ hop) * size, size, 0), hop) for hop in reversed(range(1, count))
    ]


def add_rows(partial, coming, *meanwhile):
    size = partial.shape[0] // lax.axis_size("row")
    mine = lax.dynamic_slice_in_dim(tie(partial, *meanwhile), lax.axis_index("row") * size, size, 0)
    return sum([piece.astype(f32) for piece in coming], mine.astype(f32))


def tie(value, *others):
    return lax.optimization_barrier((value,) + others)[0]


def columns_in(*weights):
    count, me = lax.axis_size("row"), lax.axis_index("row")
    size, wide = weights[0].shape[0], weights[0].shape[1] // count
    whole = jnp.zeros((count * size, wide * len(weights)), bf16)
    for hop in range(count):
        piece = jnp.concatenate(
            [lax.dynamic_slice_in_dim(w, (me ^ hop) * wide, wide, 1).astype(bf16) for w in weights], axis=1
        )
        if hop:
            piece = swap(piece, hop)
        whole = lax.dynamic_update_slice_in_dim(whole, piece, (me ^ hop) * size, 0)
    return whole


def columns_out(block, many=1):
    count, me = lax.axis_size("row"), lax.axis_index("row")
    size, wide = block.shape[0] // count, block.shape[1] // many
    whole = [jnp.zeros((size, wide * count), f32)] * many
    for hop in range(count):
        piece = lax.dynamic_slice_in_dim(block, (me ^ hop) * size, size, 0)
        if hop:
            piece = swap(piece, hop)
        for i in range(many):
            own = piece[:, i * wide : (i + 1) * wide].astype(f32)
            whole[i] = lax.dynamic_update_slice_in_dim(whole[i], own, (me ^ hop) * wide, 1)
    return whole


def sum_rows(small):
    count = lax.axis_size("row")
    total = small
    for hop in range(1, count):
        total = total + swap(small, hop)
    return total


def norm_back(grad_out, unit_rows, scaled, gain_row):
    weighted = grad_out * gain_row
    inner = jnp.mean(weighted * unit_rows, axis=-1, keepdims=True)
    return (scaled * (weighted - unit_rows * inner), jnp.sum(grad_out * unit_rows, axis=0))


def tree_tables(length_row, parent_row, total):
    seg_count = parent_row.shape[0]
    segment_ids = jnp.arange(seg_count, dtype=jnp.int32)
    ends = jnp.cumsum(length_row)
    offsets = ends - length_row
    all_rows = jnp.arange(total, dtype=jnp.int32)
    owned_from = (all_rows[:, None] >= offsets[None, :]).astype(f32)
    onehot_all = owned_from - jnp.concatenate(
        [owned_from[:, 1:], jnp.zeros((total, 1), f32)], axis=1
    )
    parents = jnp.sum(onehot_all * parent_row.astype(f32)[None, :], axis=1)
    segments = jnp.sum(onehot_all * segment_ids.astype(f32)[None, :], axis=1)
    lengths = length_row.astype(f32)
    parent_lengths = jnp.sum((parent_row[:, None] == segment_ids[None, :]) * lengths[None, :], axis=1)
    above = jnp.where(segment_ids > 0, lengths[0], 0.0) + jnp.where(parent_row > 0, parent_lengths, 0.0)
    position = all_rows.astype(f32) + jnp.sum(onehot_all * (above - offsets.astype(f32))[None, :], axis=1)
    on_path = (segments[:, None] == segments[None, :]) | (segments[:, None] == parents[None, :]) | (segments[:, None] == 0.0)
    allowed = on_path & (all_rows[:, None] <= all_rows[None, :])
    bias = jnp.where(allowed, 0.0, masked_fill).astype(bf16)
    frequency = jnp.exp(
        jnp.arange(HEAD_DIM // 2, dtype=f32) * (-2.0 * math.log(rope_theta) / HEAD_DIM)
    )
    angles = position[:, None] * frequency[None, :]
    cos_half, sin_half = jnp.cos(angles), jnp.sin(angles)
    cos_wide = jnp.concatenate([cos_half, cos_half], axis=1)
    sin_wide = jnp.concatenate([-sin_half, sin_half], axis=1)
    return (bias, cos_wide, sin_wide)


def turn(vector, cos_part, sin_part):
    return vector * cos_part + pltpu.roll(vector, HEAD_DIM // 2, 1) * sin_part


def project_kernel(tokens_ref, weights_ref, query_ref, key_ref, value_ref, squares_ref):
    part = query_ref.shape[1]
    tokens = tokens_ref[...]
    for i, out_ref in enumerate((query_ref, key_ref)):
        product = dot(tokens, weights_ref[:, i * part : (i + 1) * part], NN)
        out_ref[...] = product
        square = jnp.sum(product * product, axis=1, keepdims=True)
        squares_ref[i : i + 1, :] = jnp.broadcast_to(square, (square.shape[0], HEAD_DIM)).T[0:1]
    value_ref[...] = dot(tokens, weights_ref[:, 2 * part :], NN, bf16)


def project(tokens, weights, part):
    total, width = tokens.shape
    size = 256
    rows = pl.BlockSpec((size, part), lambda i: (i, 0))
    wide = jax.ShapeDtypeStruct((total, part), f32)
    return pl.pallas_call(
        project_kernel,
        grid=(total // size,),
        in_specs=[
            pl.BlockSpec((size, width), lambda i: (i, 0)),
            pl.BlockSpec((width, 3 * part), lambda i: (0, 0)),
        ],
        out_specs=[rows, rows, rows, pl.BlockSpec((2, size), lambda i: (0, i))],
        out_shape=[
            wide,
            wide,
            jax.ShapeDtypeStruct((total, part), bf16),
            jax.ShapeDtypeStruct((2, total), f32),
        ],
        compiler_params=pltpu.CompilerParams(vmem_limit_bytes=48 * 2**20),
        cost_estimate=pl.CostEstimate(
            flops=6 * total * width * part, bytes_accessed=2 * width * (total + 3 * part) + 10 * total * part, transcendentals=0
        ),
    )(tokens, weights)


def attend_kernel(
    block,
    scale,
    query_pre_ref,
    key_pre_ref,
    value_ref,
    scales_ref,
    gains_ref,
    cos_ref,
    sin_ref,
    bias_ref,
    query_ref,
    key_ref,
    context_ref,
    lse_ref,
):
    total = key_ref.shape[0]
    cos_part, sin_part = cos_ref[...], sin_ref[...]
    query_ref[...] = turn(query_pre_ref[...] * scales_ref[:, 0:1] * gains_ref[0:1], cos_part, sin_part).astype(bf16)
    key_ref[...] = turn(key_pre_ref[...] * scales_ref[:, 1:2] * gains_ref[1:2], cos_part, sin_part).astype(bf16)
    for first in range(0, total, block):
        last = first + block
        scores = dot(key_ref[:last], query_ref[first:last], NT) * scale
        scores = scores + bias_ref[:last, first:last].astype(f32)
        top = jnp.max(scores, axis=0, keepdims=True)
        probs = jnp.exp(scores - top)
        mass = jnp.sum(probs, axis=0, keepdims=True)
        probs_low = (probs * (1.0 / mass)).astype(bf16)
        turned = dot(value_ref[:last], probs_low, TN)
        context_ref[first:last, :] = turned.T.astype(bf16)
        lse_ref[:, first:last] = jnp.broadcast_to(top + jnp.log(mass), (8, block))


def head_specs(total):
    part = pl.BlockSpec((total, HEAD_DIM), lambda h: (0, h))
    whole = pl.BlockSpec((total, HEAD_DIM), lambda h: (0, 0))
    gains = pl.BlockSpec((2, HEAD_DIM), lambda h: (0, h))
    scales = pl.BlockSpec((total, 2), lambda h: (0, 0))
    bias = pl.BlockSpec((total, total), lambda h: (0, 0))
    lse = pl.BlockSpec((8, total), lambda h: (h, 0))
    return part, whole, gains, scales, bias, lse


def attend(query_pre, key_pre, value, scales, gains, cos_wide, sin_wide, bias):
    total, width = query_pre.shape
    heads = width // HEAD_DIM
    part, whole, gain, scale, square, lse = head_specs(total)
    low = jax.ShapeDtypeStruct((total, width), bf16)
    return pl.pallas_call(
        functools.partial(attend_kernel, 256, 1.0 / math.sqrt(HEAD_DIM)),
        grid=(heads,),
        in_specs=[part, part, part, scale, gain, whole, whole, square],
        out_specs=[part, part, part, lse],
        out_shape=[low, low, low, jax.ShapeDtypeStruct((8 * heads, total), f32)],
        compiler_params=pltpu.CompilerParams(vmem_limit_bytes=56 * 2**20),
        cost_estimate=pl.CostEstimate(
            flops=4 * total * total * width, bytes_accessed=16 * total * width, transcendentals=total * total * heads
        ),
    )(query_pre, key_pre, value, scales, gains, cos_wide, sin_wide, bias)


def attend_back_kernel(
    block,
    scale,
    query_ref,
    key_ref,
    value_ref,
    bias_ref,
    lse_ref,
    grad_ref,
    query_pre_ref,
    key_pre_ref,
    scales_ref,
    gains_ref,
    cos_ref,
    sin_ref,
    grad_query_ref,
    grad_key_ref,
    grad_value_ref,
    inner_query_ref,
    inner_key_ref,
    grad_gains_ref,
    key_sum,
    value_sum,
):
    total = key_ref.shape[0]

    @pl.when(pl.program_id(0) == 0)
    def _():
        inner_query_ref[...] = jnp.zeros_like(inner_query_ref)
        inner_key_ref[...] = jnp.zeros_like(inner_key_ref)

    key_sum[...] = jnp.zeros_like(key_sum)
    value_sum[...] = jnp.zeros_like(value_sum)
    for first in range(0, total, block):
        last = first + block
        scores = dot(key_ref[:last], query_ref[first:last], NT) * scale
        scores = scores + bias_ref[:last, first:last].astype(f32)
        probs = jnp.exp(scores - lse_ref[0:1, first:last])
        grad_probs = dot(value_ref[:last], grad_ref[first:last], NT)
        inner = jnp.sum(probs * grad_probs, axis=0, keepdims=True)
        grad_scores = (probs * (grad_probs - inner)).astype(bf16)
        turned = dot(key_ref[:last], grad_scores, TN)
        grad_query_ref[first:last, :] = turned.T
        key_sum[:last, :] += dot(grad_scores, query_ref[first:last], NN)
        value_sum[:last, :] += dot(probs.astype(bf16), grad_ref[first:last], NN)
    grad_value_ref[...] = value_sum[...].astype(bf16)
    cos_part, sin_part = cos_ref[...], -sin_ref[...]
    for row, (grad, out_ref, pre_ref, inner_ref) in enumerate(
        (
            (grad_query_ref[...], grad_query_ref, query_pre_ref, inner_query_ref),
            (key_sum[...], grad_key_ref, key_pre_ref, inner_key_ref),
        )
    ):
        grad = turn(grad * scale, cos_part, sin_part)
        by_unit = grad * (pre_ref[...] * scales_ref[:, row : row + 1])
        inner_ref[...] += by_unit * gains_ref[row : row + 1]
        grad_gains_ref[row : row + 1, :] = jnp.sum(by_unit, axis=0, keepdims=True)
        out_ref[...] = grad


def attend_back(query, key, value, bias, lse, grad_context, query_pre, key_pre, scales, gains, cos_wide, sin_wide):
    total, width = query.shape
    heads = width // HEAD_DIM
    part, whole, gain, scale, square, lse_spec = head_specs(total)
    wide = jax.ShapeDtypeStruct((total, width), f32)
    narrow = jax.ShapeDtypeStruct((total, HEAD_DIM), f32)
    return pl.pallas_call(
        functools.partial(attend_back_kernel, 256, 1.0 / math.sqrt(HEAD_DIM)),
        grid=(heads,),
        in_specs=[part, part, part, square, lse_spec, part, part, part, scale, gain, whole, whole],
        out_specs=[part, part, part, whole, whole, gain],
        out_shape=[
            wide,
            wide,
            jax.ShapeDtypeStruct((total, width), bf16),
            narrow,
            narrow,
            jax.ShapeDtypeStruct((2, width), f32),
        ],
        scratch_shapes=[pltpu.VMEM((total, HEAD_DIM), f32)] * 2,
        compiler_params=pltpu.CompilerParams(vmem_limit_bytes=58 * 2**20),
        cost_estimate=pl.CostEstimate(
            flops=10 * total * total * width, bytes_accessed=30 * total * width, transcendentals=total * total * heads
        ),
    )(query, key, value, bias, lse, grad_context, query_pre, key_pre, scales, gains, cos_wide, sin_wide)


def sums_kernel(tokens_ref, grads_ref, side_ref, out_ref):
    wide = grads_ref.shape[1]
    out_ref[:, :wide] = dot(tokens_ref[...], grads_ref[...], TN, bf16)
    out_ref[:, wide:] = side_ref[...]


def sums_beside(tokens, grads, side):
    total, rows = tokens.shape
    wide, extra = grads.shape[1], side.shape[1]
    size = 256
    return pl.pallas_call(
        sums_kernel,
        grid=(rows // size,),
        in_specs=[
            pl.BlockSpec((total, size), lambda i: (0, i)),
            pl.BlockSpec((total, wide), lambda i: (0, 0)),
            pl.BlockSpec((size, extra), lambda i: (i, 0)),
        ],
        out_specs=pl.BlockSpec((size, wide + extra), lambda i: (i, 0)),
        out_shape=jax.ShapeDtypeStruct((rows, wide + extra), bf16),
        compiler_params=pltpu.CompilerParams(vmem_limit_bytes=40 * 2**20),
        cost_estimate=pl.CostEstimate(
            flops=2 * total * rows * wide, bytes_accessed=2 * rows * (total + wide + 2 * extra), transcendentals=0
        ),
    )(tokens, grads, side)


def landed(ref, sem):
    pltpu.make_async_copy(ref, ref, sem).wait()


def line_order(z):
    far, inner = z // 2, ((z + 1) // 2) % 2
    blocks = []
    for end, middle in ((3, 0), (2, 2), (1, 3), (0, 1)):
        first = end + inner * (middle - end)
        blocks.append(first + far * (3 - 2 * first))
    near = 1 + far
    chips = [near + inner * (blocks[0] - near), blocks[1], blocks[2]]
    slots = [3 + inner * (-2 - far), 2 + inner * (far - 2), far + inner * (2 - far)]
    return far, inner, blocks, chips, slots


def other(index, hop):
    return (index, index + 1 - 2 * (index % 2), (index + 2) % 4, 3 - index)[hop]


def final_kernel(
    tokens_hbm,
    grads_hbm,
    weights_hbm,
    output_hbm,
    hidden_hbm,
    up_hbm,
    gains_hbm,
    query_out,
    key_out,
    value_out,
    output_out,
    inputs_out,
    up_out,
    gains_out,
    tokens,
    grads,
    weights,
    hidden,
    core_out,
    core_in,
    mine,
    line_in,
    side,
    side_in,
    side_mine,
    side_line_in,
    tokens_send,
    tokens_in,
    rows_send,
    rows_in,
    up_in,
    gains,
    gains_in,
    gains_line,
    load_sem,
    row_send_sem,
    row_recv_sem,
    core_send_sem,
    core_recv_sem,
    line_send_sem,
    line_recv_sem,
    leaf_send_sem,
    leaf_recv_sem,
):
    leaf, row = lax.axis_index("leaf"), lax.axis_index("row")
    z, core = leaf // 2, leaf % 2
    far, inner, blocks, chips, slots = line_order(z)
    wide, own = grads.shape[1], query_out.shape[0]
    part, size = wide // 3, mine.shape[1]
    rows = tokens_in.shape[1]
    hops = (3, 1, 2)

    loads = [
        pltpu.make_async_copy(tokens_hbm, tokens, load_sem.at[0]),
        pltpu.make_async_copy(grads_hbm, grads, load_sem.at[1]),
        pltpu.make_async_copy(weights_hbm.at[:, pl.ds(0, wide)], weights, load_sem.at[2]),
        pltpu.make_async_copy(hidden_hbm, hidden, load_sem.at[3]),
        pltpu.make_async_copy(output_hbm.at[:, row], side.at[pl.ds(2 * row, 2)], load_sem.at[4]),
        pltpu.make_async_copy(gains_hbm.at[row], gains, load_sem.at[6]),
    ]
    for load in loads:
        load.start()
    barrier = pltpu.get_barrier_semaphore()
    for hop in hops:
        pl.semaphore_signal(barrier, inc=1, device_id={"row": other(row, hop)}, device_id_type=MESH)
    for step in range(1, 8):
        pl.semaphore_signal(barrier, inc=1, device_id={"leaf": (leaf + step) % 8}, device_id_type=MESH)
    pl.semaphore_wait(barrier, 10)

    sent = []

    def row_copy(source, target, kind, hop):
        copy = pltpu.make_async_remote_copy(
            source,
            target,
            row_send_sem.at[kind, hop - 1],
            row_recv_sem.at[kind, hop - 1],
            device_id={"row": other(row, hop)},
            device_id_type=MESH,
        )
        copy.start()
        sent.append(copy)

    def core_copy(source, target, kind, i):
        copy = pltpu.make_async_remote_copy(
            source,
            target,
            core_send_sem.at[kind, i],
            core_recv_sem.at[kind, i],
            device_id={"leaf": 2 * z + 1 - core},
            device_id_type=MESH,
        )
        copy.start()
        sent.append(copy)

    def line_copy(source, target, kind, i):
        return pltpu.make_async_remote_copy(
            source,
            target.at[slots[i]],
            line_send_sem.at[kind, i],
            line_recv_sem.at[kind, slots[i]],
            device_id={"leaf": 2 * chips[i] + core},
            device_id_type=MESH,
        )

    for hop in hops:
        row_copy(gains_hbm.at[other(row, hop)], gains_in.at[hop - 1], 4, hop)
    for hop in hops:
        row_copy(output_hbm.at[:, other(row, hop)], side.at[pl.ds(2 * row, 2)], 0, hop)

    loads[0].wait()
    loads[1].wait()

    def product(block):
        return dot(tokens[:, pl.ds(pl.multiple_of(block * size, size), size)], grads[...], TN)

    for i in range(4):
        core_out[i] = product(2 * blocks[i] + 1 - core).astype(bf16)
        core_copy(core_out.at[i], core_in.at[i], 0, i)

    def pair(i):
        mine[i] = (product(2 * blocks[i] + core) + core_in[i].astype(f32)).astype(bf16)

    for i in range(4):
        landed(core_in.at[i], core_recv_sem.at[0, i])
        pair(i)
        if i < 2:
            copy = line_copy(mine.at[i], line_in, 0, i)
            copy.start()
            sent.append(copy)
        if i == 2:
            last = line_copy(mine.at[2], line_in, 0, 2)
            sent.append(last)

            @pl.when(inner == 0)
            def _():
                last.start()

    loads[5].wait()
    for hop in hops:
        landed(gains_in.at[hop - 1], row_recv_sem.at[4, hop - 1])
        gains[...] += gains_in[hop - 1]
    for step in range(1, 8):
        copy = pltpu.make_async_remote_copy(
            gains.at[(leaf + step) % 8],
            gains_line.at[step - 1],
            leaf_send_sem.at[step - 1],
            leaf_recv_sem.at[step - 1],
            device_id={"leaf": (leaf + step) % 8},
            device_id_type=MESH,
        )
        copy.start()
        sent.append(copy)

    loads[2].wait()

    def tokens_part(hop, store):
        lines = grads[pl.ds(pl.multiple_of((other(row, hop)) * rows, rows), rows), :]

        def step(j, carry):
            columns = pl.ds(pl.multiple_of(j * part, part), part)
            store(columns, dot(lines, weights[columns, :], NT))
            return carry

        lax.fori_loop(0, weights.shape[0] // part, step, 0)

    for hop in hops:

        def store(columns, values):
            tokens_send[hop - 1, :, columns] = values.astype(bf16)

        tokens_part(hop, store)
        row_copy(tokens_send.at[hop - 1], tokens_in.at[hop - 1], 1, hop)

    loads[4].wait()
    for hop in hops:
        landed(side.at[pl.ds(2 * (other(row, hop)), 2)], row_recv_sem.at[0, hop - 1])
    for i in range(4):
        core_copy(side.at[2 * blocks[i] + 1 - core], side_in.at[i], 1, i)

    for hop in hops:
        row_copy(up_hbm.at[pl.ds((other(row, hop)) * own, own)], up_in.at[row], 2, hop)
    keep = pltpu.make_async_copy(up_hbm.at[pl.ds(row * own, own)], up_in.at[row], load_sem.at[5])
    keep.start()

    @pl.when(inner == 1)
    def _():
        landed(line_in.at[3], line_recv_sem.at[0, 3])
        mine[2] = (mine[2].astype(f32) + line_in[3].astype(f32)).astype(bf16)
        last.start()

    for i in range(4):
        landed(side_in.at[i], core_recv_sem.at[1, i])
        side_mine[i] = (side[2 * blocks[i] + core].astype(f32) + side_in[i].astype(f32)).astype(bf16)
        if i < 2:
            copy = line_copy(side_mine.at[i], side_line_in, 1, i)
            copy.start()
            sent.append(copy)
        if i == 2:
            side_last = line_copy(side_mine.at[2], side_line_in, 1, 2)
            sent.append(side_last)

            @pl.when(inner == 0)
            def _():
                side_last.start()

    loads[3].wait()

    def own_store(columns, values):
        hidden[:, columns] += values

    tokens_part(0, own_store)

    def total(kind, came, kept):
        landed(came.at[2], line_recv_sem.at[kind, 2])
        kept[3] = (kept[3].astype(f32) + came[2].astype(f32)).astype(bf16)
        for slot in range(2):

            @pl.when(inner + (1 - far) * slot + far * (1 - slot) > 0)
            def _():
                landed(came.at[slot], line_recv_sem.at[kind, slot])
                kept[3] = (kept[3].astype(f32) + came[slot].astype(f32)).astype(bf16)

    @pl.when(inner == 1)
    def _():
        landed(side_line_in.at[3], line_recv_sem.at[1, 3])
        side_mine[2] = (side_mine[2].astype(f32) + side_line_in[3].astype(f32)).astype(bf16)
        side_last.start()

    for hop in hops:
        landed(tokens_in.at[hop - 1], row_recv_sem.at[1, hop - 1])
        hidden[...] += tokens_in[hop - 1].astype(f32)
    inputs_out[...] = hidden[...].astype(bf16)

    keep.wait()
    for hop in hops:
        landed(up_in.at[other(row, hop)], row_recv_sem.at[2, hop - 1])
    for source in range(4):
        up_out[:, source * up_in.shape[2] : (source + 1) * up_in.shape[2]] = up_in[source].astype(f32)

    gains_out[...] = gains[leaf]
    for step in range(1, 8):
        landed(gains_line.at[step - 1], leaf_recv_sem.at[step - 1])
        gains_out[...] += gains_line[step - 1]

    total(0, line_in, mine)
    rows_send[...] = mine[3]
    for hop in hops:
        row_copy(rows_send.at[pl.ds((other(row, hop)) * own, own)], rows_in.at[hop - 1], 3, hop)

    def give(source, values):
        columns = pl.ds(pl.multiple_of(source * part, part), part)
        for i, out in enumerate((query_out, key_out, value_out)):
            out[:, columns] = values[:, i * part : (i + 1) * part].astype(f32)

    give(row, rows_send[pl.ds(pl.multiple_of(row * own, own), own), :])
    total(1, side_line_in, side_mine)
    output_out[...] = side_mine[3].astype(f32)
    for hop in hops:
        landed(rows_in.at[hop - 1], row_recv_sem.at[3, hop - 1])
        give(other(row, hop), rows_in[hop - 1])
    for copy in sent:
        copy.wait_send()


def finish(tokens, grads, weights, output_part, hidden, up_shard, gain_part):
    total, width = tokens.shape
    wide = grads.shape[1]
    own = output_part.shape[2]
    size, rows, units = 4 * own, hidden.shape[0], up_shard.shape[1]
    matrix = jax.ShapeDtypeStruct((own, width), f32)
    dma = pltpu.SemaphoreType.DMA
    return pl.pallas_call(
        final_kernel,
        in_specs=[pl.BlockSpec(memory_space=pl.ANY)] * 7,
        out_specs=[pl.BlockSpec(memory_space=pltpu.VMEM)] * 7,
        out_shape=[
            matrix,
            matrix,
            matrix,
            matrix,
            jax.ShapeDtypeStruct((rows, width), bf16),
            jax.ShapeDtypeStruct((own, 4 * units), f32),
            jax.ShapeDtypeStruct((8, HEAD_DIM), f32),
        ],
        scratch_shapes=[
            pltpu.VMEM((total, width), bf16),
            pltpu.VMEM((total, wide), bf16),
            pltpu.VMEM((width, wide), bf16),
            pltpu.VMEM((rows, width), f32),
            pltpu.VMEM((4, size, wide), bf16),
            pltpu.VMEM((4, size, wide), bf16),
            pltpu.VMEM((4, size, wide), bf16),
            pltpu.VMEM((4, size, wide), bf16),
            pltpu.VMEM((8, own, width), bf16),
            pltpu.VMEM((4, own, width), bf16),
            pltpu.VMEM((4, own, width), bf16),
            pltpu.VMEM((4, own, width), bf16),
            pltpu.VMEM((3, rows, width), bf16),
            pltpu.VMEM((3, rows, width), bf16),
            pltpu.VMEM((size, wide), bf16),
            pltpu.VMEM((3, own, wide), bf16),
            pltpu.VMEM((4, own, units), bf16),
            pltpu.VMEM((8, 8, HEAD_DIM), f32),
            pltpu.VMEM((3, 8, 8, HEAD_DIM), f32),
            pltpu.VMEM((7, 8, HEAD_DIM), f32),
            dma((7,)),
            dma((5, 3)),
            dma((5, 3)),
            dma((2, 4)),
            dma((2, 4)),
            dma((2, 3)),
            dma((2, 4)),
            dma((7,)),
            dma((7,)),
        ],
        compiler_params=pltpu.CompilerParams(
            collective_id=1, has_side_effects=True, vmem_limit_bytes=60 * 2**20
        ),
        cost_estimate=pl.CostEstimate(
            flops=4 * total * width * wide, bytes_accessed=100 * 2**20, transcendentals=0
        ),
    )(tokens, grads, weights, output_part, hidden, up_shard, gain_part)


def front_kernel(
    tokens_hbm,
    pack_hbm,
    output_hbm,
    gate_hbm,
    up_hbm,
    down_hbm,
    gains_hbm,
    cos_hbm,
    sin_hbm,
    bias_hbm,
    attn_out,
    gate_out,
    up_out,
    down_out,
    tokens_out,
    query_pre_out,
    key_pre_out,
    value_out,
    scales_out,
    query_out,
    key_out,
    context_out,
    lse_out,
    output_out,
    unit_out,
    unit_scale_out,
    hidden_out,
    hidden_all_out,
    gains_out,
    block,
    attn_mat,
    gate_block,
    up_block,
    down_block,
    tokens,
    query_pre,
    key_pre,
    value,
    query,
    key,
    context,
    lse,
    bias,
    cos_part,
    sin_part,
    scale_columns,
    output_in,
    output_mat,
    rows_send,
    rows_in,
    half_in,
    attn,
    unit_scale,
    hidden,
    hidden_all,
    squares,
    squares_in,
    scale_rows,
    gains_leaf,
    gains_all,
    gains,
    load_sem,
    save_sem,
    row_send_sem,
    row_recv_sem,
    leaf_send_sem,
    leaf_recv_sem,
    core_send_sem,
    core_recv_sem,
    line_send_sem,
    line_recv_sem,
):
    leaf, row = lax.axis_index("leaf"), lax.axis_index("row")
    z, core = leaf // 2, leaf % 2
    far, inner = z // 2, ((z + 1) // 2) % 2
    own = pack_hbm.shape[1]
    wide = pack_hbm.shape[2]
    part, size = wide // 3, 4 * own
    rows, width = tokens_hbm.shape
    units = gate_block.shape[1]
    heads = part // HEAD_DIM
    scale = 1.0 / math.sqrt(HEAD_DIM)
    hops = (3, 1, 2)
    sent, saved = [], []

    def lines(index, count):
        return pl.ds(pl.multiple_of(index * count, count), count)

    def load(source, target, i):
        copy = pltpu.make_async_copy(source, target, load_sem.at[i])
        copy.start()
        return copy

    def save(source, target):
        copy = pltpu.make_async_copy(source, target, save_sem.at[len(saved)])
        copy.start()
        saved.append(copy)

    mine = lines(row, own)
    load_pack = load(pack_hbm.at[row], block.at[mine, pl.ds(0, wide)], 0)
    load_output = load(output_hbm, block.at[:, pl.ds(wide, part)], 1)
    load_gains = load(gains_hbm, gains_leaf.at[row], 2)
    load_gate = load(gate_hbm.at[:, lines(row, units)], gate_block.at[mine], 3)
    load_tokens = load(tokens_hbm, tokens.at[lines(row, rows)], 4)
    load_up = load(up_hbm.at[:, lines(row, units)], up_block.at[mine], 5)
    load_down = load(down_hbm.at[:, lines(row, units)], down_block.at[mine], 6)
    load_tables = [load(cos_hbm, cos_part, 7), load(sin_hbm, sin_part, 8), load(bias_hbm, bias, 9)]

    barrier = pltpu.get_barrier_semaphore()
    for hop in hops:
        pl.semaphore_signal(barrier, inc=1, device_id={"row": other(row, hop)}, device_id_type=MESH)
    for step in range(1, 8):
        pl.semaphore_signal(barrier, inc=1, device_id={"leaf": (leaf + step) % 8}, device_id_type=MESH)
    pl.semaphore_wait(barrier, 10)

    def row_copy(source, target, kind, hop):
        copy = pltpu.make_async_remote_copy(
            source,
            target,
            row_send_sem.at[kind, hop - 1],
            row_recv_sem.at[kind, hop - 1],
            device_id={"row": other(row, hop)},
            device_id_type=MESH,
        )
        copy.start()
        sent.append(copy)

    def row_landed(target, kind):
        for hop in hops:
            landed(target(other(row, hop), hop), row_recv_sem.at[kind, hop - 1])

    def leaf_copy(source, target, send_sem, recv_sem, to):
        return pltpu.make_async_remote_copy(
            source, target, send_sem, recv_sem, device_id={"leaf": to}, device_id_type=MESH
        )

    for hop in hops:
        row_copy(pack_hbm.at[other(row, hop)], block.at[mine, pl.ds(0, wide)], 0, hop)
    for hop in hops:
        row_copy(gains_hbm, gains_leaf.at[row], 1, hop)
    for hop in hops:
        row_copy(gate_hbm.at[:, lines(other(row, hop), units)], gate_block.at[mine], 2, hop)
    for hop in hops:
        row_copy(tokens_hbm, tokens.at[lines(row, rows)], 3, hop)
    for hop in hops:
        row_copy(up_hbm.at[:, lines(other(row, hop), units)], up_block.at[mine], 4, hop)
    for hop in hops:
        row_copy(down_hbm.at[:, lines(other(row, hop), units)], down_block.at[mine], 5, hop)

    def spread(kind, source, whole):
        place = whole.at[lines(leaf, size)]
        across = leaf_copy(
            source, place, line_send_sem.at[kind, 2], line_recv_sem.at[kind, 2], 2 * other(z, 2) + core
        )
        across.start()
        sent.append(across)
        forth = leaf_copy(source, place, line_send_sem.at[kind, 0], line_recv_sem.at[kind, 0], 2 * z + 2 + core)
        back = leaf_copy(source, place, line_send_sem.at[kind, 1], line_recv_sem.at[kind, 1], 2 * z - 2 + core)

        @pl.when(z < 3)
        def _():
            forth.start()

        @pl.when(z > 0)
        def _():
            back.start()

        beside = leaf_copy(source, place, core_send_sem.at[kind, 3], core_recv_sem.at[kind, 3], 2 * z + 1 - core)
        beside.start()
        sent.append(beside)
        save(source, place)

        def done():
            @pl.when(z < 3)
            def _():
                forth.wait_send()

            @pl.when(z > 0)
            def _():
                back.wait_send()

        return done

    def arrival(step):
        inner_slot, inner_chip = ((2, other(z, 2)), (0, z - 1), (1, z + 1))[step]
        end_slot, end_chip = ((1 - far, 1 + far), (2, other(z, 2)), (3, 3 - z))[step]
        return end_slot + inner * (inner_slot - end_slot), end_chip + inner * (inner_chip - end_chip)

    def pass_on(kind, whole, step):
        slot, chip = arrival(step)
        place = whole.at[lines(2 * chip + core, size)]
        landed(place, line_recv_sem.at[kind, slot])
        beside = leaf_copy(place, place, core_send_sem.at[kind, step], core_recv_sem.at[kind, step], 2 * z + 1 - core)
        beside.start()
        sent.append(beside)
        if step == 0:
            onward = leaf_copy(place, place, line_send_sem.at[kind, 3], line_recv_sem.at[kind, 3], 6 * far + core)

            @pl.when(inner == 1)
            def _():
                onward.start()

            def done():
                @pl.when(inner == 1)
                def _():
                    onward.wait_send()

            return done

    def gathered(kind, whole):
        landed(whole.at[lines(2 * z + 1 - core, size)], core_recv_sem.at[kind, 3])
        for step in range(3):
            chip = arrival(step)[1]
            landed(whole.at[lines(2 * chip + 1 - core, size)], core_recv_sem.at[kind, step])

    load_pack.wait()
    load_output.wait()
    row_landed(lambda source, hop: block.at[lines(source, own), pl.ds(0, wide)], 0)
    done = [spread(0, block, attn_mat)]

    load_gains.wait()
    row_landed(lambda source, hop: gains_leaf.at[source], 1)
    for step in range(1, 8):
        copy = leaf_copy(
            gains_leaf, gains_all.at[leaf], leaf_send_sem.at[step - 1], leaf_recv_sem.at[step - 1], (leaf + step) % 8
        )
        copy.start()
        sent.append(copy)
    gains_all[leaf] = gains_leaf[...]

    load_gate.wait()
    row_landed(lambda source, hop: gate_block.at[lines(source, own)], 2)
    done.append(pass_on(0, attn_mat, 0))
    pass_on(0, attn_mat, 1)
    done.append(spread(1, gate_block, gate_out))
    pass_on(0, attn_mat, 2)
    gathered(0, attn_mat)
    saved[0].wait()

    load_tokens.wait()
    row_landed(lambda source, hop: tokens.at[lines(source, rows)], 3)

    def project_step(j, carry):
        at = lines(j, rows)
        some = tokens[at, :]
        for i, out in enumerate((query_pre, key_pre)):
            product = dot(some, attn_mat[:, i * part : (i + 1) * part], NN)
            out[at, :] = product
            square = jnp.sum(product * product, axis=1, keepdims=True)
            squares[i : i + 1, at] = jnp.broadcast_to(square, (rows, HEAD_DIM)).T[0:1]
        value[at, :] = dot(some, attn_mat[:, 2 * part : wide], NN, bf16)
        return carry

    squares[...] = jnp.zeros_like(squares)
    lax.fori_loop(0, 4, project_step, 0)
    for hop in hops:
        row_copy(squares, squares_in.at[hop - 1], 7, hop)
    for hop in hops:
        row_copy(
            attn_mat.at[lines(other(row, hop), 2 * size), pl.ds(wide, part)], output_in.at[row], 6, hop
        )
    keep = load(attn_mat.at[lines(row, 2 * size), pl.ds(wide, part)], output_in.at[row], 10)
    load_up.wait()
    row_landed(lambda source, hop: up_block.at[lines(source, own)], 4)
    done.append(spread(2, up_block, up_out))
    save(attn_mat, attn_out)
    save(tokens, tokens_out)
    save(query_pre, query_pre_out)
    save(key_pre, key_pre_out)
    save(value, value_out)
    for step in range(1, 8):
        landed(gains_all.at[(leaf - step + 8) % 8], leaf_recv_sem.at[step - 1])
    for source in range(8):
        for pair in range(2):
            first = (2 * source + pair) * HEAD_DIM
            gains[:, first : first + HEAD_DIM] = gains_all[source, 2 * pair] + gains_all[source, 2 * pair + 1]
    save(gains, gains_out)
    for table in load_tables:
        table.wait()
    row_landed(lambda source, hop: squares_in.at[hop - 1], 7)
    scales = lax.rsqrt((squares[...] + squares_in[0] + squares_in[1] + squares_in[2]) / width + epsilon)
    scale_rows[...] = scales
    save(scale_rows, scales_out)
    for i in range(2):
        scale_columns[i] = jnp.broadcast_to(scales[i : i + 1], (HEAD_DIM, 4 * rows)).T

    def head_step(h, carry):
        at = lines(h, HEAD_DIM)
        at_gain = lines(row * heads + h, HEAD_DIM)
        for i, (pre, out) in enumerate(((query_pre, query), (key_pre, key))):
            scaled = pre[:, at] * scale_columns[i] * gains[i : i + 1, at_gain]
            out[:, at] = turn(scaled, cos_part[...], sin_part[...]).astype(bf16)
        for first in range(0, 4 * rows, rows):
            last = first + rows
            scores = dot(key[:last, at], query[first:last, at], NT) * scale
            scores = scores + bias[:last, first:last].astype(f32)
            top = jnp.max(scores, axis=0, keepdims=True)
            probs = jnp.exp(scores - top)
            mass = jnp.sum(probs, axis=0, keepdims=True)
            probs_low = (probs * (1.0 / mass)).astype(bf16)
            turned = dot(value[:last, at], probs_low, TN)
            context[first:last, at] = turned.T.astype(bf16)
            lse[lines(h, 8), first:last] = jnp.broadcast_to(top + jnp.log(mass), (8, rows))
        return carry

    lax.fori_loop(0, heads, head_step, 0)
    done.append(pass_on(1, gate_out, 0))
    save(query, query_out)
    save(key, key_out)
    save(context, context_out)
    save(lse, lse_out)

    keep.wait()
    row_landed(lambda source, hop: output_in.at[source], 6)
    for i in range(2):
        for source in range(4):
            for j in range(4):
                output_mat[i * size + source * own : i * size + (source + 1) * own, j * part : (j + 1) * part] = (
                    output_in[source, i * size + j * own : i * size + (j + 1) * own, :]
                )
    save(output_mat, output_out)

    def output_part(hop, store):
        some = context[lines(other(row, hop), rows), :]
        for j in range(4):
            columns = slice(j * part, (j + 1) * part)
            store(columns, dot(some, output_mat[:, columns], NN))

    half = rows // 2
    top, bottom = pl.ds(0, half), pl.ds(half, half)
    for hop in hops:

        def store(columns, values):
            rows_send[hop - 1, :, columns] = values.astype(bf16)

        output_part(hop, store)
        if hop == 3:
            row_copy(rows_send.at[2, top], half_in.at[0], 8, 1)
            row_copy(rows_send.at[2, bottom], half_in.at[1], 8, 2)
        else:
            early = (top, bottom)[hop - 1]
            row_copy(rows_send.at[hop - 1, early], rows_in.at[hop - 1, early], 10, hop)
    for hop in (1, 2):
        late = (bottom, top)[hop - 1]
        landed(half_in.at[2 - hop], row_recv_sem.at[8, 2 - hop])
        rows_send[hop - 1, late] = (rows_send[hop - 1, late].astype(f32) + half_in[2 - hop].astype(f32)).astype(bf16)
        row_copy(rows_send.at[hop - 1, late], rows_in.at[hop - 1, late], 11, hop)

    def own_store(columns, values):
        attn[:, columns] = values

    output_part(0, own_store)

    pass_on(1, gate_out, 1)
    done.append(pass_on(2, up_out, 0))
    for hop in (1, 2):
        early, late = ((top, bottom), (bottom, top))[hop - 1]
        landed(rows_in.at[hop - 1, early], row_recv_sem.at[10, hop - 1])
        landed(rows_in.at[hop - 1, late], row_recv_sem.at[11, hop - 1])
        attn[...] += rows_in[hop - 1].astype(f32)
    mean = jnp.sum(attn[...] * attn[...], axis=1, keepdims=True) / width
    factor = lax.rsqrt(mean + epsilon)
    unit_scale[...] = jnp.broadcast_to(factor, unit_scale.shape)
    attn[...] = attn[...] * factor
    hidden[...] = tokens[lines(row, rows), :].astype(f32) + attn[...] * gains[2:3, :]
    hidden_all[lines(row, rows), :] = hidden[...].astype(bf16)
    for hop in (1, 2):
        place = hidden_all.at[lines(row, rows)]
        row_copy(place, place, 9, hop)
    save(attn, unit_out)
    save(unit_scale, unit_scale_out)
    save(hidden, hidden_out)
    load_down.wait()
    row_landed(lambda source, hop: down_block.at[lines(source, own)], 5)
    save(down_block, down_out)

    for hop in (1, 2):
        landed(hidden_all.at[lines(other(row, hop), rows)], row_recv_sem.at[9, hop - 1])
        place = hidden_all.at[lines(2 * other(row, hop) + hop - 1, half)]
        row_copy(place, place, 12, 3 - hop)
    for hop in (1, 2):
        landed(hidden_all.at[lines(2 * other(row, 3) + 2 - hop, half)], row_recv_sem.at[12, hop - 1])
    save(hidden_all, hidden_all_out)
    pass_on(1, gate_out, 2)
    pass_on(2, up_out, 1)
    pass_on(2, up_out, 2)
    gathered(1, gate_out)
    gathered(2, up_out)

    for finish_sends in done:
        finish_sends()
    for copy in sent:
        copy.wait_send()
    for copy in saved[1:]:
        copy.wait()


def front(tokens, pack, output_block, gate, up, down, gain_tile, cos_wide, sin_wide, bias):
    rows, width = tokens.shape
    total, part, own = 4 * rows, width // 4, pack.shape[1]
    wide, units, size = 3 * part, gate.shape[1] // 4, 4 * own
    heads = part // HEAD_DIM
    shape = jax.ShapeDtypeStruct
    outs = [
        shape((width, width), bf16),
        shape((width, units), bf16),
        shape((width, units), bf16),
        shape((size, units), bf16),
        shape((total, width), bf16),
        shape((total, part), f32),
        shape((total, part), f32),
        shape((total, part), bf16),
        shape((8, total), f32),
        shape((total, part), bf16),
        shape((total, part), bf16),
        shape((total, part), bf16),
        shape((8 * heads, total), f32),
        shape((part, width), bf16),
        shape((rows, width), f32),
        shape((rows, HEAD_DIM), f32),
        shape((rows, width), f32),
        shape((total, width), bf16),
        shape((8, width), f32),
    ]
    vmem, dma = pltpu.VMEM, pltpu.SemaphoreType.DMA
    return pl.pallas_call(
        front_kernel,
        in_specs=[pl.BlockSpec(memory_space=pl.ANY)] * 10,
        out_specs=[pl.BlockSpec(memory_space=pl.ANY)] * len(outs),
        out_shape=outs,
        scratch_shapes=[
            vmem((size, width), bf16),
            vmem((width, width), bf16),
            vmem((size, units), bf16),
            vmem((size, units), bf16),
            vmem((size, units), bf16),
            vmem((total, width), bf16),
            vmem((total, part), f32),
            vmem((total, part), f32),
            vmem((total, part), bf16),
            vmem((total, part), bf16),
            vmem((total, part), bf16),
            vmem((total, part), bf16),
            vmem((8 * heads, total), f32),
            vmem((total, total), bf16),
            vmem((total, HEAD_DIM), f32),
            vmem((total, HEAD_DIM), f32),
            vmem((2, total, HEAD_DIM), f32),
            vmem((4, part, part), bf16),
            vmem((part, width), bf16),
            vmem((3, rows, width), bf16),
            vmem((2, rows, width), bf16),
            vmem((2, rows // 2, width), bf16),
            vmem((rows, width), f32),
            vmem((rows, HEAD_DIM), f32),
            vmem((rows, width), f32),
            vmem((total, width), bf16),
            vmem((8, total), f32),
            vmem((3, 8, total), f32),
            vmem((8, total), f32),
            vmem((4, 8, HEAD_DIM), f32),
            vmem((8, 4, 8, HEAD_DIM), f32),
            vmem((8, width), f32),
            dma((11,)),
            dma((24,)),
            dma((13, 3)),
            dma((13, 3)),
            dma((7,)),
            dma((7,)),
            dma((3, 4)),
            dma((3, 4)),
            dma((3, 4)),
            dma((3, 4)),
        ],
        compiler_params=pltpu.CompilerParams(
            collective_id=2, has_side_effects=True, vmem_limit_bytes=62 * 2**20
        ),
        cost_estimate=pl.CostEstimate(
            flops=10 * total * width * part, bytes_accessed=100 * 2**20, transcendentals=0
        ),
    )(tokens, pack, output_block, gate, up, down, gain_tile, cos_wide, sin_wide, bias)


def body(
    inputs,
    cotangent,
    seg_lengths,
    seg_parents,
    w_query,
    w_key,
    w_value,
    w_output,
    gain_query,
    gain_key,
    gain_attn,
    w_gate,
    w_up,
    w_down,
    gain_mlp,
):
    trees, rows_dev, width = inputs.shape
    count, leaves, me = lax.axis_size("row"), lax.axis_size("leaf"), lax.axis_index("row")
    tree_len = rows_dev * count
    part = width // count
    own = w_query.shape[0]
    group = count * own // 2
    units = w_gate.shape[1] // count
    tokens = inputs.reshape(rows_dev, width)

    def leaf_gather(block):
        return lax.all_gather(block, "leaf", axis=0, tiled=True)

    def leaf_scatter(block):
        return lax.psum_scatter(block, "leaf", scatter_dimension=0, tiled=True)

    bias, cos_wide, sin_wide = tree_tables(seg_lengths[0], seg_parents[0], tree_len)
    fast = leaves == 8 and count == 4
    if fast:
        def split_columns(weight):
            return jnp.swapaxes(weight.astype(bf16).reshape(own, count, -1), 0, 1)

        gain_own = jnp.stack([gain_query, gain_key, gain_attn, gain_mlp]).astype(bf16).astype(f32)
        gain_tile = lax.dynamic_update_slice(jnp.zeros((8, HEAD_DIM), f32), gain_own, (0, (me % 2) * own))
        (
            attn_mat,
            gate_mat,
            up_mat,
            down_block,
            all_tokens,
            query_pre,
            key_pre,
            value,
            scales,
            query,
            key,
            context,
            lse,
            output_mat,
            attn_unit,
            attn_scale,
            hidden,
            hidden_all,
            gains_all,
        ) = front(
            tokens,
            jnp.concatenate([split_columns(w) for w in (w_query, w_key, w_value)], axis=2),
            split_columns(w_output).reshape(count * own, part),
            w_gate.astype(bf16),
            w_up.astype(bf16),
            w_down.astype(bf16),
            gain_tile,
            cos_wide,
            sin_wide,
            bias,
        )
        scales, attn_scale = scales[:2], attn_scale[:, :1]
        down_halves = [leaf_gather(down_block[h * group : (h + 1) * group]) for h in range(2)]
        query_scale, key_scale = scales[0][:, None], scales[1][:, None]
        attn_gain, mlp_gain = gains_all[2], gains_all[3]
        head_gains = lax.dynamic_slice_in_dim(gains_all[:2], me * part, part, 1)
    else:
        qkv_block = columns_in(w_query, w_key, w_value)
        gains_own = jnp.stack([gain_query, gain_key, gain_attn, gain_mlp]).astype(bf16).reshape(1, 4 * own)
        gains_leaf = gather_rows(gains_own).reshape(count * own, 4)
        attn_block = jnp.concatenate(
            [
                qkv_block,
                w_output.astype(bf16).reshape(count * own, part),
                jnp.pad(gains_leaf, ((0, 0), (0, HEAD_DIM - 4))),
            ],
            axis=1,
        )
        attn_mat = leaf_gather(attn_block)
        qkv_mat = attn_mat[:, : 3 * part]
        output_rows = attn_mat[:, 3 * part : 4 * part].reshape(count, leaves // count, own, width)
        gains_all = attn_mat[:, 4 * part : 4 * part + 4].reshape(leaves, count, 4, own)
        gains_all = jnp.moveaxis(gains_all, 2, 0).reshape(4, width).astype(f32)
        gate_block = columns_in(tie(w_gate, qkv_block))
        up_block = columns_in(tie(w_up, qkv_block))
        down_block = columns_in(tie(w_down, qkv_block))
        all_tokens = gather_rows(tie(tokens, gate_block, up_block, down_block))

        query_pre, key_pre, value, squares = project(all_tokens, attn_mat, part)
        gate_mat = leaf_gather(gate_block)
        up_mat = leaf_gather(up_block)
        down_halves = [leaf_gather(down_block[h * group : (h + 1) * group]) for h in range(2)]

        squares = sum_rows(squares)
        scales = lax.rsqrt(squares / width + epsilon)
        query_scale, key_scale = scales[0][:, None], scales[1][:, None]
        attn_gain, mlp_gain = gains_all[2], gains_all[3]
        head_gains = lax.dynamic_slice_in_dim(gains_all[:2], me * part, part, 1)
        output_rows = tie(output_rows, scales)
        output_mat = jnp.zeros((leaves // count, count, own, width), bf16)
        for hop in range(count):
            piece = lax.dynamic_index_in_dim(output_rows, me ^ hop, 0, keepdims=False)
            if hop:
                piece = swap(piece, hop)
            output_mat = lax.dynamic_update_index_in_dim(output_mat, piece, me ^ hop, 1)
        output_mat = output_mat.reshape(part, width)
        query, key, context, lse = attend(
            query_pre, key_pre, value, scales.T, head_gains, cos_wide, sin_wide, bias
        )
        attn_pre = dot_scatter([context], [output_mat], NN)
        attn_scale = lax.rsqrt(jnp.mean(attn_pre * attn_pre, axis=-1, keepdims=True) + epsilon)
        attn_unit = attn_pre * attn_scale
        hidden = tokens.astype(f32) + attn_unit * attn_gain
        hidden_all = gather_rows(hidden.astype(bf16))

    gate_pre = dot(hidden_all, gate_mat, NN)
    up_pre = dot(hidden_all, up_mat, NN)
    sigmoid_gate = jax.nn.sigmoid(gate_pre)
    activated = (gate_pre * sigmoid_gate * up_pre).astype(bf16)
    mlp_halves = [dot_scatter([activated], [down_halves[h]], NT) for h in range(2)]
    grad_final = cotangent.reshape(rows_dev, width).astype(f32)
    halves = range(2)

    def split(rows):
        rows = rows.reshape(rows.shape[:-1] + (leaves, 2, group))
        return [rows[..., h, :].reshape(rows.shape[:-3] + (width // 2,)) for h in halves]

    weighted = tie(split(grad_final * mlp_gain), hidden_all)
    square = sum(jnp.sum(m * m, axis=-1, keepdims=True) for m in mlp_halves) / width
    cross = sum(jnp.sum(m * w, axis=-1, keepdims=True) for m, w in zip(mlp_halves, weighted)) / width
    mlp_scale = lax.rsqrt(square + epsilon)
    grad_mlp = [
        (mlp_scale * (w - m * (mlp_scale * mlp_scale * cross))).astype(bf16) for m, w in zip(mlp_halves, weighted)
    ]
    grad_mlp_halves = [gather_rows(grad_mlp[h]) for h in halves]
    down_sums = [dot(grad_mlp_halves[h], activated, TN, bf16) for h in range(2)]
    down_shards = [leaf_scatter(down_sums[h]) for h in range(2)]
    grad_act = dot(tie(grad_mlp_halves[0], down_sums[0]), down_halves[0], NN)
    grad_act = grad_act + dot(tie(grad_mlp_halves[1], down_sums[1]), down_halves[1], NN)
    grad_gate = (grad_act * up_pre * sigmoid_gate * (1.0 + gate_pre * (1.0 - sigmoid_gate))).astype(bf16)
    grad_up = (grad_act * gate_pre * sigmoid_gate).astype(bf16)
    wide = width // 2
    parts, coming = [], []
    for h in range(2):
        one = tie(grad_gate, *parts), tie(grad_up, *parts)
        part_h = sum(
            dot(left, right[h * wide : (h + 1) * wide], NT) for left, right in zip(one, (gate_mat, up_mat))
        ).astype(bf16)
        parts.append(part_h)
        coming.append(send_rows(part_h))
    gate_sum = dot(hidden_all, tie(grad_gate, *parts), TN, bf16)
    grad_hidden = grad_final + jnp.concatenate(
        [add_rows(part_h, pieces, gate_sum) for part_h, pieces in zip(parts, coming)], axis=1
    )
    gate_sum = tie(gate_sum, *down_sums)
    gate_shard = leaf_scatter(gate_sum)

    grad_attn, grad_attn_gain = norm_back(grad_hidden, attn_unit, attn_scale, attn_gain)
    grad_attn_low = grad_attn.astype(bf16)
    up_sum = dot(hidden_all, tie(grad_up, grad_attn_low), TN, bf16)
    grad_attn_all = gather_rows(tie(grad_attn_low, *down_shards), up_sum)
    grad_context = dot(grad_attn_all, output_mat, NT, bf16)
    up_shard = leaf_scatter(tie(up_sum, gate_sum))
    grad_context = tie(grad_context, gate_shard)
    grad_query, grad_key, grad_value, inner_query, inner_key, grad_head_gains = attend_back(
        query, key, value, bias, lse, grad_context, query_pre, key_pre, scales.T, head_gains, cos_wide, sin_wide
    )
    inner = sum_rows(jnp.stack([jnp.sum(inner_query, axis=1), jnp.sum(inner_key, axis=1)])) / width
    output_part = dot(context, tie(grad_attn_all, inner), TN, bf16).reshape(leaves // count, count, own, width)
    grad_query_low = (
        query_scale * (grad_query * head_gains[0] - query_pre * (query_scale * inner[0][:, None]))
    ).astype(bf16)
    grad_key_low = (
        key_scale * (grad_key * head_gains[1] - key_pre * (key_scale * inner[1][:, None]))
    ).astype(bf16)
    grad_qkv = jnp.concatenate([grad_query_low, grad_key_low, grad_value], axis=1)
    gate_out = columns_out(tie(gate_shard, inner_query))
    down_out = columns_out(tie(jnp.concatenate(down_shards), inner_query))
    mlp_halves = tie(mlp_halves, inner_query)
    mlp_unit = jnp.stack([m.reshape(rows_dev, leaves, group) for m in mlp_halves], axis=2).reshape(rows_dev, width)
    mlp_unit = mlp_unit * mlp_scale
    outputs = (hidden + mlp_unit * mlp_gain).astype(bf16).reshape(inputs.shape)
    grad_mlp_gain = jnp.sum(grad_final * mlp_unit, axis=0)

    wide_part = jnp.stack([tie(grad_attn_gain, inner), grad_mlp_gain]).reshape(2, leaves, count, own)
    narrow_part = grad_head_gains.reshape(2, leaves // count, count, own)
    grad_qkv = tie(grad_qkv, gate_out, down_out, outputs)
    if fast:
        gain_part = jnp.zeros((count, leaves, 8, HEAD_DIM), f32)
        gain_part = lax.dynamic_update_slice(
            gain_part, jnp.transpose(narrow_part, (2, 1, 0, 3)), (0, me * (leaves // count), 0, 0)
        )
        gain_part = lax.dynamic_update_slice(gain_part, jnp.transpose(wide_part, (2, 1, 0, 3)), (0, 0, 2, 0))
        *grad_mats, grad_output, grad_tokens, up_out, grad_gains = finish(
            all_tokens, grad_qkv, attn_mat, output_part, grad_hidden, up_shard, gain_part
        )
        grad_inputs, up_out, grad_gains = grad_tokens.reshape(inputs.shape), [up_out], grad_gains[:4, :own]
    else:
        wide_sum = jnp.zeros((2, leaves, own), f32)
        narrow_all = jnp.zeros((2, leaves, own), f32)
        for hop in range(count):
            piece = lax.dynamic_index_in_dim(jnp.concatenate([wide_part, narrow_part], axis=1), me ^ hop, 2, keepdims=False)
            if hop:
                piece = swap(piece, hop)
            wide_sum = wide_sum + piece[:, :leaves]
            narrow_all = lax.dynamic_update_slice_in_dim(
                narrow_all, piece[:, leaves:], (me ^ hop) * (leaves // count), 1
            )
        grad_gains = jnp.concatenate([narrow_all, wide_sum], axis=0)
        stride = 1
        while stride < leaves:
            grad_gains = grad_gains + lax.ppermute(
                grad_gains, "leaf", [(i, i ^ stride) for i in range(leaves)]
            )
            stride *= 2
        grad_gains = lax.dynamic_index_in_dim(grad_gains, lax.axis_index("leaf"), 1, keepdims=False)
        output_turned = jnp.zeros((count, leaves // count, own, width), bf16)
        for hop in range(count):
            piece = lax.dynamic_index_in_dim(output_part, me ^ hop, 1, keepdims=False)
            if hop:
                piece = swap(piece, hop)
            output_turned = lax.dynamic_update_index_in_dim(output_turned, piece, me ^ hop, 0)
        attn_sum = sums_beside(all_tokens, grad_qkv, output_turned.reshape(leaves * count * own, part))
        grad_tokens = grad_hidden + dot_scatter([grad_qkv], [qkv_mat], NT)
        grad_inputs = grad_tokens.astype(bf16).reshape(inputs.shape)
        attn_shard = leaf_scatter(tie(attn_sum, up_shard))
        up_out = columns_out(up_shard)
        grad_mats = columns_out(attn_shard[:, : 3 * part], 3)
        grad_output = attn_shard[:, 3 * part :].reshape(own, width).astype(f32)
    return (
        outputs,
        grad_inputs,
        *grad_mats,
        grad_output,
        grad_gains[0],
        grad_gains[1],
        grad_gains[2],
        *gate_out,
        *up_out,
        *down_out,
        grad_gains[3],
    )


def solution(mesh):
    both = ("leaf", "row")
    token_spec, tree_spec, matrix_spec, gain_spec = P("leaf", "row", None), P("leaf", None), P(both, None), P(both)
    return jax.shard_map(
        body,
        mesh=mesh,
        in_specs=(token_spec,) * 2 + (tree_spec,) * 2 + (matrix_spec,) * 4 + (gain_spec,) * 3 + (matrix_spec,) * 3 + (gain_spec,),
        out_specs=(token_spec,) * 2 + (matrix_spec,) * 4 + (gain_spec,) * 3 + (matrix_spec,) * 3 + (gain_spec,),
        check_vma=False,
    )
```

```python
import functools
import math

import jax
import jax.numpy as jnp
from jax import lax
from jax.experimental import pallas as pl
from jax.experimental.pallas import tpu as pltpu
from jax.sharding import PartitionSpec as P

HEAD_DIM = 128
MESH = pl.DeviceIdType.MESH

epsilon = 1e-06
rope_theta = 500000.0
masked_fill = -1e30
bf16 = jnp.bfloat16
f32 = jnp.float32
NN = (((1,), (0,)), ((), ()))
NT = (((1,), (1,)), ((), ()))
TN = (((0,), (0,)), ((), ()))


def dot(left, right, dims, kind=f32):
    return lax.dot_general(left, right, dims, preferred_element_type=f32).astype(kind)


def swap(piece, hop):
    count = lax.axis_size("row")
    return lax.ppermute(piece, "row", [(i, i ^ hop) for i in range(count)])


def gather_rows(rows, *meanwhile):
    count, me = lax.axis_size("row"), lax.axis_index("row")
    size = rows.shape[0]
    whole = jnp.zeros((count * size,) + rows.shape[1:], rows.dtype)
    for hop in range(1, count):
        whole = lax.dynamic_update_slice_in_dim(whole, swap(rows, hop), (me ^ hop) * size, 0)
    return lax.dynamic_update_slice_in_dim(whole, tie(rows, *meanwhile), me * size, 0)


def dot_scatter(lefts, rights, dims, *meanwhile):
    count, me = lax.axis_size("row"), lax.axis_index("row")
    size = lefts[0].shape[0] // count

    def rows_of(hop, lefts):
        parts = [lax.dynamic_slice_in_dim(left, (me ^ hop) * size, size, 0) for left in lefts]
        return sum(dot(part, right, dims) for part, right in zip(parts, rights))

    coming = [swap(rows_of(hop, lefts).astype(bf16), hop) for hop in reversed(range(1, count))]
    total = rows_of(0, [tie(left, *meanwhile) for left in lefts])
    for piece in coming:
        total = total + piece.astype(f32)
    return total


def send_rows(partial):
    count, me = lax.axis_size("row"), lax.axis_index("row")
    size = partial.shape[0] // count
    return [
        swap(lax.dynamic_slice_in_dim(partial, (me ^ hop) * size, size, 0), hop) for hop in reversed(range(1, count))
    ]


def add_rows(partial, coming, *meanwhile):
    size = partial.shape[0] // lax.axis_size("row")
    mine = lax.dynamic_slice_in_dim(tie(partial, *meanwhile), lax.axis_index("row") * size, size, 0)
    return sum([piece.astype(f32) for piece in coming], mine.astype(f32))


def tie(value, *others):
    return lax.optimization_barrier((value,) + others)[0]


def columns_in(*weights):
    count, me = lax.axis_size("row"), lax.axis_index("row")
    size, wide = weights[0].shape[0], weights[0].shape[1] // count
    whole = jnp.zeros((count * size, wide * len(weights)), bf16)
    for hop in range(count):
        piece = jnp.concatenate(
            [lax.dynamic_slice_in_dim(w, (me ^ hop) * wide, wide, 1).astype(bf16) for w in weights], axis=1
        )
        if hop:
            piece = swap(piece, hop)
        whole = lax.dynamic_update_slice_in_dim(whole, piece, (me ^ hop) * size, 0)
    return whole


def columns_out(block, many=1):
    count, me = lax.axis_size("row"), lax.axis_index("row")
    size, wide = block.shape[0] // count, block.shape[1] // many
    whole = [jnp.zeros((size, wide * count), f32)] * many
    for hop in range(count):
        piece = lax.dynamic_slice_in_dim(block, (me ^ hop) * size, size, 0)
        if hop:
            piece = swap(piece, hop)
        for i in range(many):
            own = piece[:, i * wide : (i + 1) * wide].astype(f32)
            whole[i] = lax.dynamic_update_slice_in_dim(whole[i], own, (me ^ hop) * wide, 1)
    return whole


def sum_rows(small):
    count = lax.axis_size("row")
    total = small
    for hop in range(1, count):
        total = total + swap(small, hop)
    return total


def norm_back(grad_out, unit_rows, scaled, gain_row):
    weighted = grad_out * gain_row
    inner = jnp.mean(weighted * unit_rows, axis=-1, keepdims=True)
    return (scaled * (weighted - unit_rows * inner), jnp.sum(grad_out * unit_rows, axis=0))


def tree_tables(length_row, parent_row, total):
    seg_count = parent_row.shape[0]
    segment_ids = jnp.arange(seg_count, dtype=jnp.int32)
    ends = jnp.cumsum(length_row)
    offsets = ends - length_row
    all_rows = jnp.arange(total, dtype=jnp.int32)
    owned_from = (all_rows[:, None] >= offsets[None, :]).astype(f32)
    onehot_all = owned_from - jnp.concatenate(
        [owned_from[:, 1:], jnp.zeros((total, 1), f32)], axis=1
    )
    parents = jnp.sum(onehot_all * parent_row.astype(f32)[None, :], axis=1)
    segments = jnp.sum(onehot_all * segment_ids.astype(f32)[None, :], axis=1)
    lengths = length_row.astype(f32)
    parent_lengths = jnp.sum((parent_row[:, None] == segment_ids[None, :]) * lengths[None, :], axis=1)
    above = jnp.where(segment_ids > 0, lengths[0], 0.0) + jnp.where(parent_row > 0, parent_lengths, 0.0)
    position = all_rows.astype(f32) + jnp.sum(onehot_all * (above - offsets.astype(f32))[None, :], axis=1)
    on_path = (segments[:, None] == segments[None, :]) | (segments[:, None] == parents[None, :]) | (segments[:, None] == 0.0)
    allowed = on_path & (all_rows[:, None] <= all_rows[None, :])
    bias = jnp.where(allowed, 0.0, masked_fill).astype(bf16)
    frequency = jnp.exp(
        jnp.arange(HEAD_DIM // 2, dtype=f32) * (-2.0 * math.log(rope_theta) / HEAD_DIM)
    )
    angles = position[:, None] * frequency[None, :]
    cos_half, sin_half = jnp.cos(angles), jnp.sin(angles)
    cos_wide = jnp.concatenate([cos_half, cos_half], axis=1)
    sin_wide = jnp.concatenate([-sin_half, sin_half], axis=1)
    return (bias, cos_wide, sin_wide)


def turn(vector, cos_part, sin_part):
    return vector * cos_part + pltpu.roll(vector, HEAD_DIM // 2, 1) * sin_part


def project_kernel(tokens_ref, weights_ref, query_ref, key_ref, value_ref, squares_ref):
    part = query_ref.shape[1]
    tokens = tokens_ref[...]
    for i, out_ref in enumerate((query_ref, key_ref)):
        product = dot(tokens, weights_ref[:, i * part : (i + 1) * part], NN)
        out_ref[...] = product
        square = jnp.sum(product * product, axis=1, keepdims=True)
        squares_ref[i : i + 1, :] = jnp.broadcast_to(square, (square.shape[0], HEAD_DIM)).T[0:1]
    value_ref[...] = dot(tokens, weights_ref[:, 2 * part :], NN, bf16)


def project(tokens, weights, part):
    total, width = tokens.shape
    size = 256
    rows = pl.BlockSpec((size, part), lambda i: (i, 0))
    wide = jax.ShapeDtypeStruct((total, part), f32)
    return pl.pallas_call(
        project_kernel,
        grid=(total // size,),
        in_specs=[
            pl.BlockSpec((size, width), lambda i: (i, 0)),
            pl.BlockSpec((width, 3 * part), lambda i: (0, 0)),
        ],
        out_specs=[rows, rows, rows, pl.BlockSpec((2, size), lambda i: (0, i))],
        out_shape=[
            wide,
            wide,
            jax.ShapeDtypeStruct((total, part), bf16),
            jax.ShapeDtypeStruct((2, total), f32),
        ],
        compiler_params=pltpu.CompilerParams(vmem_limit_bytes=48 * 2**20),
        cost_estimate=pl.CostEstimate(
            flops=6 * total * width * part, bytes_accessed=2 * width * (total + 3 * part) + 10 * total * part, transcendentals=0
        ),
    )(tokens, weights)


def attend_kernel(
    block,
    scale,
    query_pre_ref,
    key_pre_ref,
    value_ref,
    scales_ref,
    gains_ref,
    cos_ref,
    sin_ref,
    bias_ref,
    query_ref,
    key_ref,
    context_ref,
    lse_ref,
):
    total = key_ref.shape[0]
    cos_part, sin_part = cos_ref[...], sin_ref[...]
    query_ref[...] = turn(query_pre_ref[...] * scales_ref[:, 0:1] * gains_ref[0:1], cos_part, sin_part).astype(bf16)
    key_ref[...] = turn(key_pre_ref[...] * scales_ref[:, 1:2] * gains_ref[1:2], cos_part, sin_part).astype(bf16)
    for first in range(0, total, block):
        last = first + block
        scores = dot(key_ref[:last], query_ref[first:last], NT) * scale
        scores = scores + bias_ref[:last, first:last].astype(f32)
        top = jnp.max(scores, axis=0, keepdims=True)
        probs = jnp.exp(scores - top)
        mass = jnp.sum(probs, axis=0, keepdims=True)
        probs_low = (probs * (1.0 / mass)).astype(bf16)
        turned = dot(value_ref[:last], probs_low, TN)
        context_ref[first:last, :] = turned.T.astype(bf16)
        lse_ref[:, first:last] = jnp.broadcast_to(top + jnp.log(mass), (8, block))


def head_specs(total):
    part = pl.BlockSpec((total, HEAD_DIM), lambda h: (0, h))
    whole = pl.BlockSpec((total, HEAD_DIM), lambda h: (0, 0))
    gains = pl.BlockSpec((2, HEAD_DIM), lambda h: (0, h))
    scales = pl.BlockSpec((total, 2), lambda h: (0, 0))
    bias = pl.BlockSpec((total, total), lambda h: (0, 0))
    lse = pl.BlockSpec((8, total), lambda h: (h, 0))
    return part, whole, gains, scales, bias, lse


def attend(query_pre, key_pre, value, scales, gains, cos_wide, sin_wide, bias):
    total, width = query_pre.shape
    heads = width // HEAD_DIM
    part, whole, gain, scale, square, lse = head_specs(total)
    low = jax.ShapeDtypeStruct((total, width), bf16)
    return pl.pallas_call(
        functools.partial(attend_kernel, 256, 1.0 / math.sqrt(HEAD_DIM)),
        grid=(heads,),
        in_specs=[part, part, part, scale, gain, whole, whole, square],
        out_specs=[part, part, part, lse],
        out_shape=[low, low, low, jax.ShapeDtypeStruct((8 * heads, total), f32)],
        compiler_params=pltpu.CompilerParams(vmem_limit_bytes=56 * 2**20),
        cost_estimate=pl.CostEstimate(
            flops=4 * total * total * width, bytes_accessed=16 * total * width, transcendentals=total * total * heads
        ),
    )(query_pre, key_pre, value, scales, gains, cos_wide, sin_wide, bias)


def attend_back_kernel(
    block,
    scale,
    query_ref,
    key_ref,
    value_ref,
    bias_ref,
    lse_ref,
    grad_ref,
    query_pre_ref,
    key_pre_ref,
    scales_ref,
    gains_ref,
    cos_ref,
    sin_ref,
    grad_query_ref,
    grad_key_ref,
    grad_value_ref,
    inner_query_ref,
    inner_key_ref,
    grad_gains_ref,
    key_sum,
    value_sum,
):
    total = key_ref.shape[0]

    @pl.when(pl.program_id(0) == 0)
    def _():
        inner_query_ref[...] = jnp.zeros_like(inner_query_ref)
        inner_key_ref[...] = jnp.zeros_like(inner_key_ref)

    key_sum[...] = jnp.zeros_like(key_sum)
    value_sum[...] = jnp.zeros_like(value_sum)
    for first in range(0, total, block):
        last = first + block
        scores = dot(key_ref[:last], query_ref[first:last], NT) * scale
        scores = scores + bias_ref[:last, first:last].astype(f32)
        probs = jnp.exp(scores - lse_ref[0:1, first:last])
        grad_probs = dot(value_ref[:last], grad_ref[first:last], NT)
        inner = jnp.sum(probs * grad_probs, axis=0, keepdims=True)
        grad_scores = (probs * (grad_probs - inner)).astype(bf16)
        turned = dot(key_ref[:last], grad_scores, TN)
        grad_query_ref[first:last, :] = turned.T
        key_sum[:last, :] += dot(grad_scores, query_ref[first:last], NN)
        value_sum[:last, :] += dot(probs.astype(bf16), grad_ref[first:last], NN)
    grad_value_ref[...] = value_sum[...].astype(bf16)
    cos_part, sin_part = cos_ref[...], -sin_ref[...]
    for row, (grad, out_ref, pre_ref, inner_ref) in enumerate(
        (
            (grad_query_ref[...], grad_query_ref, query_pre_ref, inner_query_ref),
            (key_sum[...], grad_key_ref, key_pre_ref, inner_key_ref),
        )
    ):
        grad = turn(grad * scale, cos_part, sin_part)
        by_unit = grad * (pre_ref[...] * scales_ref[:, row : row + 1])
        inner_ref[...] += by_unit * gains_ref[row : row + 1]
        grad_gains_ref[row : row + 1, :] = jnp.sum(by_unit, axis=0, keepdims=True)
        out_ref[...] = grad


def attend_back(query, key, value, bias, lse, grad_context, query_pre, key_pre, scales, gains, cos_wide, sin_wide):
    total, width = query.shape
    heads = width // HEAD_DIM
    part, whole, gain, scale, square, lse_spec = head_specs(total)
    wide = jax.ShapeDtypeStruct((total, width), f32)
    narrow = jax.ShapeDtypeStruct((total, HEAD_DIM), f32)
    return pl.pallas_call(
        functools.partial(attend_back_kernel, 256, 1.0 / math.sqrt(HEAD_DIM)),
        grid=(heads,),
        in_specs=[part, part, part, square, lse_spec, part, part, part, scale, gain, whole, whole],
        out_specs=[part, part, part, whole, whole, gain],
        out_shape=[
            wide,
            wide,
            jax.ShapeDtypeStruct((total, width), bf16),
            narrow,
            narrow,
            jax.ShapeDtypeStruct((2, width), f32),
        ],
        scratch_shapes=[pltpu.VMEM((total, HEAD_DIM), f32)] * 2,
        compiler_params=pltpu.CompilerParams(vmem_limit_bytes=58 * 2**20),
        cost_estimate=pl.CostEstimate(
            flops=10 * total * total * width, bytes_accessed=30 * total * width, transcendentals=total * total * heads
        ),
    )(query, key, value, bias, lse, grad_context, query_pre, key_pre, scales, gains, cos_wide, sin_wide)


def sums_kernel(tokens_ref, grads_ref, side_ref, out_ref):
    wide = grads_ref.shape[1]
    out_ref[:, :wide] = dot(tokens_ref[...], grads_ref[...], TN, bf16)
    out_ref[:, wide:] = side_ref[...]


def sums_beside(tokens, grads, side):
    total, rows = tokens.shape
    wide, extra = grads.shape[1], side.shape[1]
    size = 256
    return pl.pallas_call(
        sums_kernel,
        grid=(rows // size,),
        in_specs=[
            pl.BlockSpec((total, size), lambda i: (0, i)),
            pl.BlockSpec((total, wide), lambda i: (0, 0)),
            pl.BlockSpec((size, extra), lambda i: (i, 0)),
        ],
        out_specs=pl.BlockSpec((size, wide + extra), lambda i: (i, 0)),
        out_shape=jax.ShapeDtypeStruct((rows, wide + extra), bf16),
        compiler_params=pltpu.CompilerParams(vmem_limit_bytes=40 * 2**20),
        cost_estimate=pl.CostEstimate(
            flops=2 * total * rows * wide, bytes_accessed=2 * rows * (total + wide + 2 * extra), transcendentals=0
        ),
    )(tokens, grads, side)


def landed(ref, sem):
    pltpu.make_async_copy(ref, ref, sem).wait()


def line_order(z):
    far, inner = z // 2, ((z + 1) // 2) % 2
    blocks = []
    for end, middle in ((3, 0), (2, 2), (1, 3), (0, 1)):
        first = end + inner * (middle - end)
        blocks.append(first + far * (3 - 2 * first))
    near = 1 + far
    chips = [near + inner * (blocks[0] - near), blocks[1], blocks[2]]
    slots = [3 + inner * (-2 - far), 2 + inner * (far - 2), far + inner * (2 - far)]
    return far, inner, blocks, chips, slots


def other(index, hop):
    return (index, index + 1 - 2 * (index % 2), (index + 2) % 4, 3 - index)[hop]


def final_kernel(
    tokens_hbm,
    grads_hbm,
    weights_hbm,
    output_hbm,
    hidden_hbm,
    up_hbm,
    gains_hbm,
    query_out,
    key_out,
    value_out,
    output_out,
    inputs_out,
    up_out,
    gains_out,
    tokens,
    grads,
    weights,
    hidden,
    core_out,
    core_in,
    mine,
    line_in,
    side,
    side_in,
    side_mine,
    side_line_in,
    tokens_send,
    tokens_in,
    rows_send,
    rows_in,
    up_in,
    gains,
    gains_in,
    gains_line,
    load_sem,
    row_send_sem,
    row_recv_sem,
    core_send_sem,
    core_recv_sem,
    line_send_sem,
    line_recv_sem,
    leaf_send_sem,
    leaf_recv_sem,
):
    leaf, row = lax.axis_index("leaf"), lax.axis_index("row")
    z, core = leaf // 2, leaf % 2
    far, inner, blocks, chips, slots = line_order(z)
    wide, own = grads.shape[1], query_out.shape[0]
    part, size = wide // 3, mine.shape[1]
    rows = tokens_in.shape[1]
    hops = (3, 1, 2)

    loads = [
        pltpu.make_async_copy(tokens_hbm, tokens, load_sem.at[0]),
        pltpu.make_async_copy(grads_hbm, grads, load_sem.at[1]),
        pltpu.make_async_copy(weights_hbm.at[:, pl.ds(0, wide)], weights, load_sem.at[2]),
        pltpu.make_async_copy(hidden_hbm, hidden, load_sem.at[3]),
        pltpu.make_async_copy(output_hbm.at[:, row], side.at[pl.ds(2 * row, 2)], load_sem.at[4]),
        pltpu.make_async_copy(gains_hbm.at[row], gains, load_sem.at[6]),
    ]
    for load in loads:
        load.start()
    barrier = pltpu.get_barrier_semaphore()
    for hop in hops:
        pl.semaphore_signal(barrier, inc=1, device_id={"row": other(row, hop)}, device_id_type=MESH)
    for step in range(1, 8):
        pl.semaphore_signal(barrier, inc=1, device_id={"leaf": (leaf + step) % 8}, device_id_type=MESH)
    pl.semaphore_wait(barrier, 10)

    sent = []

    def row_copy(source, target, kind, hop):
        copy = pltpu.make_async_remote_copy(
            source,
            target,
            row_send_sem.at[kind, hop - 1],
            row_recv_sem.at[kind, hop - 1],
            device_id={"row": other(row, hop)},
            device_id_type=MESH,
        )
        copy.start()
        sent.append(copy)

    def core_copy(source, target, kind, i):
        copy = pltpu.make_async_remote_copy(
            source,
            target,
            core_send_sem.at[kind, i],
            core_recv_sem.at[kind, i],
            device_id={"leaf": 2 * z + 1 - core},
            device_id_type=MESH,
        )
        copy.start()
        sent.append(copy)

    def line_copy(source, target, kind, i):
        return pltpu.make_async_remote_copy(
            source,
            target.at[slots[i]],
            line_send_sem.at[kind, i],
            line_recv_sem.at[kind, slots[i]],
            device_id={"leaf": 2 * chips[i] + core},
            device_id_type=MESH,
        )

    for hop in hops:
        row_copy(gains_hbm.at[other(row, hop)], gains_in.at[hop - 1], 4, hop)
    for hop in hops:
        row_copy(output_hbm.at[:, other(row, hop)], side.at[pl.ds(2 * row, 2)], 0, hop)

    loads[0].wait()
    loads[1].wait()

    def product(block):
        return dot(tokens[:, pl.ds(pl.multiple_of(block * size, size), size)], grads[...], TN)

    for i in range(4):
        core_out[i] = product(2 * blocks[i] + 1 - core).astype(bf16)
        core_copy(core_out.at[i], core_in.at[i], 0, i)

    def pair(i):
        mine[i] = (product(2 * blocks[i] + core) + core_in[i].astype(f32)).astype(bf16)

    for i in range(4):
        landed(core_in.at[i], core_recv_sem.at[0, i])
        pair(i)
        if i < 2:
            copy = line_copy(mine.at[i], line_in, 0, i)
            copy.start()
            sent.append(copy)
        if i == 2:
            last = line_copy(mine.at[2], line_in, 0, 2)
            sent.append(last)

            @pl.when(inner == 0)
            def _():
                last.start()

    loads[5].wait()
    for hop in hops:
        landed(gains_in.at[hop - 1], row_recv_sem.at[4, hop - 1])
        gains[...] += gains_in[hop - 1]
    for step in range(1, 8):
        copy = pltpu.make_async_remote_copy(
            gains.at[(leaf + step) % 8],
            gains_line.at[step - 1],
            leaf_send_sem.at[step - 1],
            leaf_recv_sem.at[step - 1],
            device_id={"leaf": (leaf + step) % 8},
            device_id_type=MESH,
        )
        copy.start()
        sent.append(copy)

    loads[2].wait()

    def tokens_part(hop, store):
        lines = grads[pl.ds(pl.multiple_of((other(row, hop)) * rows, rows), rows), :]

        def step(j, carry):
            columns = pl.ds(pl.multiple_of(j * part, part), part)
            store(columns, dot(lines, weights[columns, :], NT))
            return carry

        lax.fori_loop(0, weights.shape[0] // part, step, 0)

    for hop in hops:

        def store(columns, values):
            tokens_send[hop - 1, :, columns] = values.astype(bf16)

        tokens_part(hop, store)
        row_copy(tokens_send.at[hop - 1], tokens_in.at[hop - 1], 1, hop)

    loads[4].wait()
    for hop in hops:
        landed(side.at[pl.ds(2 * (other(row, hop)), 2)], row_recv_sem.at[0, hop - 1])
    for i in range(4):
        core_copy(side.at[2 * blocks[i] + 1 - core], side_in.at[i], 1, i)

    for hop in hops:
        row_copy(up_hbm.at[pl.ds((other(row, hop)) * own, own)], up_in.at[row], 2, hop)
    keep = pltpu.make_async_copy(up_hbm.at[pl.ds(row * own, own)], up_in.at[row], load_sem.at[5])
    keep.start()

    @pl.when(inner == 1)
    def _():
        landed(line_in.at[3], line_recv_sem.at[0, 3])
        mine[2] = (mine[2].astype(f32) + line_in[3].astype(f32)).astype(bf16)
        last.start()

    for i in range(4):
        landed(side_in.at[i], core_recv_sem.at[1, i])
        side_mine[i] = (side[2 * blocks[i] + core].astype(f32) + side_in[i].astype(f32)).astype(bf16)

    loads[3].wait()

    def own_store(columns, values):
        hidden[:, columns] += values

    tokens_part(0, own_store)
    gains_out[...] = gains[leaf]
    for step in range(1, 8):
        landed(gains_line.at[step - 1], leaf_recv_sem.at[step - 1])
        gains_out[...] += gains_line[step - 1]

    def near(kind, came, kept):
        for slot in range(2):

            @pl.when(inner + (1 - far) * slot + far * (1 - slot) > 0)
            def _():
                landed(came.at[slot], line_recv_sem.at[kind, slot])
                kept[3] = (kept[3].astype(f32) + came[slot].astype(f32)).astype(bf16)

    def beyond(kind, came, kept):
        landed(came.at[2], line_recv_sem.at[kind, 2])
        kept[3] = (kept[3].astype(f32) + came[2].astype(f32)).astype(bf16)

    near(0, line_in, mine)
    for i in range(2):
        copy = line_copy(side_mine.at[i], side_line_in, 1, i)
        copy.start()
        sent.append(copy)
    side_last = line_copy(side_mine.at[2], side_line_in, 1, 2)
    sent.append(side_last)

    @pl.when(inner == 0)
    def _():
        side_last.start()

    beyond(0, line_in, mine)
    rows_send[...] = mine[3]
    for hop in hops:
        row_copy(rows_send.at[pl.ds(other(row, hop) * own, own)], rows_in.at[hop - 1], 3, hop)

    @pl.when(inner == 1)
    def _():
        landed(side_line_in.at[3], line_recv_sem.at[1, 3])
        side_mine[2] = (side_mine[2].astype(f32) + side_line_in[3].astype(f32)).astype(bf16)
        side_last.start()

    for hop in hops:
        landed(tokens_in.at[hop - 1], row_recv_sem.at[1, hop - 1])
        hidden[...] += tokens_in[hop - 1].astype(f32)
    inputs_out[...] = hidden[...].astype(bf16)

    keep.wait()
    for hop in hops:
        landed(up_in.at[other(row, hop)], row_recv_sem.at[2, hop - 1])
    for source in range(4):
        up_out[:, source * up_in.shape[2] : (source + 1) * up_in.shape[2]] = up_in[source].astype(f32)

    def give(source, values):
        columns = pl.ds(pl.multiple_of(source * part, part), part)
        for i, out in enumerate((query_out, key_out, value_out)):
            out[:, columns] = values[:, i * part : (i + 1) * part].astype(f32)

    give(row, rows_send[pl.ds(pl.multiple_of(row * own, own), own), :])
    near(1, side_line_in, side_mine)
    beyond(1, side_line_in, side_mine)
    output_out[...] = side_mine[3].astype(f32)
    for hop in hops:
        landed(rows_in.at[hop - 1], row_recv_sem.at[3, hop - 1])
        give(other(row, hop), rows_in[hop - 1])
    for copy in sent:
        copy.wait_send()


def finish(tokens, grads, weights, output_part, hidden, up_shard, gain_part):
    total, width = tokens.shape
    wide = grads.shape[1]
    own = output_part.shape[2]
    size, rows, units = 4 * own, hidden.shape[0], up_shard.shape[1]
    matrix = jax.ShapeDtypeStruct((own, width), f32)
    dma = pltpu.SemaphoreType.DMA
    return pl.pallas_call(
        final_kernel,
        in_specs=[pl.BlockSpec(memory_space=pl.ANY)] * 7,
        out_specs=[pl.BlockSpec(memory_space=pltpu.VMEM)] * 7,
        out_shape=[
            matrix,
            matrix,
            matrix,
            matrix,
            jax.ShapeDtypeStruct((rows, width), bf16),
            jax.ShapeDtypeStruct((own, 4 * units), f32),
            jax.ShapeDtypeStruct((8, HEAD_DIM), f32),
        ],
        scratch_shapes=[
            pltpu.VMEM((total, width), bf16),
            pltpu.VMEM((total, wide), bf16),
            pltpu.VMEM((width, wide), bf16),
            pltpu.VMEM((rows, width), f32),
            pltpu.VMEM((4, size, wide), bf16),
            pltpu.VMEM((4, size, wide), bf16),
            pltpu.VMEM((4, size, wide), bf16),
            pltpu.VMEM((4, size, wide), bf16),
            pltpu.VMEM((8, own, width), bf16),
            pltpu.VMEM((4, own, width), bf16),
            pltpu.VMEM((4, own, width), bf16),
            pltpu.VMEM((4, own, width), bf16),
            pltpu.VMEM((3, rows, width), bf16),
            pltpu.VMEM((3, rows, width), bf16),
            pltpu.VMEM((size, wide), bf16),
            pltpu.VMEM((3, own, wide), bf16),
            pltpu.VMEM((4, own, units), bf16),
            pltpu.VMEM((8, 8, HEAD_DIM), f32),
            pltpu.VMEM((3, 8, 8, HEAD_DIM), f32),
            pltpu.VMEM((7, 8, HEAD_DIM), f32),
            dma((7,)),
            dma((5, 3)),
            dma((5, 3)),
            dma((2, 4)),
            dma((2, 4)),
            dma((2, 3)),
            dma((2, 4)),
            dma((7,)),
            dma((7,)),
        ],
        compiler_params=pltpu.CompilerParams(
            collective_id=1, has_side_effects=True, vmem_limit_bytes=60 * 2**20
        ),
        cost_estimate=pl.CostEstimate(
            flops=4 * total * width * wide, bytes_accessed=100 * 2**20, transcendentals=0
        ),
    )(tokens, grads, weights, output_part, hidden, up_shard, gain_part)


def front_kernel(
    tokens_hbm,
    pack_hbm,
    output_hbm,
    gate_hbm,
    up_hbm,
    down_hbm,
    gains_hbm,
    cos_hbm,
    sin_hbm,
    bias_hbm,
    attn_out,
    gate_out,
    up_out,
    first_out,
    second_out,
    gate_pre_out,
    up_pre_out,
    activated_out,
    tokens_out,
    query_pre_out,
    key_pre_out,
    value_out,
    scales_out,
    query_out,
    key_out,
    context_out,
    lse_out,
    output_out,
    unit_out,
    unit_scale_out,
    hidden_out,
    hidden_all_out,
    gains_out,
    block,
    attn_mat,
    gate_block,
    up_block,
    down_block,
    tokens,
    query_pre,
    key_pre,
    value,
    query,
    key,
    context,
    lse,
    bias,
    cos_part,
    sin_part,
    scale_columns,
    output_in,
    output_mat,
    rows_send,
    rows_in,
    half_in,
    attn,
    unit_scale,
    hidden,
    hidden_all,
    squares,
    squares_in,
    scale_rows,
    gains_leaf,
    gains_all,
    gains,
    load_sem,
    save_sem,
    row_send_sem,
    row_recv_sem,
    leaf_send_sem,
    leaf_recv_sem,
    core_send_sem,
    core_recv_sem,
    line_send_sem,
    line_recv_sem,
):
    leaf, row = lax.axis_index("leaf"), lax.axis_index("row")
    z, core = leaf // 2, leaf % 2
    far, inner = z // 2, ((z + 1) // 2) % 2
    own = pack_hbm.shape[1]
    wide = pack_hbm.shape[2]
    part, size = wide // 3, 4 * own
    rows, width = tokens_hbm.shape
    units = gate_block.shape[1]
    heads = part // HEAD_DIM
    scale = 1.0 / math.sqrt(HEAD_DIM)
    hops = (3, 1, 2)
    sent, saved = [], []

    def lines(index, count):
        return pl.ds(pl.multiple_of(index * count, count), count)

    def load(source, target, i):
        copy = pltpu.make_async_copy(source, target, load_sem.at[i])
        copy.start()
        return copy

    def save(source, target):
        copy = pltpu.make_async_copy(source, target, save_sem.at[len(saved)])
        copy.start()
        saved.append(copy)

    mine = lines(row, own)
    load_pack = load(pack_hbm.at[row], block.at[mine, pl.ds(0, wide)], 0)
    load_output = load(output_hbm, block.at[:, pl.ds(wide, part)], 1)
    load_gains = load(gains_hbm, gains_leaf.at[row], 2)
    load_gate = load(gate_hbm.at[:, lines(row, units)], gate_block.at[mine], 3)
    load_tokens = load(tokens_hbm, tokens.at[lines(row, rows)], 4)
    load_up = load(up_hbm.at[:, lines(row, units)], up_block.at[mine], 5)
    load_down = load(down_hbm.at[:, lines(row, units)], down_block.at[mine], 6)
    load_tables = [load(cos_hbm, cos_part, 7), load(sin_hbm, sin_part, 8), load(bias_hbm, bias, 9)]

    barrier = pltpu.get_barrier_semaphore()
    for hop in hops:
        pl.semaphore_signal(barrier, inc=1, device_id={"row": other(row, hop)}, device_id_type=MESH)
    for step in range(1, 8):
        pl.semaphore_signal(barrier, inc=1, device_id={"leaf": (leaf + step) % 8}, device_id_type=MESH)
    pl.semaphore_wait(barrier, 10)

    def row_copy(source, target, kind, hop):
        copy = pltpu.make_async_remote_copy(
            source,
            target,
            row_send_sem.at[kind, hop - 1],
            row_recv_sem.at[kind, hop - 1],
            device_id={"row": other(row, hop)},
            device_id_type=MESH,
        )
        copy.start()
        sent.append(copy)

    def row_landed(target, kind):
        for hop in hops:
            landed(target(other(row, hop), hop), row_recv_sem.at[kind, hop - 1])

    def leaf_copy(source, target, send_sem, recv_sem, to):
        return pltpu.make_async_remote_copy(
            source, target, send_sem, recv_sem, device_id={"leaf": to}, device_id_type=MESH
        )

    for hop in hops:
        row_copy(pack_hbm.at[other(row, hop)], block.at[mine, pl.ds(0, wide)], 0, hop)
    for hop in hops:
        row_copy(gains_hbm, gains_leaf.at[row], 1, hop)
    for hop in hops:
        row_copy(gate_hbm.at[:, lines(other(row, hop), units)], gate_block.at[mine], 2, hop)
    for hop in hops:
        row_copy(tokens_hbm, tokens.at[lines(row, rows)], 3, hop)
    for hop in hops:
        row_copy(up_hbm.at[:, lines(other(row, hop), units)], up_block.at[mine], 4, hop)
    for hop in hops:
        row_copy(down_hbm.at[:, lines(other(row, hop), units)], down_block.at[mine], 5, hop)

    sizes = (size, size, size, size // 2, size // 2)

    def spread(kind, source, whole):
        place = whole.at[lines(leaf, sizes[kind])]
        across = leaf_copy(
            source, place, line_send_sem.at[kind, 2], line_recv_sem.at[kind, 2], 2 * other(z, 2) + core
        )
        across.start()
        sent.append(across)
        forth = leaf_copy(source, place, line_send_sem.at[kind, 0], line_recv_sem.at[kind, 0], 2 * z + 2 + core)
        back = leaf_copy(source, place, line_send_sem.at[kind, 1], line_recv_sem.at[kind, 1], 2 * z - 2 + core)

        @pl.when(z < 3)
        def _():
            forth.start()

        @pl.when(z > 0)
        def _():
            back.start()

        beside = leaf_copy(source, place, core_send_sem.at[kind, 3], core_recv_sem.at[kind, 3], 2 * z + 1 - core)
        beside.start()
        sent.append(beside)
        save(source, place)

        def done():
            @pl.when(z < 3)
            def _():
                forth.wait_send()

            @pl.when(z > 0)
            def _():
                back.wait_send()

        return done

    def arrival(step):
        inner_slot, inner_chip = ((2, other(z, 2)), (0, z - 1), (1, z + 1))[step]
        end_slot, end_chip = ((1 - far, 1 + far), (2, other(z, 2)), (3, 3 - z))[step]
        return end_slot + inner * (inner_slot - end_slot), end_chip + inner * (inner_chip - end_chip)

    def pass_on(kind, whole, step):
        slot, chip = arrival(step)
        place = whole.at[lines(2 * chip + core, sizes[kind])]
        landed(place, line_recv_sem.at[kind, slot])
        beside = leaf_copy(place, place, core_send_sem.at[kind, step], core_recv_sem.at[kind, step], 2 * z + 1 - core)
        beside.start()
        sent.append(beside)
        if step == 0:
            onward = leaf_copy(place, place, line_send_sem.at[kind, 3], line_recv_sem.at[kind, 3], 6 * far + core)

            @pl.when(inner == 1)
            def _():
                onward.start()

            def done():
                @pl.when(inner == 1)
                def _():
                    onward.wait_send()

            return done

    def gathered(kind, whole):
        landed(whole.at[lines(2 * z + 1 - core, sizes[kind])], core_recv_sem.at[kind, 3])
        for step in range(3):
            chip = arrival(step)[1]
            landed(whole.at[lines(2 * chip + 1 - core, sizes[kind])], core_recv_sem.at[kind, step])

    load_pack.wait()
    load_output.wait()
    row_landed(lambda source, hop: block.at[lines(source, own), pl.ds(0, wide)], 0)
    done = [spread(0, block, attn_mat)]

    load_gains.wait()
    row_landed(lambda source, hop: gains_leaf.at[source], 1)
    for step in range(1, 8):
        copy = leaf_copy(
            gains_leaf, gains_all.at[leaf], leaf_send_sem.at[step - 1], leaf_recv_sem.at[step - 1], (leaf + step) % 8
        )
        copy.start()
        sent.append(copy)
    gains_all[leaf] = gains_leaf[...]

    load_gate.wait()
    row_landed(lambda source, hop: gate_block.at[lines(source, own)], 2)
    done.append(pass_on(0, attn_mat, 0))
    pass_on(0, attn_mat, 1)
    done.append(spread(1, gate_block, gate_out))
    pass_on(0, attn_mat, 2)
    gathered(0, attn_mat)
    saved[0].wait()

    load_tokens.wait()
    row_landed(lambda source, hop: tokens.at[lines(source, rows)], 3)

    def project_step(j, carry):
        at = lines(j, rows)
        some = tokens[at, :]
        for i, out in enumerate((query_pre, key_pre)):
            product = dot(some, attn_mat[:, i * part : (i + 1) * part], NN)
            out[at, :] = product
            square = jnp.sum(product * product, axis=1, keepdims=True)
            squares[i : i + 1, at] = jnp.broadcast_to(square, (rows, HEAD_DIM)).T[0:1]
        value[at, :] = dot(some, attn_mat[:, 2 * part : wide], NN, bf16)
        return carry

    squares[...] = jnp.zeros_like(squares)
    lax.fori_loop(0, 4, project_step, 0)
    for hop in hops:
        row_copy(squares, squares_in.at[hop - 1], 7, hop)
    for hop in hops:
        row_copy(
            attn_mat.at[lines(other(row, hop), 2 * size), pl.ds(wide, part)], output_in.at[row], 6, hop
        )
    swapped = len(sent)
    keep = load(attn_mat.at[lines(row, 2 * size), pl.ds(wide, part)], output_in.at[row], 10)
    load_up.wait()
    row_landed(lambda source, hop: up_block.at[lines(source, own)], 4)
    done.append(spread(2, up_block, up_out))
    save(attn_mat, attn_out)
    save(tokens, tokens_out)
    save(query_pre, query_pre_out)
    save(key_pre, key_pre_out)
    save(value, value_out)
    for step in range(1, 8):
        landed(gains_all.at[(leaf - step + 8) % 8], leaf_recv_sem.at[step - 1])
    for source in range(8):
        for pair in range(2):
            first = (2 * source + pair) * HEAD_DIM
            gains[:, first : first + HEAD_DIM] = gains_all[source, 2 * pair] + gains_all[source, 2 * pair + 1]
    save(gains, gains_out)
    for table in load_tables:
        table.wait()
    row_landed(lambda source, hop: squares_in.at[hop - 1], 7)
    scales = lax.rsqrt((squares[...] + squares_in[0] + squares_in[1] + squares_in[2]) / width + epsilon)
    scale_rows[...] = scales
    save(scale_rows, scales_out)
    for i in range(2):
        scale_columns[i] = jnp.broadcast_to(scales[i : i + 1], (HEAD_DIM, 4 * rows)).T

    def head_step(h, carry):
        at = lines(h, HEAD_DIM)
        at_gain = lines(row * heads + h, HEAD_DIM)
        for i, (pre, out) in enumerate(((query_pre, query), (key_pre, key))):
            scaled = pre[:, at] * scale_columns[i] * gains[i : i + 1, at_gain]
            out[:, at] = turn(scaled, cos_part[...], sin_part[...]).astype(bf16)
        for first in range(0, 4 * rows, rows):
            last = first + rows
            scores = dot(key[:last, at], query[first:last, at], NT) * scale
            scores = scores + bias[:last, first:last].astype(f32)
            top = jnp.max(scores, axis=0, keepdims=True)
            probs = jnp.exp(scores - top)
            mass = jnp.sum(probs, axis=0, keepdims=True)
            probs_low = (probs * (1.0 / mass)).astype(bf16)
            turned = dot(value[:last, at], probs_low, TN)
            context[first:last, at] = turned.T.astype(bf16)
            lse[lines(h, 8), first:last] = jnp.broadcast_to(top + jnp.log(mass), (8, rows))
        return carry

    lax.fori_loop(0, heads, head_step, 0)
    done.append(pass_on(1, gate_out, 0))
    save(query, query_out)
    save(key, key_out)
    save(context, context_out)
    save(lse, lse_out)

    keep.wait()
    row_landed(lambda source, hop: output_in.at[source], 6)
    for i in range(2):
        for source in range(4):
            for j in range(4):
                output_mat[i * size + source * own : i * size + (source + 1) * own, j * part : (j + 1) * part] = (
                    output_in[source, i * size + j * own : i * size + (j + 1) * own, :]
                )
    save(output_mat, output_out)

    def output_part(hop, store):
        some = context[lines(other(row, hop), rows), :]
        for j in range(4):
            columns = slice(j * part, (j + 1) * part)
            store(columns, dot(some, output_mat[:, columns], NN))

    half = rows // 2
    top, bottom = pl.ds(0, half), pl.ds(half, half)
    for hop in hops:

        def store(columns, values):
            rows_send[hop - 1, :, columns] = values.astype(bf16)

        output_part(hop, store)
        if hop == 3:
            row_copy(rows_send.at[2, top], half_in.at[0], 8, 1)
            row_copy(rows_send.at[2, bottom], half_in.at[1], 8, 2)
        else:
            early = (top, bottom)[hop - 1]
            row_copy(rows_send.at[hop - 1, early], rows_in.at[hop - 1, early], 10, hop)
    for hop in (1, 2):
        late = (bottom, top)[hop - 1]
        landed(half_in.at[2 - hop], row_recv_sem.at[8, 2 - hop])
        rows_send[hop - 1, late] = (rows_send[hop - 1, late].astype(f32) + half_in[2 - hop].astype(f32)).astype(bf16)
        row_copy(rows_send.at[hop - 1, late], rows_in.at[hop - 1, late], 11, hop)

    def own_store(columns, values):
        attn[:, columns] = values

    output_part(0, own_store)

    pass_on(1, gate_out, 1)
    done.append(pass_on(2, up_out, 0))
    for hop in (1, 2):
        early, late = ((top, bottom), (bottom, top))[hop - 1]
        landed(rows_in.at[hop - 1, early], row_recv_sem.at[10, hop - 1])
        landed(rows_in.at[hop - 1, late], row_recv_sem.at[11, hop - 1])
        attn[...] += rows_in[hop - 1].astype(f32)
    mean = jnp.sum(attn[...] * attn[...], axis=1, keepdims=True) / width
    factor = lax.rsqrt(mean + epsilon)
    unit_scale[...] = jnp.broadcast_to(factor, unit_scale.shape)
    attn[...] = attn[...] * factor
    hidden[...] = tokens[lines(row, rows), :].astype(f32) + attn[...] * gains[2:3, :]
    hidden_all[lines(row, rows), :] = hidden[...].astype(bf16)
    for hop in (1, 2):
        place = hidden_all.at[lines(row, rows)]
        row_copy(place, place, 9, hop)
    save(attn, unit_out)
    save(unit_scale, unit_scale_out)
    save(hidden, hidden_out)
    for hop in (1, 2):
        landed(hidden_all.at[lines(other(row, hop), rows)], row_recv_sem.at[9, hop - 1])
        place = hidden_all.at[lines(2 * other(row, hop) + hop - 1, half)]
        row_copy(place, place, 12, 3 - hop)
    for hop in (1, 2):
        landed(hidden_all.at[lines(2 * other(row, 3) + 2 - hop, half)], row_recv_sem.at[12, hop - 1])
    save(hidden_all, hidden_all_out)
    pass_on(1, gate_out, 2)
    pass_on(2, up_out, 1)
    load_down.wait()
    row_landed(lambda source, hop: down_block.at[lines(source, own)], 5)
    downs = (first_out, second_out)
    for h in range(2):
        done.append(spread(3 + h, down_block.at[pl.ds(h * size // 2, size // 2)], downs[h]))
    pass_on(2, up_out, 2)
    gathered(1, gate_out)
    gathered(2, up_out)

    for copy in sent[:swapped]:
        copy.wait_send()
    for finish_sends in done[:2]:
        finish_sends()
    for copy in saved[1:]:
        copy.wait()
    saved.clear()

    def quarter(j):
        columns = pl.ds(j * part, part)
        return [
            load(source.at[:, columns], attn_mat.at[:, pl.ds((2 * i + j % 2) * part, part)], 11 + 2 * i + j % 2)
            for i, source in enumerate((gate_out, up_out))
        ]

    coming = quarter(0)
    for j in range(4):
        for copy in coming:
            copy.wait()
        if j < 3:
            coming = quarter(j + 1)
        for copy in saved:
            copy.wait()
        saved.clear()

        slot = j % 2

        def units_step(i, carry):
            at = lines(i, rows)
            some = hidden_all[at, :]
            gate = dot(some, attn_mat[:, slot * part : (slot + 1) * part], NN)
            up = dot(some, attn_mat[:, (2 + slot) * part : (3 + slot) * part], NN)
            query_pre[at, :] = gate
            key_pre[at, :] = up
            value[at, :] = (gate * jax.nn.sigmoid(gate) * up).astype(bf16)
            return carry

        lax.fori_loop(0, 4, units_step, 0)
        columns = pl.ds(j * part, part)
        save(query_pre, gate_pre_out.at[:, columns])
        save(key_pre, up_pre_out.at[:, columns])
        save(value, activated_out.at[:, columns])
        if j == 1:
            done.append(pass_on(3, first_out, 0))
        if j == 2:
            done.append(pass_on(4, second_out, 0))
            pass_on(3, first_out, 1)
    pass_on(3, first_out, 2)
    pass_on(4, second_out, 1)
    pass_on(4, second_out, 2)
    gathered(3, first_out)
    gathered(4, second_out)

    for finish_sends in done[2:]:
        finish_sends()
    for copy in sent[swapped:]:
        copy.wait_send()
    for copy in saved:
        copy.wait()


def front(tokens, pack, output_block, gate, up, down, gain_tile, cos_wide, sin_wide, bias):
    rows, width = tokens.shape
    total, part, own = 4 * rows, width // 4, pack.shape[1]
    wide, units, size = 3 * part, gate.shape[1] // 4, 4 * own
    heads = part // HEAD_DIM
    shape = jax.ShapeDtypeStruct
    outs = [
        shape((width, width), bf16),
        shape((width, units), bf16),
        shape((width, units), bf16),
        shape((width // 2, units), bf16),
        shape((width // 2, units), bf16),
        shape((total, units), f32),
        shape((total, units), f32),
        shape((total, units), bf16),
        shape((total, width), bf16),
        shape((total, part), f32),
        shape((total, part), f32),
        shape((total, part), bf16),
        shape((8, total), f32),
        shape((total, part), bf16),
        shape((total, part), bf16),
        shape((total, part), bf16),
        shape((8 * heads, total), f32),
        shape((part, width), bf16),
        shape((rows, width), f32),
        shape((rows, HEAD_DIM), f32),
        shape((rows, width), f32),
        shape((total, width), bf16),
        shape((8, width), f32),
    ]
    vmem, dma = pltpu.VMEM, pltpu.SemaphoreType.DMA
    return pl.pallas_call(
        front_kernel,
        in_specs=[pl.BlockSpec(memory_space=pl.ANY)] * 10,
        out_specs=[pl.BlockSpec(memory_space=pl.ANY)] * len(outs),
        out_shape=outs,
        scratch_shapes=[
            vmem((size, width), bf16),
            vmem((width, width), bf16),
            vmem((size, units), bf16),
            vmem((size, units), bf16),
            vmem((size, units), bf16),
            vmem((total, width), bf16),
            vmem((total, part), f32),
            vmem((total, part), f32),
            vmem((total, part), bf16),
            vmem((total, part), bf16),
            vmem((total, part), bf16),
            vmem((total, part), bf16),
            vmem((8 * heads, total), f32),
            vmem((total, total), bf16),
            vmem((total, HEAD_DIM), f32),
            vmem((total, HEAD_DIM), f32),
            vmem((2, total, HEAD_DIM), f32),
            vmem((4, part, part), bf16),
            vmem((part, width), bf16),
            vmem((3, rows, width), bf16),
            vmem((2, rows, width), bf16),
            vmem((2, rows // 2, width), bf16),
            vmem((rows, width), f32),
            vmem((rows, HEAD_DIM), f32),
            vmem((rows, width), f32),
            vmem((total, width), bf16),
            vmem((8, total), f32),
            vmem((3, 8, total), f32),
            vmem((8, total), f32),
            vmem((4, 8, HEAD_DIM), f32),
            vmem((8, 4, 8, HEAD_DIM), f32),
            vmem((8, width), f32),
            dma((15,)),
            dma((32,)),
            dma((13, 3)),
            dma((13, 3)),
            dma((7,)),
            dma((7,)),
            dma((5, 4)),
            dma((5, 4)),
            dma((5, 4)),
            dma((5, 4)),
        ],
        compiler_params=pltpu.CompilerParams(
            collective_id=2, has_side_effects=True, vmem_limit_bytes=62 * 2**20
        ),
        cost_estimate=pl.CostEstimate(
            flops=10 * total * width * part, bytes_accessed=100 * 2**20, transcendentals=0
        ),
    )(tokens, pack, output_block, gate, up, down, gain_tile, cos_wide, sin_wide, bias)


def body(
    inputs,
    cotangent,
    seg_lengths,
    seg_parents,
    w_query,
    w_key,
    w_value,
    w_output,
    gain_query,
    gain_key,
    gain_attn,
    w_gate,
    w_up,
    w_down,
    gain_mlp,
):
    trees, rows_dev, width = inputs.shape
    count, leaves, me = lax.axis_size("row"), lax.axis_size("leaf"), lax.axis_index("row")
    tree_len = rows_dev * count
    part = width // count
    own = w_query.shape[0]
    group = count * own // 2
    units = w_gate.shape[1] // count
    tokens = inputs.reshape(rows_dev, width)

    def leaf_gather(block):
        return lax.all_gather(block, "leaf", axis=0, tiled=True)

    def leaf_scatter(block):
        return lax.psum_scatter(block, "leaf", scatter_dimension=0, tiled=True)

    bias, cos_wide, sin_wide = tree_tables(seg_lengths[0], seg_parents[0], tree_len)
    fast = leaves == 8 and count == 4
    if fast:
        def split_columns(weight):
            return jnp.swapaxes(weight.astype(bf16).reshape(own, count, -1), 0, 1)

        gain_own = jnp.stack([gain_query, gain_key, gain_attn, gain_mlp]).astype(bf16).astype(f32)
        gain_tile = lax.dynamic_update_slice(jnp.zeros((8, HEAD_DIM), f32), gain_own, (0, (me % 2) * own))
        (
            attn_mat,
            gate_mat,
            up_mat,
            down_first,
            down_second,
            gate_pre,
            up_pre,
            activated,
            all_tokens,
            query_pre,
            key_pre,
            value,
            scales,
            query,
            key,
            context,
            lse,
            output_mat,
            attn_unit,
            attn_scale,
            hidden,
            hidden_all,
            gains_all,
        ) = front(
            tokens,
            jnp.concatenate([split_columns(w) for w in (w_query, w_key, w_value)], axis=2),
            split_columns(w_output).reshape(count * own, part),
            w_gate.astype(bf16),
            w_up.astype(bf16),
            w_down.astype(bf16),
            gain_tile,
            cos_wide,
            sin_wide,
            bias,
        )
        scales, attn_scale = scales[:2], attn_scale[:, :1]
        down_halves = [down_first, down_second]
        query_scale, key_scale = scales[0][:, None], scales[1][:, None]
        attn_gain, mlp_gain = gains_all[2], gains_all[3]
        head_gains = lax.dynamic_slice_in_dim(gains_all[:2], me * part, part, 1)
    else:
        qkv_block = columns_in(w_query, w_key, w_value)
        gains_own = jnp.stack([gain_query, gain_key, gain_attn, gain_mlp]).astype(bf16).reshape(1, 4 * own)
        gains_leaf = gather_rows(gains_own).reshape(count * own, 4)
        attn_block = jnp.concatenate(
            [
                qkv_block,
                w_output.astype(bf16).reshape(count * own, part),
                jnp.pad(gains_leaf, ((0, 0), (0, HEAD_DIM - 4))),
            ],
            axis=1,
        )
        attn_mat = leaf_gather(attn_block)
        qkv_mat = attn_mat[:, : 3 * part]
        output_rows = attn_mat[:, 3 * part : 4 * part].reshape(count, leaves // count, own, width)
        gains_all = attn_mat[:, 4 * part : 4 * part + 4].reshape(leaves, count, 4, own)
        gains_all = jnp.moveaxis(gains_all, 2, 0).reshape(4, width).astype(f32)
        gate_block = columns_in(tie(w_gate, qkv_block))
        up_block = columns_in(tie(w_up, qkv_block))
        down_block = columns_in(tie(w_down, qkv_block))
        all_tokens = gather_rows(tie(tokens, gate_block, up_block, down_block))

        query_pre, key_pre, value, squares = project(all_tokens, attn_mat, part)
        gate_mat = leaf_gather(gate_block)
        up_mat = leaf_gather(up_block)
        down_halves = [leaf_gather(down_block[h * group : (h + 1) * group]) for h in range(2)]

        squares = sum_rows(squares)
        scales = lax.rsqrt(squares / width + epsilon)
        query_scale, key_scale = scales[0][:, None], scales[1][:, None]
        attn_gain, mlp_gain = gains_all[2], gains_all[3]
        head_gains = lax.dynamic_slice_in_dim(gains_all[:2], me * part, part, 1)
        output_rows = tie(output_rows, scales)
        output_mat = jnp.zeros((leaves // count, count, own, width), bf16)
        for hop in range(count):
            piece = lax.dynamic_index_in_dim(output_rows, me ^ hop, 0, keepdims=False)
            if hop:
                piece = swap(piece, hop)
            output_mat = lax.dynamic_update_index_in_dim(output_mat, piece, me ^ hop, 1)
        output_mat = output_mat.reshape(part, width)
        query, key, context, lse = attend(
            query_pre, key_pre, value, scales.T, head_gains, cos_wide, sin_wide, bias
        )
        attn_pre = dot_scatter([context], [output_mat], NN)
        attn_scale = lax.rsqrt(jnp.mean(attn_pre * attn_pre, axis=-1, keepdims=True) + epsilon)
        attn_unit = attn_pre * attn_scale
        hidden = tokens.astype(f32) + attn_unit * attn_gain
        hidden_all = gather_rows(hidden.astype(bf16))

    if not fast:
        gate_pre = dot(hidden_all, gate_mat, NN)
        up_pre = dot(hidden_all, up_mat, NN)
        activated = (gate_pre * jax.nn.sigmoid(gate_pre) * up_pre).astype(bf16)
    sigmoid_gate = jax.nn.sigmoid(gate_pre)
    mlp_halves = [dot_scatter([activated], [down_halves[h]], NT) for h in range(2)]
    grad_final = cotangent.reshape(rows_dev, width).astype(f32)
    halves = range(2)

    def split(rows):
        rows = rows.reshape(rows.shape[:-1] + (leaves, 2, group))
        return [rows[..., h, :].reshape(rows.shape[:-3] + (width // 2,)) for h in halves]

    weighted = tie(split(grad_final * mlp_gain), hidden_all)
    square = sum(jnp.sum(m * m, axis=-1, keepdims=True) for m in mlp_halves) / width
    cross = sum(jnp.sum(m * w, axis=-1, keepdims=True) for m, w in zip(mlp_halves, weighted)) / width
    mlp_scale = lax.rsqrt(square + epsilon)
    grad_mlp = [
        (mlp_scale * (w - m * (mlp_scale * mlp_scale * cross))).astype(bf16) for m, w in zip(mlp_halves, weighted)
    ]
    grad_mlp_halves = [gather_rows(grad_mlp[h]) for h in halves]
    down_sums = [dot(grad_mlp_halves[h], activated, TN, bf16) for h in range(2)]
    down_shards = [leaf_scatter(down_sums[h]) for h in range(2)]
    grad_act = dot(tie(grad_mlp_halves[0], down_sums[0]), down_halves[0], NN)
    grad_act = grad_act + dot(tie(grad_mlp_halves[1], down_sums[1]), down_halves[1], NN)
    grad_gate = (grad_act * up_pre * sigmoid_gate * (1.0 + gate_pre * (1.0 - sigmoid_gate))).astype(bf16)
    grad_up = (grad_act * gate_pre * sigmoid_gate).astype(bf16)
    wide = width // 2
    gate_sum = dot(hidden_all, grad_gate, TN, bf16)
    parts, coming = [], []
    for h in range(2):
        one = tie(grad_gate, gate_sum, *parts), tie(grad_up, gate_sum, *parts)
        part_h = sum(
            dot(left, right[h * wide : (h + 1) * wide], NT) for left, right in zip(one, (gate_mat, up_mat))
        ).astype(bf16)
        parts.append(part_h)
        coming.append(send_rows(part_h))
    grad_hidden = grad_final + jnp.concatenate(
        [add_rows(part_h, pieces) for part_h, pieces in zip(parts, coming)], axis=1
    )
    gate_sum = tie(gate_sum, *down_sums)
    gate_shard = leaf_scatter(gate_sum)

    grad_attn, grad_attn_gain = norm_back(grad_hidden, attn_unit, attn_scale, attn_gain)
    grad_attn_low = grad_attn.astype(bf16)
    up_sum = dot(hidden_all, tie(grad_up, grad_attn_low), TN, bf16)
    grad_attn_all = gather_rows(tie(grad_attn_low, *down_shards), up_sum)
    grad_context = dot(grad_attn_all, output_mat, NT, bf16)
    up_shard = leaf_scatter(tie(up_sum, gate_sum))
    grad_context = tie(grad_context, gate_shard)
    grad_query, grad_key, grad_value, inner_query, inner_key, grad_head_gains = attend_back(
        query, key, value, bias, lse, grad_context, query_pre, key_pre, scales.T, head_gains, cos_wide, sin_wide
    )
    inner = sum_rows(jnp.stack([jnp.sum(inner_query, axis=1), jnp.sum(inner_key, axis=1)])) / width
    output_part = dot(context, tie(grad_attn_all, inner), TN, bf16).reshape(leaves // count, count, own, width)
    grad_query_low = (
        query_scale * (grad_query * head_gains[0] - query_pre * (query_scale * inner[0][:, None]))
    ).astype(bf16)
    grad_key_low = (
        key_scale * (grad_key * head_gains[1] - key_pre * (key_scale * inner[1][:, None]))
    ).astype(bf16)
    grad_qkv = jnp.concatenate([grad_query_low, grad_key_low, grad_value], axis=1)
    gate_out = columns_out(tie(gate_shard, inner_query))
    down_out = columns_out(tie(jnp.concatenate(down_shards), inner_query))
    mlp_halves = tie(mlp_halves, inner_query)
    mlp_unit = jnp.stack([m.reshape(rows_dev, leaves, group) for m in mlp_halves], axis=2).reshape(rows_dev, width)
    mlp_unit = mlp_unit * mlp_scale
    outputs = (hidden + mlp_unit * mlp_gain).astype(bf16).reshape(inputs.shape)
    grad_mlp_gain = jnp.sum(grad_final * mlp_unit, axis=0)

    wide_part = jnp.stack([tie(grad_attn_gain, inner), grad_mlp_gain]).reshape(2, leaves, count, own)
    narrow_part = grad_head_gains.reshape(2, leaves // count, count, own)
    grad_qkv = tie(grad_qkv, gate_out, down_out, outputs)
    if fast:
        gain_part = jnp.zeros((count, leaves, 8, HEAD_DIM), f32)
        gain_part = lax.dynamic_update_slice(
            gain_part, jnp.transpose(narrow_part, (2, 1, 0, 3)), (0, me * (leaves // count), 0, 0)
        )
        gain_part = lax.dynamic_update_slice(gain_part, jnp.transpose(wide_part, (2, 1, 0, 3)), (0, 0, 2, 0))
        *grad_mats, grad_output, grad_tokens, up_out, grad_gains = finish(
            all_tokens, grad_qkv, attn_mat, output_part, grad_hidden, up_shard, gain_part
        )
        grad_inputs, up_out, grad_gains = grad_tokens.reshape(inputs.shape), [up_out], grad_gains[:4, :own]
    else:
        wide_sum = jnp.zeros((2, leaves, own), f32)
        narrow_all = jnp.zeros((2, leaves, own), f32)
        for hop in range(count):
            piece = lax.dynamic_index_in_dim(jnp.concatenate([wide_part, narrow_part], axis=1), me ^ hop, 2, keepdims=False)
            if hop:
                piece = swap(piece, hop)
            wide_sum = wide_sum + piece[:, :leaves]
            narrow_all = lax.dynamic_update_slice_in_dim(
                narrow_all, piece[:, leaves:], (me ^ hop) * (leaves // count), 1
            )
        grad_gains = jnp.concatenate([narrow_all, wide_sum], axis=0)
        stride = 1
        while stride < leaves:
            grad_gains = grad_gains + lax.ppermute(
                grad_gains, "leaf", [(i, i ^ stride) for i in range(leaves)]
            )
            stride *= 2
        grad_gains = lax.dynamic_index_in_dim(grad_gains, lax.axis_index("leaf"), 1, keepdims=False)
        output_turned = jnp.zeros((count, leaves // count, own, width), bf16)
        for hop in range(count):
            piece = lax.dynamic_index_in_dim(output_part, me ^ hop, 1, keepdims=False)
            if hop:
                piece = swap(piece, hop)
            output_turned = lax.dynamic_update_index_in_dim(output_turned, piece, me ^ hop, 0)
        attn_sum = sums_beside(all_tokens, grad_qkv, output_turned.reshape(leaves * count * own, part))
        grad_tokens = grad_hidden + dot_scatter([grad_qkv], [qkv_mat], NT)
        grad_inputs = grad_tokens.astype(bf16).reshape(inputs.shape)
        attn_shard = leaf_scatter(tie(attn_sum, up_shard))
        up_out = columns_out(up_shard)
        grad_mats = columns_out(attn_shard[:, : 3 * part], 3)
        grad_output = attn_shard[:, 3 * part :].reshape(own, width).astype(f32)
    return (
        outputs,
        grad_inputs,
        *grad_mats,
        grad_output,
        grad_gains[0],
        grad_gains[1],
        grad_gains[2],
        *gate_out,
        *up_out,
        *down_out,
        grad_gains[3],
    )


def solution(mesh):
    both = ("leaf", "row")
    token_spec, tree_spec, matrix_spec, gain_spec = P("leaf", "row", None), P("leaf", None), P(both, None), P(both)
    return jax.shard_map(
        body,
        mesh=mesh,
        in_specs=(token_spec,) * 2 + (tree_spec,) * 2 + (matrix_spec,) * 4 + (gain_spec,) * 3 + (matrix_spec,) * 3 + (gain_spec,),
        out_specs=(token_spec,) * 2 + (matrix_spec,) * 4 + (gain_spec,) * 3 + (matrix_spec,) * 3 + (gain_spec,),
        check_vma=False,
    )
```

```python
import functools
import math

import jax
import jax.numpy as jnp
from jax import lax
from jax.experimental import pallas as pl
from jax.experimental.pallas import tpu as pltpu
from jax.sharding import PartitionSpec as P

HEAD_DIM = 128
MESH = pl.DeviceIdType.MESH

epsilon = 1e-06
rope_theta = 500000.0
masked_fill = -1e30
bf16 = jnp.bfloat16
f32 = jnp.float32
NN = (((1,), (0,)), ((), ()))
NT = (((1,), (1,)), ((), ()))
TN = (((0,), (0,)), ((), ()))


def dot(left, right, dims, kind=f32):
    return lax.dot_general(left, right, dims, preferred_element_type=f32).astype(kind)


def swap(piece, hop):
    count = lax.axis_size("row")
    return lax.ppermute(piece, "row", [(i, i ^ hop) for i in range(count)])


def gather_rows(rows, *meanwhile):
    count, me = lax.axis_size("row"), lax.axis_index("row")
    size = rows.shape[0]
    whole = jnp.zeros((count * size,) + rows.shape[1:], rows.dtype)
    for hop in range(1, count):
        whole = lax.dynamic_update_slice_in_dim(whole, swap(rows, hop), (me ^ hop) * size, 0)
    return lax.dynamic_update_slice_in_dim(whole, tie(rows, *meanwhile), me * size, 0)


def dot_scatter(lefts, rights, dims, *meanwhile):
    count, me = lax.axis_size("row"), lax.axis_index("row")
    size = lefts[0].shape[0] // count

    def rows_of(hop, lefts):
        parts = [lax.dynamic_slice_in_dim(left, (me ^ hop) * size, size, 0) for left in lefts]
        return sum(dot(part, right, dims) for part, right in zip(parts, rights))

    coming = [swap(rows_of(hop, lefts).astype(bf16), hop) for hop in reversed(range(1, count))]
    total = rows_of(0, [tie(left, *meanwhile) for left in lefts])
    for piece in coming:
        total = total + piece.astype(f32)
    return total


def send_rows(partial):
    count, me = lax.axis_size("row"), lax.axis_index("row")
    size = partial.shape[0] // count
    return [
        swap(lax.dynamic_slice_in_dim(partial, (me ^ hop) * size, size, 0), hop) for hop in reversed(range(1, count))
    ]


def add_rows(partial, coming, *meanwhile):
    size = partial.shape[0] // lax.axis_size("row")
    mine = lax.dynamic_slice_in_dim(tie(partial, *meanwhile), lax.axis_index("row") * size, size, 0)
    return sum([piece.astype(f32) for piece in coming], mine.astype(f32))


def tie(value, *others):
    return lax.optimization_barrier((value,) + others)[0]


def columns_in(*weights):
    count, me = lax.axis_size("row"), lax.axis_index("row")
    size, wide = weights[0].shape[0], weights[0].shape[1] // count
    whole = jnp.zeros((count * size, wide * len(weights)), bf16)
    for hop in range(count):
        piece = jnp.concatenate(
            [lax.dynamic_slice_in_dim(w, (me ^ hop) * wide, wide, 1).astype(bf16) for w in weights], axis=1
        )
        if hop:
            piece = swap(piece, hop)
        whole = lax.dynamic_update_slice_in_dim(whole, piece, (me ^ hop) * size, 0)
    return whole


def columns_out(block, many=1):
    count, me = lax.axis_size("row"), lax.axis_index("row")
    size, wide = block.shape[0] // count, block.shape[1] // many
    whole = [jnp.zeros((size, wide * count), f32)] * many
    for hop in range(count):
        piece = lax.dynamic_slice_in_dim(block, (me ^ hop) * size, size, 0)
        if hop:
            piece = swap(piece, hop)
        for i in range(many):
            own = piece[:, i * wide : (i + 1) * wide].astype(f32)
            whole[i] = lax.dynamic_update_slice_in_dim(whole[i], own, (me ^ hop) * wide, 1)
    return whole


def sum_rows(small):
    count = lax.axis_size("row")
    total = small
    for hop in range(1, count):
        total = total + swap(small, hop)
    return total


def norm_back(grad_out, unit_rows, scaled, gain_row):
    weighted = grad_out * gain_row
    inner = jnp.mean(weighted * unit_rows, axis=-1, keepdims=True)
    return (scaled * (weighted - unit_rows * inner), jnp.sum(grad_out * unit_rows, axis=0))


def tree_tables(length_row, parent_row, total):
    seg_count = parent_row.shape[0]
    segment_ids = jnp.arange(seg_count, dtype=jnp.int32)
    ends = jnp.cumsum(length_row)
    offsets = ends - length_row
    all_rows = jnp.arange(total, dtype=jnp.int32)
    owned_from = (all_rows[:, None] >= offsets[None, :]).astype(f32)
    onehot_all = owned_from - jnp.concatenate(
        [owned_from[:, 1:], jnp.zeros((total, 1), f32)], axis=1
    )
    parents = jnp.sum(onehot_all * parent_row.astype(f32)[None, :], axis=1)
    segments = jnp.sum(onehot_all * segment_ids.astype(f32)[None, :], axis=1)
    lengths = length_row.astype(f32)
    parent_lengths = jnp.sum((parent_row[:, None] == segment_ids[None, :]) * lengths[None, :], axis=1)
    above = jnp.where(segment_ids > 0, lengths[0], 0.0) + jnp.where(parent_row > 0, parent_lengths, 0.0)
    position = all_rows.astype(f32) + jnp.sum(onehot_all * (above - offsets.astype(f32))[None, :], axis=1)
    on_path = (segments[:, None] == segments[None, :]) | (segments[:, None] == parents[None, :]) | (segments[:, None] == 0.0)
    allowed = on_path & (all_rows[:, None] <= all_rows[None, :])
    bias = jnp.where(allowed, 0.0, masked_fill).astype(bf16)
    frequency = jnp.exp(
        jnp.arange(HEAD_DIM // 2, dtype=f32) * (-2.0 * math.log(rope_theta) / HEAD_DIM)
    )
    angles = position[:, None] * frequency[None, :]
    cos_half, sin_half = jnp.cos(angles), jnp.sin(angles)
    cos_wide = jnp.concatenate([cos_half, cos_half], axis=1)
    sin_wide = jnp.concatenate([-sin_half, sin_half], axis=1)
    return (bias, cos_wide, sin_wide)


def turn(vector, cos_part, sin_part):
    return vector * cos_part + pltpu.roll(vector, HEAD_DIM // 2, 1) * sin_part


def project_kernel(tokens_ref, weights_ref, query_ref, key_ref, value_ref, squares_ref):
    part = query_ref.shape[1]
    tokens = tokens_ref[...]
    for i, out_ref in enumerate((query_ref, key_ref)):
        product = dot(tokens, weights_ref[:, i * part : (i + 1) * part], NN)
        out_ref[...] = product
        square = jnp.sum(product * product, axis=1, keepdims=True)
        squares_ref[i : i + 1, :] = jnp.broadcast_to(square, (square.shape[0], HEAD_DIM)).T[0:1]
    value_ref[...] = dot(tokens, weights_ref[:, 2 * part :], NN, bf16)


def project(tokens, weights, part):
    total, width = tokens.shape
    size = 256
    rows = pl.BlockSpec((size, part), lambda i: (i, 0))
    wide = jax.ShapeDtypeStruct((total, part), f32)
    return pl.pallas_call(
        project_kernel,
        grid=(total // size,),
        in_specs=[
            pl.BlockSpec((size, width), lambda i: (i, 0)),
            pl.BlockSpec((width, 3 * part), lambda i: (0, 0)),
        ],
        out_specs=[rows, rows, rows, pl.BlockSpec((2, size), lambda i: (0, i))],
        out_shape=[
            wide,
            wide,
            jax.ShapeDtypeStruct((total, part), bf16),
            jax.ShapeDtypeStruct((2, total), f32),
        ],
        compiler_params=pltpu.CompilerParams(vmem_limit_bytes=48 * 2**20),
        cost_estimate=pl.CostEstimate(
            flops=6 * total * width * part, bytes_accessed=2 * width * (total + 3 * part) + 10 * total * part, transcendentals=0
        ),
    )(tokens, weights)


def attend_kernel(
    block,
    scale,
    query_pre_ref,
    key_pre_ref,
    value_ref,
    scales_ref,
    gains_ref,
    cos_ref,
    sin_ref,
    bias_ref,
    query_ref,
    key_ref,
    context_ref,
    lse_ref,
):
    total = key_ref.shape[0]
    cos_part, sin_part = cos_ref[...], sin_ref[...]
    query_ref[...] = turn(query_pre_ref[...] * scales_ref[:, 0:1] * gains_ref[0:1], cos_part, sin_part).astype(bf16)
    key_ref[...] = turn(key_pre_ref[...] * scales_ref[:, 1:2] * gains_ref[1:2], cos_part, sin_part).astype(bf16)
    for first in range(0, total, block):
        last = first + block
        scores = dot(key_ref[:last], query_ref[first:last], NT) * scale
        scores = scores + bias_ref[:last, first:last].astype(f32)
        top = jnp.max(scores, axis=0, keepdims=True)
        probs = jnp.exp(scores - top)
        mass = jnp.sum(probs, axis=0, keepdims=True)
        probs_low = (probs * (1.0 / mass)).astype(bf16)
        turned = dot(value_ref[:last], probs_low, TN)
        context_ref[first:last, :] = turned.T.astype(bf16)
        lse_ref[:, first:last] = jnp.broadcast_to(top + jnp.log(mass), (8, block))


def head_specs(total):
    part = pl.BlockSpec((total, HEAD_DIM), lambda h: (0, h))
    whole = pl.BlockSpec((total, HEAD_DIM), lambda h: (0, 0))
    gains = pl.BlockSpec((2, HEAD_DIM), lambda h: (0, h))
    scales = pl.BlockSpec((total, 2), lambda h: (0, 0))
    bias = pl.BlockSpec((total, total), lambda h: (0, 0))
    lse = pl.BlockSpec((8, total), lambda h: (h, 0))
    return part, whole, gains, scales, bias, lse


def attend(query_pre, key_pre, value, scales, gains, cos_wide, sin_wide, bias):
    total, width = query_pre.shape
    heads = width // HEAD_DIM
    part, whole, gain, scale, square, lse = head_specs(total)
    low = jax.ShapeDtypeStruct((total, width), bf16)
    return pl.pallas_call(
        functools.partial(attend_kernel, 256, 1.0 / math.sqrt(HEAD_DIM)),
        grid=(heads,),
        in_specs=[part, part, part, scale, gain, whole, whole, square],
        out_specs=[part, part, part, lse],
        out_shape=[low, low, low, jax.ShapeDtypeStruct((8 * heads, total), f32)],
        compiler_params=pltpu.CompilerParams(vmem_limit_bytes=56 * 2**20),
        cost_estimate=pl.CostEstimate(
            flops=4 * total * total * width, bytes_accessed=16 * total * width, transcendentals=total * total * heads
        ),
    )(query_pre, key_pre, value, scales, gains, cos_wide, sin_wide, bias)


def attend_back_kernel(
    block,
    scale,
    query_ref,
    key_ref,
    value_ref,
    bias_ref,
    lse_ref,
    grad_ref,
    query_pre_ref,
    key_pre_ref,
    scales_ref,
    gains_ref,
    cos_ref,
    sin_ref,
    grad_query_ref,
    grad_key_ref,
    grad_value_ref,
    inner_query_ref,
    inner_key_ref,
    grad_gains_ref,
    key_sum,
    value_sum,
):
    total = key_ref.shape[0]

    @pl.when(pl.program_id(0) == 0)
    def _():
        inner_query_ref[...] = jnp.zeros_like(inner_query_ref)
        inner_key_ref[...] = jnp.zeros_like(inner_key_ref)

    key_sum[...] = jnp.zeros_like(key_sum)
    value_sum[...] = jnp.zeros_like(value_sum)
    for first in range(0, total, block):
        last = first + block
        scores = dot(key_ref[:last], query_ref[first:last], NT) * scale
        scores = scores + bias_ref[:last, first:last].astype(f32)
        probs = jnp.exp(scores - lse_ref[0:1, first:last])
        grad_probs = dot(value_ref[:last], grad_ref[first:last], NT)
        inner = jnp.sum(probs * grad_probs, axis=0, keepdims=True)
        grad_scores = (probs * (grad_probs - inner)).astype(bf16)
        turned = dot(key_ref[:last], grad_scores, TN)
        grad_query_ref[first:last, :] = turned.T
        key_sum[:last, :] += dot(grad_scores, query_ref[first:last], NN)
        value_sum[:last, :] += dot(probs.astype(bf16), grad_ref[first:last], NN)
    grad_value_ref[...] = value_sum[...].astype(bf16)
    cos_part, sin_part = cos_ref[...], -sin_ref[...]
    for row, (grad, out_ref, pre_ref, inner_ref) in enumerate(
        (
            (grad_query_ref[...], grad_query_ref, query_pre_ref, inner_query_ref),
            (key_sum[...], grad_key_ref, key_pre_ref, inner_key_ref),
        )
    ):
        grad = turn(grad * scale, cos_part, sin_part)
        by_unit = grad * (pre_ref[...] * scales_ref[:, row : row + 1])
        inner_ref[...] += by_unit * gains_ref[row : row + 1]
        grad_gains_ref[row : row + 1, :] = jnp.sum(by_unit, axis=0, keepdims=True)
        out_ref[...] = grad


def attend_back(query, key, value, bias, lse, grad_context, query_pre, key_pre, scales, gains, cos_wide, sin_wide):
    total, width = query.shape
    heads = width // HEAD_DIM
    part, whole, gain, scale, square, lse_spec = head_specs(total)
    wide = jax.ShapeDtypeStruct((total, width), f32)
    narrow = jax.ShapeDtypeStruct((total, HEAD_DIM), f32)
    return pl.pallas_call(
        functools.partial(attend_back_kernel, 256, 1.0 / math.sqrt(HEAD_DIM)),
        grid=(heads,),
        in_specs=[part, part, part, square, lse_spec, part, part, part, scale, gain, whole, whole],
        out_specs=[part, part, part, whole, whole, gain],
        out_shape=[
            wide,
            wide,
            jax.ShapeDtypeStruct((total, width), bf16),
            narrow,
            narrow,
            jax.ShapeDtypeStruct((2, width), f32),
        ],
        scratch_shapes=[pltpu.VMEM((total, HEAD_DIM), f32)] * 2,
        compiler_params=pltpu.CompilerParams(vmem_limit_bytes=58 * 2**20),
        cost_estimate=pl.CostEstimate(
            flops=10 * total * total * width, bytes_accessed=30 * total * width, transcendentals=total * total * heads
        ),
    )(query, key, value, bias, lse, grad_context, query_pre, key_pre, scales, gains, cos_wide, sin_wide)


def sums_kernel(tokens_ref, grads_ref, side_ref, out_ref):
    wide = grads_ref.shape[1]
    out_ref[:, :wide] = dot(tokens_ref[...], grads_ref[...], TN, bf16)
    out_ref[:, wide:] = side_ref[...]


def sums_beside(tokens, grads, side):
    total, rows = tokens.shape
    wide, extra = grads.shape[1], side.shape[1]
    size = 256
    return pl.pallas_call(
        sums_kernel,
        grid=(rows // size,),
        in_specs=[
            pl.BlockSpec((total, size), lambda i: (0, i)),
            pl.BlockSpec((total, wide), lambda i: (0, 0)),
            pl.BlockSpec((size, extra), lambda i: (i, 0)),
        ],
        out_specs=pl.BlockSpec((size, wide + extra), lambda i: (i, 0)),
        out_shape=jax.ShapeDtypeStruct((rows, wide + extra), bf16),
        compiler_params=pltpu.CompilerParams(vmem_limit_bytes=40 * 2**20),
        cost_estimate=pl.CostEstimate(
            flops=2 * total * rows * wide, bytes_accessed=2 * rows * (total + wide + 2 * extra), transcendentals=0
        ),
    )(tokens, grads, side)


def landed(ref, sem):
    pltpu.make_async_copy(ref, ref, sem).wait()


def line_order(z):
    far, inner = z // 2, ((z + 1) // 2) % 2
    blocks = []
    for end, middle in ((3, 0), (2, 2), (1, 3), (0, 1)):
        first = end + inner * (middle - end)
        blocks.append(first + far * (3 - 2 * first))
    near = 1 + far
    chips = [near + inner * (blocks[0] - near), blocks[1], blocks[2]]
    slots = [3 + inner * (-2 - far), 2 + inner * (far - 2), far + inner * (2 - far)]
    return far, inner, blocks, chips, slots


def other(index, hop):
    return (index, index + 1 - 2 * (index % 2), (index + 2) % 4, 3 - index)[hop]


def final_kernel(
    tokens_hbm,
    grads_hbm,
    weights_hbm,
    output_hbm,
    hidden_hbm,
    up_hbm,
    gains_hbm,
    query_out,
    key_out,
    value_out,
    output_out,
    inputs_out,
    up_out,
    gains_out,
    tokens,
    grads,
    weights,
    hidden,
    core_out,
    core_in,
    mine,
    line_in,
    side,
    side_in,
    side_mine,
    side_line_in,
    tokens_send,
    tokens_in,
    rows_send,
    rows_in,
    up_in,
    gains,
    gains_in,
    gains_line,
    load_sem,
    row_send_sem,
    row_recv_sem,
    core_send_sem,
    core_recv_sem,
    line_send_sem,
    line_recv_sem,
    leaf_send_sem,
    leaf_recv_sem,
):
    leaf, row = lax.axis_index("leaf"), lax.axis_index("row")
    z, core = leaf // 2, leaf % 2
    far, inner, blocks, chips, slots = line_order(z)
    wide, own = grads.shape[1], query_out.shape[0]
    part, size = wide // 3, mine.shape[1]
    rows = tokens_in.shape[1]
    hops = (3, 1, 2)

    loads = [
        pltpu.make_async_copy(tokens_hbm, tokens, load_sem.at[0]),
        pltpu.make_async_copy(grads_hbm, grads, load_sem.at[1]),
        pltpu.make_async_copy(weights_hbm.at[:, pl.ds(0, wide)], weights, load_sem.at[2]),
        pltpu.make_async_copy(hidden_hbm, hidden, load_sem.at[3]),
        pltpu.make_async_copy(output_hbm.at[:, row], side.at[pl.ds(2 * row, 2)], load_sem.at[4]),
        pltpu.make_async_copy(gains_hbm.at[row], gains, load_sem.at[6]),
    ]
    for load in loads:
        load.start()
    barrier = pltpu.get_barrier_semaphore()
    for hop in hops:
        pl.semaphore_signal(barrier, inc=1, device_id={"row": other(row, hop)}, device_id_type=MESH)
    for step in range(1, 8):
        pl.semaphore_signal(barrier, inc=1, device_id={"leaf": (leaf + step) % 8}, device_id_type=MESH)
    pl.semaphore_wait(barrier, 10)

    sent = []

    def row_copy(source, target, kind, hop):
        copy = pltpu.make_async_remote_copy(
            source,
            target,
            row_send_sem.at[kind, hop - 1],
            row_recv_sem.at[kind, hop - 1],
            device_id={"row": other(row, hop)},
            device_id_type=MESH,
        )
        copy.start()
        sent.append(copy)

    def core_copy(source, target, kind, i):
        copy = pltpu.make_async_remote_copy(
            source,
            target,
            core_send_sem.at[kind, i],
            core_recv_sem.at[kind, i],
            device_id={"leaf": 2 * z + 1 - core},
            device_id_type=MESH,
        )
        copy.start()
        sent.append(copy)

    def line_copy(source, target, kind, i):
        return pltpu.make_async_remote_copy(
            source,
            target.at[slots[i]],
            line_send_sem.at[kind, i],
            line_recv_sem.at[kind, slots[i]],
            device_id={"leaf": 2 * chips[i] + core},
            device_id_type=MESH,
        )

    for hop in hops:
        row_copy(gains_hbm.at[other(row, hop)], gains_in.at[hop - 1], 4, hop)
    for hop in hops:
        row_copy(output_hbm.at[:, other(row, hop)], side.at[pl.ds(2 * row, 2)], 0, hop)

    loads[0].wait()
    loads[1].wait()

    def product(block):
        return dot(tokens[:, pl.ds(pl.multiple_of(block * size, size), size)], grads[...], TN)

    def across(i):
        core_out[i] = product(2 * blocks[i] + 1 - core).astype(bf16)
        core_copy(core_out.at[i], core_in.at[i], 0, i)

    across(0)
    across(1)

    def pair(i):
        mine[i] = (product(2 * blocks[i] + core) + core_in[i].astype(f32)).astype(bf16)

    for i in range(4):
        landed(core_in.at[i], core_recv_sem.at[0, i])
        pair(i)
        if i < 2:
            copy = line_copy(mine.at[i], line_in, 0, i)
            copy.start()
            sent.append(copy)
            across(i + 2)
        if i == 2:
            last = line_copy(mine.at[2], line_in, 0, 2)
            sent.append(last)

            @pl.when(inner == 0)
            def _():
                last.start()

    loads[5].wait()
    for hop in hops:
        landed(gains_in.at[hop - 1], row_recv_sem.at[4, hop - 1])
        gains[...] += gains_in[hop - 1]
    for step in range(1, 8):
        copy = pltpu.make_async_remote_copy(
            gains.at[(leaf + step) % 8],
            gains_line.at[step - 1],
            leaf_send_sem.at[step - 1],
            leaf_recv_sem.at[step - 1],
            device_id={"leaf": (leaf + step) % 8},
            device_id_type=MESH,
        )
        copy.start()
        sent.append(copy)

    loads[2].wait()

    def tokens_part(hop, store):
        lines = grads[pl.ds(pl.multiple_of((other(row, hop)) * rows, rows), rows), :]

        def step(j, carry):
            columns = pl.ds(pl.multiple_of(j * part, part), part)
            store(columns, dot(lines, weights[columns, :], NT))
            return carry

        lax.fori_loop(0, weights.shape[0] // part, step, 0)

    for hop in hops:

        def store(columns, values):
            tokens_send[hop - 1, :, columns] = values.astype(bf16)

        tokens_part(hop, store)
        row_copy(tokens_send.at[hop - 1], tokens_in.at[hop - 1], 1, hop)

    loads[4].wait()
    for hop in hops:
        landed(side.at[pl.ds(2 * (other(row, hop)), 2)], row_recv_sem.at[0, hop - 1])
    for i in range(4):
        core_copy(side.at[2 * blocks[i] + 1 - core], side_in.at[i], 1, i)

    for hop in hops:
        row_copy(up_hbm.at[pl.ds((other(row, hop)) * own, own)], up_in.at[row], 2, hop)
    keep = pltpu.make_async_copy(up_hbm.at[pl.ds(row * own, own)], up_in.at[row], load_sem.at[5])
    keep.start()

    @pl.when(inner == 1)
    def _():
        landed(line_in.at[3], line_recv_sem.at[0, 3])
        mine[2] = (mine[2].astype(f32) + line_in[3].astype(f32)).astype(bf16)
        last.start()

    for i in range(4):
        landed(side_in.at[i], core_recv_sem.at[1, i])
        side_mine[i] = (side[2 * blocks[i] + core].astype(f32) + side_in[i].astype(f32)).astype(bf16)

    loads[3].wait()

    def own_store(columns, values):
        hidden[:, columns] += values

    tokens_part(0, own_store)
    gains_out[...] = gains[leaf]
    for step in range(1, 8):
        landed(gains_line.at[step - 1], leaf_recv_sem.at[step - 1])
        gains_out[...] += gains_line[step - 1]

    def near(kind, came, kept):
        for slot in range(2):

            @pl.when(inner + (1 - far) * slot + far * (1 - slot) > 0)
            def _():
                landed(came.at[slot], line_recv_sem.at[kind, slot])
                kept[3] = (kept[3].astype(f32) + came[slot].astype(f32)).astype(bf16)

    def beyond(kind, came, kept):
        landed(came.at[2], line_recv_sem.at[kind, 2])
        kept[3] = (kept[3].astype(f32) + came[2].astype(f32)).astype(bf16)

    near(0, line_in, mine)
    for i in range(2):
        copy = line_copy(side_mine.at[i], side_line_in, 1, i)
        copy.start()
        sent.append(copy)
    side_last = line_copy(side_mine.at[2], side_line_in, 1, 2)
    sent.append(side_last)

    @pl.when(inner == 0)
    def _():
        side_last.start()

    beyond(0, line_in, mine)
    rows_send[...] = mine[3]
    for hop in hops:
        row_copy(rows_send.at[pl.ds(other(row, hop) * own, own)], rows_in.at[hop - 1], 3, hop)

    @pl.when(inner == 1)
    def _():
        landed(side_line_in.at[3], line_recv_sem.at[1, 3])
        side_mine[2] = (side_mine[2].astype(f32) + side_line_in[3].astype(f32)).astype(bf16)
        side_last.start()

    for hop in hops:
        landed(tokens_in.at[hop - 1], row_recv_sem.at[1, hop - 1])
        hidden[...] += tokens_in[hop - 1].astype(f32)
    inputs_out[...] = hidden[...].astype(bf16)

    keep.wait()
    for hop in hops:
        landed(up_in.at[other(row, hop)], row_recv_sem.at[2, hop - 1])
    for source in range(4):
        up_out[:, source * up_in.shape[2] : (source + 1) * up_in.shape[2]] = up_in[source].astype(f32)

    def give(source, values):
        columns = pl.ds(pl.multiple_of(source * part, part), part)
        for i, out in enumerate((query_out, key_out, value_out)):
            out[:, columns] = values[:, i * part : (i + 1) * part].astype(f32)

    give(row, rows_send[pl.ds(pl.multiple_of(row * own, own), own), :])
    near(1, side_line_in, side_mine)
    beyond(1, side_line_in, side_mine)
    output_out[...] = side_mine[3].astype(f32)
    for hop in hops:
        landed(rows_in.at[hop - 1], row_recv_sem.at[3, hop - 1])
        give(other(row, hop), rows_in[hop - 1])
    for copy in sent:
        copy.wait_send()


def finish(tokens, grads, weights, output_part, hidden, up_shard, gain_part):
    total, width = tokens.shape
    wide = grads.shape[1]
    own = output_part.shape[2]
    size, rows, units = 4 * own, hidden.shape[0], up_shard.shape[1]
    matrix = jax.ShapeDtypeStruct((own, width), f32)
    dma = pltpu.SemaphoreType.DMA
    return pl.pallas_call(
        final_kernel,
        in_specs=[pl.BlockSpec(memory_space=pl.ANY)] * 7,
        out_specs=[pl.BlockSpec(memory_space=pltpu.VMEM)] * 7,
        out_shape=[
            matrix,
            matrix,
            matrix,
            matrix,
            jax.ShapeDtypeStruct((rows, width), bf16),
            jax.ShapeDtypeStruct((own, 4 * units), f32),
            jax.ShapeDtypeStruct((8, HEAD_DIM), f32),
        ],
        scratch_shapes=[
            pltpu.VMEM((total, width), bf16),
            pltpu.VMEM((total, wide), bf16),
            pltpu.VMEM((width, wide), bf16),
            pltpu.VMEM((rows, width), f32),
            pltpu.VMEM((4, size, wide), bf16),
            pltpu.VMEM((4, size, wide), bf16),
            pltpu.VMEM((4, size, wide), bf16),
            pltpu.VMEM((4, size, wide), bf16),
            pltpu.VMEM((8, own, width), bf16),
            pltpu.VMEM((4, own, width), bf16),
            pltpu.VMEM((4, own, width), bf16),
            pltpu.VMEM((4, own, width), bf16),
            pltpu.VMEM((3, rows, width), bf16),
            pltpu.VMEM((3, rows, width), bf16),
            pltpu.VMEM((size, wide), bf16),
            pltpu.VMEM((3, own, wide), bf16),
            pltpu.VMEM((4, own, units), bf16),
            pltpu.VMEM((8, 8, HEAD_DIM), f32),
            pltpu.VMEM((3, 8, 8, HEAD_DIM), f32),
            pltpu.VMEM((7, 8, HEAD_DIM), f32),
            dma((7,)),
            dma((5, 3)),
            dma((5, 3)),
            dma((2, 4)),
            dma((2, 4)),
            dma((2, 3)),
            dma((2, 4)),
            dma((7,)),
            dma((7,)),
        ],
        compiler_params=pltpu.CompilerParams(
            collective_id=1, has_side_effects=True, vmem_limit_bytes=60 * 2**20
        ),
        cost_estimate=pl.CostEstimate(
            flops=4 * total * width * wide, bytes_accessed=100 * 2**20, transcendentals=0
        ),
    )(tokens, grads, weights, output_part, hidden, up_shard, gain_part)


def front_kernel(
    tokens_hbm,
    query_hbm,
    key_hbm,
    value_hbm,
    output_hbm,
    gate_hbm,
    up_hbm,
    down_hbm,
    gains_hbm,
    cos_hbm,
    sin_hbm,
    bias_hbm,
    attn_out,
    gate_out,
    up_out,
    first_out,
    second_out,
    gate_pre_out,
    up_pre_out,
    activated_out,
    tokens_out,
    query_pre_out,
    key_pre_out,
    value_out,
    scales_out,
    query_out,
    key_out,
    context_out,
    lse_out,
    output_out,
    unit_out,
    unit_scale_out,
    hidden_out,
    hidden_all_out,
    gains_out,
    block,
    attn_mat,
    gate_block,
    up_block,
    down_block,
    tokens,
    query_pre,
    key_pre,
    value,
    query,
    key,
    context,
    lse,
    bias,
    cos_part,
    sin_part,
    scale_columns,
    output_in,
    output_mat,
    rows_send,
    rows_in,
    half_in,
    attn,
    unit_scale,
    hidden,
    hidden_all,
    squares,
    squares_in,
    scale_rows,
    gains_leaf,
    gains_all,
    gains,
    load_sem,
    save_sem,
    row_send_sem,
    row_recv_sem,
    leaf_send_sem,
    leaf_recv_sem,
    core_send_sem,
    core_recv_sem,
    line_send_sem,
    line_recv_sem,
):
    leaf, row = lax.axis_index("leaf"), lax.axis_index("row")
    z, core = leaf // 2, leaf % 2
    far, inner = z // 2, ((z + 1) // 2) % 2
    own, width = query_hbm.shape
    part, size = width // 4, 4 * own
    rows, wide = tokens_hbm.shape[0], 3 * part
    units = gate_block.shape[1]
    heads = part // HEAD_DIM
    scale = 1.0 / math.sqrt(HEAD_DIM)
    hops = (3, 1, 2)
    sent, saved = [], []

    def lines(index, count):
        return pl.ds(pl.multiple_of(index * count, count), count)

    def load(source, target, i):
        copy = pltpu.make_async_copy(source, target, load_sem.at[i])
        copy.start()
        return copy

    def save(source, target):
        copy = pltpu.make_async_copy(source, target, save_sem.at[len(saved)])
        copy.start()
        saved.append(copy)

    mine = lines(row, own)
    load_weights = [
        load(source, attn.at[pl.ds(i * own, own)], (0, 1, 15, 16)[i])
        for i, source in enumerate((query_hbm, key_hbm, value_hbm, output_hbm))
    ]
    load_gains = load(gains_hbm, gains_leaf.at[row], 2)
    load_gate = load(gate_hbm.at[:, lines(row, units)], gate_block.at[mine], 3)
    load_tokens = load(tokens_hbm, tokens.at[lines(row, rows)], 4)
    load_up = load(up_hbm.at[:, lines(row, units)], up_block.at[mine], 5)
    load_down = load(down_hbm.at[:, lines(row, units)], down_block.at[mine], 6)
    load_tables = [load(cos_hbm, cos_part, 7), load(sin_hbm, sin_part, 8), load(bias_hbm, bias, 9)]

    barrier = pltpu.get_barrier_semaphore()
    for hop in hops:
        pl.semaphore_signal(barrier, inc=1, device_id={"row": other(row, hop)}, device_id_type=MESH)
    for step in range(1, 8):
        pl.semaphore_signal(barrier, inc=1, device_id={"leaf": (leaf + step) % 8}, device_id_type=MESH)
    pl.semaphore_wait(barrier, 10)

    def row_copy(source, target, kind, hop):
        copy = pltpu.make_async_remote_copy(
            source,
            target,
            row_send_sem.at[kind, hop - 1],
            row_recv_sem.at[kind, hop - 1],
            device_id={"row": other(row, hop)},
            device_id_type=MESH,
        )
        copy.start()
        sent.append(copy)

    def row_landed(target, kind):
        for hop in hops:
            landed(target(other(row, hop), hop), row_recv_sem.at[kind, hop - 1])

    def leaf_copy(source, target, send_sem, recv_sem, to):
        return pltpu.make_async_remote_copy(
            source, target, send_sem, recv_sem, device_id={"leaf": to}, device_id_type=MESH
        )

    for copy in load_weights:
        copy.wait()
    for hop in hops:
        for i in range(3):
            some = attn[i * own : (i + 1) * own, lines(other(row, hop), part)]
            rows_send[hop - 1, :own, i * part : (i + 1) * part] = some.astype(bf16)
        row_copy(rows_send.at[hop - 1, pl.ds(0, own), pl.ds(0, wide)], block.at[mine, pl.ds(0, wide)], 0, hop)
    packs = sent[:]
    sent.clear()
    for i in range(3):
        block[mine, i * part : (i + 1) * part] = attn[i * own : (i + 1) * own, lines(row, part)].astype(bf16)
    for i in range(4):
        block[i * own : (i + 1) * own, wide:] = attn[3 * own :, i * part : (i + 1) * part].astype(bf16)
    for hop in hops:
        row_copy(gains_hbm, gains_leaf.at[row], 1, hop)
    for hop in hops:
        row_copy(gate_hbm.at[:, lines(other(row, hop), units)], gate_block.at[mine], 2, hop)
    for hop in hops:
        row_copy(tokens_hbm, tokens.at[lines(row, rows)], 3, hop)
    for hop in hops:
        row_copy(up_hbm.at[:, lines(other(row, hop), units)], up_block.at[mine], 4, hop)
    for hop in hops:
        row_copy(down_hbm.at[:, lines(other(row, hop), units)], down_block.at[mine], 5, hop)

    sizes = (size, size, size, size // 2, size // 2)

    def spread(kind, source, whole):
        place = whole.at[lines(leaf, sizes[kind])]
        across = leaf_copy(
            source, place, line_send_sem.at[kind, 2], line_recv_sem.at[kind, 2], 2 * other(z, 2) + core
        )
        across.start()
        sent.append(across)
        forth = leaf_copy(source, place, line_send_sem.at[kind, 0], line_recv_sem.at[kind, 0], 2 * z + 2 + core)
        back = leaf_copy(source, place, line_send_sem.at[kind, 1], line_recv_sem.at[kind, 1], 2 * z - 2 + core)

        @pl.when(z < 3)
        def _():
            forth.start()

        @pl.when(z > 0)
        def _():
            back.start()

        beside = leaf_copy(source, place, core_send_sem.at[kind, 3], core_recv_sem.at[kind, 3], 2 * z + 1 - core)
        beside.start()
        sent.append(beside)
        save(source, place)

        def done():
            @pl.when(z < 3)
            def _():
                forth.wait_send()

            @pl.when(z > 0)
            def _():
                back.wait_send()

        return done

    def arrival(step):
        inner_slot, inner_chip = ((2, other(z, 2)), (0, z - 1), (1, z + 1))[step]
        end_slot, end_chip = ((1 - far, 1 + far), (2, other(z, 2)), (3, 3 - z))[step]
        return end_slot + inner * (inner_slot - end_slot), end_chip + inner * (inner_chip - end_chip)

    def pass_on(kind, whole, step):
        slot, chip = arrival(step)
        place = whole.at[lines(2 * chip + core, sizes[kind])]
        landed(place, line_recv_sem.at[kind, slot])
        beside = leaf_copy(place, place, core_send_sem.at[kind, step], core_recv_sem.at[kind, step], 2 * z + 1 - core)
        beside.start()
        sent.append(beside)
        if step == 0:
            onward = leaf_copy(place, place, line_send_sem.at[kind, 3], line_recv_sem.at[kind, 3], 6 * far + core)

            @pl.when(inner == 1)
            def _():
                onward.start()

            def done():
                @pl.when(inner == 1)
                def _():
                    onward.wait_send()

            return done

    def gathered(kind, whole):
        landed(whole.at[lines(2 * z + 1 - core, sizes[kind])], core_recv_sem.at[kind, 3])
        for step in range(3):
            chip = arrival(step)[1]
            landed(whole.at[lines(2 * chip + 1 - core, sizes[kind])], core_recv_sem.at[kind, step])

    row_landed(lambda source, hop: block.at[lines(source, own), pl.ds(0, wide)], 0)
    done = [spread(0, block, attn_mat)]

    load_gains.wait()
    row_landed(lambda source, hop: gains_leaf.at[source], 1)
    for step in range(1, 8):
        copy = leaf_copy(
            gains_leaf, gains_all.at[leaf], leaf_send_sem.at[step - 1], leaf_recv_sem.at[step - 1], (leaf + step) % 8
        )
        copy.start()
        sent.append(copy)
    gains_all[leaf] = gains_leaf[...]

    load_gate.wait()
    row_landed(lambda source, hop: gate_block.at[lines(source, own)], 2)
    done.append(pass_on(0, attn_mat, 0))
    pass_on(0, attn_mat, 1)
    done.append(spread(1, gate_block, gate_out))
    pass_on(0, attn_mat, 2)
    gathered(0, attn_mat)
    saved[0].wait()

    load_tokens.wait()
    row_landed(lambda source, hop: tokens.at[lines(source, rows)], 3)

    def project_step(j, carry):
        at = lines(j, rows)
        some = tokens[at, :]
        for i, out in enumerate((query_pre, key_pre)):
            product = dot(some, attn_mat[:, i * part : (i + 1) * part], NN)
            out[at, :] = product
            square = jnp.sum(product * product, axis=1, keepdims=True)
            squares[i : i + 1, at] = jnp.broadcast_to(square, (rows, HEAD_DIM)).T[0:1]
        value[at, :] = dot(some, attn_mat[:, 2 * part : wide], NN, bf16)
        return carry

    squares[...] = jnp.zeros_like(squares)
    lax.fori_loop(0, 4, project_step, 0)
    for hop in hops:
        row_copy(squares, squares_in.at[hop - 1], 7, hop)
    for hop in hops:
        row_copy(
            attn_mat.at[lines(other(row, hop), 2 * size), pl.ds(wide, part)], output_in.at[row], 6, hop
        )
    swapped = len(sent)
    keep = load(attn_mat.at[lines(row, 2 * size), pl.ds(wide, part)], output_in.at[row], 10)
    load_up.wait()
    row_landed(lambda source, hop: up_block.at[lines(source, own)], 4)
    done.append(spread(2, up_block, up_out))
    save(attn_mat, attn_out)
    save(tokens, tokens_out)
    save(query_pre, query_pre_out)
    save(key_pre, key_pre_out)
    save(value, value_out)
    for step in range(1, 8):
        landed(gains_all.at[(leaf - step + 8) % 8], leaf_recv_sem.at[step - 1])
    for source in range(8):
        for pair in range(2):
            first = (2 * source + pair) * HEAD_DIM
            gains[:, first : first + HEAD_DIM] = gains_all[source, 2 * pair] + gains_all[source, 2 * pair + 1]
    save(gains, gains_out)
    for table in load_tables:
        table.wait()
    row_landed(lambda source, hop: squares_in.at[hop - 1], 7)
    scales = lax.rsqrt((squares[...] + squares_in[0] + squares_in[1] + squares_in[2]) / width + epsilon)
    scale_rows[...] = scales
    save(scale_rows, scales_out)
    for i in range(2):
        scale_columns[i] = jnp.broadcast_to(scales[i : i + 1], (HEAD_DIM, 4 * rows)).T

    def head_step(h, carry):
        at = lines(h, HEAD_DIM)
        at_gain = lines(row * heads + h, HEAD_DIM)
        for i, (pre, out) in enumerate(((query_pre, query), (key_pre, key))):
            scaled = pre[:, at] * scale_columns[i] * gains[i : i + 1, at_gain]
            out[:, at] = turn(scaled, cos_part[...], sin_part[...]).astype(bf16)
        for first in range(0, 4 * rows, rows):
            last = first + rows
            scores = dot(key[:last, at], query[first:last, at], NT) * scale
            scores = scores + bias[:last, first:last].astype(f32)
            top = jnp.max(scores, axis=0, keepdims=True)
            probs = jnp.exp(scores - top)
            mass = jnp.sum(probs, axis=0, keepdims=True)
            probs_low = (probs * (1.0 / mass)).astype(bf16)
            turned = dot(value[:last, at], probs_low, TN)
            context[first:last, at] = turned.T.astype(bf16)
            lse[lines(h, 8), first:last] = jnp.broadcast_to(top + jnp.log(mass), (8, rows))
        return carry

    lax.fori_loop(0, heads, head_step, 0)
    done.append(pass_on(1, gate_out, 0))
    save(query, query_out)
    save(key, key_out)
    save(context, context_out)
    save(lse, lse_out)

    keep.wait()
    row_landed(lambda source, hop: output_in.at[source], 6)
    for i in range(2):
        for source in range(4):
            for j in range(4):
                output_mat[i * size + source * own : i * size + (source + 1) * own, j * part : (j + 1) * part] = (
                    output_in[source, i * size + j * own : i * size + (j + 1) * own, :]
                )
    save(output_mat, output_out)

    def output_part(hop, store):
        some = context[lines(other(row, hop), rows), :]
        for j in range(4):
            columns = slice(j * part, (j + 1) * part)
            store(columns, dot(some, output_mat[:, columns], NN))

    for copy in packs:
        copy.wait_send()
    half = rows // 2
    top, bottom = pl.ds(0, half), pl.ds(half, half)
    for hop in hops:

        def store(columns, values):
            rows_send[hop - 1, :, columns] = values.astype(bf16)

        output_part(hop, store)
        if hop == 3:
            row_copy(rows_send.at[2, top], half_in.at[0], 8, 1)
            row_copy(rows_send.at[2, bottom], half_in.at[1], 8, 2)
        else:
            early = (top, bottom)[hop - 1]
            row_copy(rows_send.at[hop - 1, early], rows_in.at[hop - 1, early], 10, hop)
    for hop in (1, 2):
        late = (bottom, top)[hop - 1]
        landed(half_in.at[2 - hop], row_recv_sem.at[8, 2 - hop])
        rows_send[hop - 1, late] = (rows_send[hop - 1, late].astype(f32) + half_in[2 - hop].astype(f32)).astype(bf16)
        row_copy(rows_send.at[hop - 1, late], rows_in.at[hop - 1, late], 11, hop)

    def own_store(columns, values):
        attn[:, columns] = values

    output_part(0, own_store)

    pass_on(1, gate_out, 1)
    done.append(pass_on(2, up_out, 0))
    for hop in (1, 2):
        early, late = ((top, bottom), (bottom, top))[hop - 1]
        landed(rows_in.at[hop - 1, early], row_recv_sem.at[10, hop - 1])
        landed(rows_in.at[hop - 1, late], row_recv_sem.at[11, hop - 1])
        attn[...] += rows_in[hop - 1].astype(f32)
    mean = jnp.sum(attn[...] * attn[...], axis=1, keepdims=True) / width
    factor = lax.rsqrt(mean + epsilon)
    unit_scale[...] = jnp.broadcast_to(factor, unit_scale.shape)
    attn[...] = attn[...] * factor
    hidden[...] = tokens[lines(row, rows), :].astype(f32) + attn[...] * gains[2:3, :]
    hidden_all[lines(row, rows), :] = hidden[...].astype(bf16)
    for hop in (1, 2):
        place = hidden_all.at[lines(row, rows)]
        row_copy(place, place, 9, hop)
    save(attn, unit_out)
    save(unit_scale, unit_scale_out)
    save(hidden, hidden_out)
    for hop in (1, 2):
        landed(hidden_all.at[lines(other(row, hop), rows)], row_recv_sem.at[9, hop - 1])
        place = hidden_all.at[lines(2 * other(row, hop) + hop - 1, half)]
        row_copy(place, place, 12, 3 - hop)
    for hop in (1, 2):
        landed(hidden_all.at[lines(2 * other(row, 3) + 2 - hop, half)], row_recv_sem.at[12, hop - 1])
    save(hidden_all, hidden_all_out)
    pass_on(1, gate_out, 2)
    pass_on(2, up_out, 1)
    load_down.wait()
    row_landed(lambda source, hop: down_block.at[lines(source, own)], 5)
    downs = (first_out, second_out)
    for h in range(2):
        done.append(spread(3 + h, down_block.at[pl.ds(h * size // 2, size // 2)], downs[h]))
    pass_on(2, up_out, 2)
    gathered(1, gate_out)
    gathered(2, up_out)

    for copy in sent[:swapped]:
        copy.wait_send()
    for finish_sends in done[:2]:
        finish_sends()
    for copy in saved[1:]:
        copy.wait()
    saved.clear()

    def quarter(j):
        columns = pl.ds(j * part, part)
        return [
            load(source.at[:, columns], attn_mat.at[:, pl.ds((2 * i + j % 2) * part, part)], 11 + 2 * i + j % 2)
            for i, source in enumerate((gate_out, up_out))
        ]

    coming = quarter(0)
    for j in range(4):
        for copy in coming:
            copy.wait()
        if j < 3:
            coming = quarter(j + 1)
        for copy in saved:
            copy.wait()
        saved.clear()

        slot = j % 2

        def units_step(i, carry):
            at = lines(i, rows)
            some = hidden_all[at, :]
            gate = dot(some, attn_mat[:, slot * part : (slot + 1) * part], NN)
            up = dot(some, attn_mat[:, (2 + slot) * part : (3 + slot) * part], NN)
            query_pre[at, :] = gate
            key_pre[at, :] = up
            value[at, :] = (gate * jax.nn.sigmoid(gate) * up).astype(bf16)
            return carry

        lax.fori_loop(0, 4, units_step, 0)
        columns = pl.ds(j * part, part)
        save(query_pre, gate_pre_out.at[:, columns])
        save(key_pre, up_pre_out.at[:, columns])
        save(value, activated_out.at[:, columns])
        if j == 1:
            done.append(pass_on(3, first_out, 0))
        if j == 2:
            done.append(pass_on(4, second_out, 0))
            pass_on(3, first_out, 1)
    pass_on(3, first_out, 2)
    pass_on(4, second_out, 1)
    pass_on(4, second_out, 2)
    gathered(3, first_out)
    gathered(4, second_out)

    for finish_sends in done[2:]:
        finish_sends()
    for copy in sent[swapped:]:
        copy.wait_send()
    for copy in saved:
        copy.wait()


def front(tokens, weights, gate, up, down, gain_tile, cos_wide, sin_wide, bias):
    rows, width = tokens.shape
    total, part, own = 4 * rows, width // 4, gate.shape[0]
    wide, units, size = 3 * part, gate.shape[1] // 4, 4 * own
    heads = part // HEAD_DIM
    shape = jax.ShapeDtypeStruct
    outs = [
        shape((width, width), bf16),
        shape((width, units), bf16),
        shape((width, units), bf16),
        shape((width // 2, units), bf16),
        shape((width // 2, units), bf16),
        shape((total, units), f32),
        shape((total, units), f32),
        shape((total, units), bf16),
        shape((total, width), bf16),
        shape((total, part), f32),
        shape((total, part), f32),
        shape((total, part), bf16),
        shape((8, total), f32),
        shape((total, part), bf16),
        shape((total, part), bf16),
        shape((total, part), bf16),
        shape((8 * heads, total), f32),
        shape((part, width), bf16),
        shape((rows, width), f32),
        shape((rows, HEAD_DIM), f32),
        shape((rows, width), f32),
        shape((total, width), bf16),
        shape((8, width), f32),
    ]
    vmem, dma = pltpu.VMEM, pltpu.SemaphoreType.DMA
    return pl.pallas_call(
        front_kernel,
        in_specs=[pl.BlockSpec(memory_space=pl.ANY)] * 12,
        out_specs=[pl.BlockSpec(memory_space=pl.ANY)] * len(outs),
        out_shape=outs,
        scratch_shapes=[
            vmem((size, width), bf16),
            vmem((width, width), bf16),
            vmem((size, units), bf16),
            vmem((size, units), bf16),
            vmem((size, units), bf16),
            vmem((total, width), bf16),
            vmem((total, part), f32),
            vmem((total, part), f32),
            vmem((total, part), bf16),
            vmem((total, part), bf16),
            vmem((total, part), bf16),
            vmem((total, part), bf16),
            vmem((8 * heads, total), f32),
            vmem((total, total), bf16),
            vmem((total, HEAD_DIM), f32),
            vmem((total, HEAD_DIM), f32),
            vmem((2, total, HEAD_DIM), f32),
            vmem((4, part, part), bf16),
            vmem((part, width), bf16),
            vmem((3, rows, width), bf16),
            vmem((2, rows, width), bf16),
            vmem((2, rows // 2, width), bf16),
            vmem((rows, width), f32),
            vmem((rows, HEAD_DIM), f32),
            vmem((rows, width), f32),
            vmem((total, width), bf16),
            vmem((8, total), f32),
            vmem((3, 8, total), f32),
            vmem((8, total), f32),
            vmem((4, 8, HEAD_DIM), f32),
            vmem((8, 4, 8, HEAD_DIM), f32),
            vmem((8, width), f32),
            dma((17,)),
            dma((32,)),
            dma((13, 3)),
            dma((13, 3)),
            dma((7,)),
            dma((7,)),
            dma((5, 4)),
            dma((5, 4)),
            dma((5, 4)),
            dma((5, 4)),
        ],
        compiler_params=pltpu.CompilerParams(
            collective_id=2, has_side_effects=True, vmem_limit_bytes=62 * 2**20
        ),
        cost_estimate=pl.CostEstimate(
            flops=10 * total * width * part, bytes_accessed=100 * 2**20, transcendentals=0
        ),
    )(tokens, *weights, gate, up, down, gain_tile, cos_wide, sin_wide, bias)


def body(
    inputs,
    cotangent,
    seg_lengths,
    seg_parents,
    w_query,
    w_key,
    w_value,
    w_output,
    gain_query,
    gain_key,
    gain_attn,
    w_gate,
    w_up,
    w_down,
    gain_mlp,
):
    trees, rows_dev, width = inputs.shape
    count, leaves, me = lax.axis_size("row"), lax.axis_size("leaf"), lax.axis_index("row")
    tree_len = rows_dev * count
    part = width // count
    own = w_query.shape[0]
    group = count * own // 2
    units = w_gate.shape[1] // count
    tokens = inputs.reshape(rows_dev, width)

    def leaf_gather(block):
        return lax.all_gather(block, "leaf", axis=0, tiled=True)

    def leaf_scatter(block):
        return lax.psum_scatter(block, "leaf", scatter_dimension=0, tiled=True)

    bias, cos_wide, sin_wide = tree_tables(seg_lengths[0], seg_parents[0], tree_len)
    fast = leaves == 8 and count == 4
    if fast:
        gain_own = jnp.stack([gain_query, gain_key, gain_attn, gain_mlp]).astype(bf16).astype(f32)
        gain_tile = lax.dynamic_update_slice(jnp.zeros((8, HEAD_DIM), f32), gain_own, (0, (me % 2) * own))
        (
            attn_mat,
            gate_mat,
            up_mat,
            down_first,
            down_second,
            gate_pre,
            up_pre,
            activated,
            all_tokens,
            query_pre,
            key_pre,
            value,
            scales,
            query,
            key,
            context,
            lse,
            output_mat,
            attn_unit,
            attn_scale,
            hidden,
            hidden_all,
            gains_all,
        ) = front(
            tokens,
            (w_query, w_key, w_value, w_output),
            w_gate.astype(bf16),
            w_up.astype(bf16),
            w_down.astype(bf16),
            gain_tile,
            cos_wide,
            sin_wide,
            bias,
        )
        scales, attn_scale = scales[:2], attn_scale[:, :1]
        down_halves = [down_first, down_second]
        query_scale, key_scale = scales[0][:, None], scales[1][:, None]
        attn_gain, mlp_gain = gains_all[2], gains_all[3]
        head_gains = lax.dynamic_slice_in_dim(gains_all[:2], me * part, part, 1)
    else:
        qkv_block = columns_in(w_query, w_key, w_value)
        gains_own = jnp.stack([gain_query, gain_key, gain_attn, gain_mlp]).astype(bf16).reshape(1, 4 * own)
        gains_leaf = gather_rows(gains_own).reshape(count * own, 4)
        attn_block = jnp.concatenate(
            [
                qkv_block,
                w_output.astype(bf16).reshape(count * own, part),
                jnp.pad(gains_leaf, ((0, 0), (0, HEAD_DIM - 4))),
            ],
            axis=1,
        )
        attn_mat = leaf_gather(attn_block)
        qkv_mat = attn_mat[:, : 3 * part]
        output_rows = attn_mat[:, 3 * part : 4 * part].reshape(count, leaves // count, own, width)
        gains_all = attn_mat[:, 4 * part : 4 * part + 4].reshape(leaves, count, 4, own)
        gains_all = jnp.moveaxis(gains_all, 2, 0).reshape(4, width).astype(f32)
        gate_block = columns_in(tie(w_gate, qkv_block))
        up_block = columns_in(tie(w_up, qkv_block))
        down_block = columns_in(tie(w_down, qkv_block))
        all_tokens = gather_rows(tie(tokens, gate_block, up_block, down_block))

        query_pre, key_pre, value, squares = project(all_tokens, attn_mat, part)
        gate_mat = leaf_gather(gate_block)
        up_mat = leaf_gather(up_block)
        down_halves = [leaf_gather(down_block[h * group : (h + 1) * group]) for h in range(2)]

        squares = sum_rows(squares)
        scales = lax.rsqrt(squares / width + epsilon)
        query_scale, key_scale = scales[0][:, None], scales[1][:, None]
        attn_gain, mlp_gain = gains_all[2], gains_all[3]
        head_gains = lax.dynamic_slice_in_dim(gains_all[:2], me * part, part, 1)
        output_rows = tie(output_rows, scales)
        output_mat = jnp.zeros((leaves // count, count, own, width), bf16)
        for hop in range(count):
            piece = lax.dynamic_index_in_dim(output_rows, me ^ hop, 0, keepdims=False)
            if hop:
                piece = swap(piece, hop)
            output_mat = lax.dynamic_update_index_in_dim(output_mat, piece, me ^ hop, 1)
        output_mat = output_mat.reshape(part, width)
        query, key, context, lse = attend(
            query_pre, key_pre, value, scales.T, head_gains, cos_wide, sin_wide, bias
        )
        attn_pre = dot_scatter([context], [output_mat], NN)
        attn_scale = lax.rsqrt(jnp.mean(attn_pre * attn_pre, axis=-1, keepdims=True) + epsilon)
        attn_unit = attn_pre * attn_scale
        hidden = tokens.astype(f32) + attn_unit * attn_gain
        hidden_all = gather_rows(hidden.astype(bf16))

    if not fast:
        gate_pre = dot(hidden_all, gate_mat, NN)
        up_pre = dot(hidden_all, up_mat, NN)
        activated = (gate_pre * jax.nn.sigmoid(gate_pre) * up_pre).astype(bf16)
    sigmoid_gate = jax.nn.sigmoid(gate_pre)
    mlp_halves = [dot_scatter([activated], [down_halves[h]], NT) for h in range(2)]
    grad_final = cotangent.reshape(rows_dev, width).astype(f32)
    halves = range(2)

    def split(rows):
        rows = rows.reshape(rows.shape[:-1] + (leaves, 2, group))
        return [rows[..., h, :].reshape(rows.shape[:-3] + (width // 2,)) for h in halves]

    weighted = tie(split(grad_final * mlp_gain), hidden_all)
    square = sum(jnp.sum(m * m, axis=-1, keepdims=True) for m in mlp_halves) / width
    cross = sum(jnp.sum(m * w, axis=-1, keepdims=True) for m, w in zip(mlp_halves, weighted)) / width
    mlp_scale = lax.rsqrt(square + epsilon)
    grad_mlp = [
        (mlp_scale * (w - m * (mlp_scale * mlp_scale * cross))).astype(bf16) for m, w in zip(mlp_halves, weighted)
    ]
    grad_mlp_halves = [gather_rows(grad_mlp[h]) for h in halves]
    down_sums = [dot(grad_mlp_halves[h], activated, TN, bf16) for h in range(2)]
    down_shards = [leaf_scatter(down_sums[h]) for h in range(2)]
    grad_act = dot(tie(grad_mlp_halves[0], down_sums[0]), down_halves[0], NN)
    grad_act = grad_act + dot(tie(grad_mlp_halves[1], down_sums[1]), down_halves[1], NN)
    grad_gate = (grad_act * up_pre * sigmoid_gate * (1.0 + gate_pre * (1.0 - sigmoid_gate))).astype(bf16)
    grad_up = (grad_act * gate_pre * sigmoid_gate).astype(bf16)
    wide = width // 2
    gate_sum = dot(hidden_all, grad_gate, TN, bf16)
    parts, coming = [], []
    for h in range(2):
        one = tie(grad_gate, gate_sum, *parts), tie(grad_up, gate_sum, *parts)
        part_h = sum(
            dot(left, right[h * wide : (h + 1) * wide], NT) for left, right in zip(one, (gate_mat, up_mat))
        ).astype(bf16)
        parts.append(part_h)
        coming.append(send_rows(part_h))
    grad_hidden = grad_final + jnp.concatenate(
        [add_rows(part_h, pieces) for part_h, pieces in zip(parts, coming)], axis=1
    )
    gate_sum = tie(gate_sum, *down_sums)
    gate_shard = leaf_scatter(gate_sum)

    grad_attn, grad_attn_gain = norm_back(grad_hidden, attn_unit, attn_scale, attn_gain)
    grad_attn_low = grad_attn.astype(bf16)
    up_sum = dot(hidden_all, tie(grad_up, grad_attn_low), TN, bf16)
    grad_attn_all = gather_rows(tie(grad_attn_low, *down_shards), up_sum)
    grad_context = dot(grad_attn_all, output_mat, NT, bf16)
    up_shard = leaf_scatter(tie(up_sum, gate_sum))
    grad_context = tie(grad_context, gate_shard)
    grad_query, grad_key, grad_value, inner_query, inner_key, grad_head_gains = attend_back(
        query, key, value, bias, lse, grad_context, query_pre, key_pre, scales.T, head_gains, cos_wide, sin_wide
    )
    inner = sum_rows(jnp.stack([jnp.sum(inner_query, axis=1), jnp.sum(inner_key, axis=1)])) / width
    output_part = dot(context, tie(grad_attn_all, inner), TN, bf16).reshape(leaves // count, count, own, width)
    grad_query_low = (
        query_scale * (grad_query * head_gains[0] - query_pre * (query_scale * inner[0][:, None]))
    ).astype(bf16)
    grad_key_low = (
        key_scale * (grad_key * head_gains[1] - key_pre * (key_scale * inner[1][:, None]))
    ).astype(bf16)
    grad_qkv = jnp.concatenate([grad_query_low, grad_key_low, grad_value], axis=1)
    gate_out = columns_out(tie(gate_shard, inner_query))
    down_out = columns_out(tie(jnp.concatenate(down_shards), inner_query))
    mlp_halves = tie(mlp_halves, inner_query)
    mlp_unit = jnp.stack([m.reshape(rows_dev, leaves, group) for m in mlp_halves], axis=2).reshape(rows_dev, width)
    mlp_unit = mlp_unit * mlp_scale
    outputs = (hidden + mlp_unit * mlp_gain).astype(bf16).reshape(inputs.shape)
    grad_mlp_gain = jnp.sum(grad_final * mlp_unit, axis=0)

    wide_part = jnp.stack([tie(grad_attn_gain, inner), grad_mlp_gain]).reshape(2, leaves, count, own)
    narrow_part = grad_head_gains.reshape(2, leaves // count, count, own)
    grad_qkv = tie(grad_qkv, gate_out, down_out, outputs)
    if fast:
        gain_part = jnp.zeros((count, leaves, 8, HEAD_DIM), f32)
        gain_part = lax.dynamic_update_slice(
            gain_part, jnp.transpose(narrow_part, (2, 1, 0, 3)), (0, me * (leaves // count), 0, 0)
        )
        gain_part = lax.dynamic_update_slice(gain_part, jnp.transpose(wide_part, (2, 1, 0, 3)), (0, 0, 2, 0))
        *grad_mats, grad_output, grad_tokens, up_out, grad_gains = finish(
            all_tokens, grad_qkv, attn_mat, output_part, grad_hidden, up_shard, gain_part
        )
        grad_inputs, up_out, grad_gains = grad_tokens.reshape(inputs.shape), [up_out], grad_gains[:4, :own]
    else:
        wide_sum = jnp.zeros((2, leaves, own), f32)
        narrow_all = jnp.zeros((2, leaves, own), f32)
        for hop in range(count):
            piece = lax.dynamic_index_in_dim(jnp.concatenate([wide_part, narrow_part], axis=1), me ^ hop, 2, keepdims=False)
            if hop:
                piece = swap(piece, hop)
            wide_sum = wide_sum + piece[:, :leaves]
            narrow_all = lax.dynamic_update_slice_in_dim(
                narrow_all, piece[:, leaves:], (me ^ hop) * (leaves // count), 1
            )
        grad_gains = jnp.concatenate([narrow_all, wide_sum], axis=0)
        stride = 1
        while stride < leaves:
            grad_gains = grad_gains + lax.ppermute(
                grad_gains, "leaf", [(i, i ^ stride) for i in range(leaves)]
            )
            stride *= 2
        grad_gains = lax.dynamic_index_in_dim(grad_gains, lax.axis_index("leaf"), 1, keepdims=False)
        output_turned = jnp.zeros((count, leaves // count, own, width), bf16)
        for hop in range(count):
            piece = lax.dynamic_index_in_dim(output_part, me ^ hop, 1, keepdims=False)
            if hop:
                piece = swap(piece, hop)
            output_turned = lax.dynamic_update_index_in_dim(output_turned, piece, me ^ hop, 0)
        attn_sum = sums_beside(all_tokens, grad_qkv, output_turned.reshape(leaves * count * own, part))
        grad_tokens = grad_hidden + dot_scatter([grad_qkv], [qkv_mat], NT)
        grad_inputs = grad_tokens.astype(bf16).reshape(inputs.shape)
        attn_shard = leaf_scatter(tie(attn_sum, up_shard))
        up_out = columns_out(up_shard)
        grad_mats = columns_out(attn_shard[:, : 3 * part], 3)
        grad_output = attn_shard[:, 3 * part :].reshape(own, width).astype(f32)
    return (
        outputs,
        grad_inputs,
        *grad_mats,
        grad_output,
        grad_gains[0],
        grad_gains[1],
        grad_gains[2],
        *gate_out,
        *up_out,
        *down_out,
        grad_gains[3],
    )


def solution(mesh):
    both = ("leaf", "row")
    token_spec, tree_spec, matrix_spec, gain_spec = P("leaf", "row", None), P("leaf", None), P(both, None), P(both)
    return jax.shard_map(
        body,
        mesh=mesh,
        in_specs=(token_spec,) * 2 + (tree_spec,) * 2 + (matrix_spec,) * 4 + (gain_spec,) * 3 + (matrix_spec,) * 3 + (gain_spec,),
        out_specs=(token_spec,) * 2 + (matrix_spec,) * 4 + (gain_spec,) * 3 + (matrix_spec,) * 3 + (gain_spec,),
        check_vma=False,
    )
```

```python
import functools
import math

import jax
import jax.numpy as jnp
from jax import lax
from jax.experimental import pallas as pl
from jax.experimental.pallas import tpu as pltpu
from jax.sharding import PartitionSpec as P

HEAD_DIM = 128
MESH = pl.DeviceIdType.MESH

epsilon = 1e-06
rope_theta = 500000.0
masked_fill = -1e30
bf16 = jnp.bfloat16
f32 = jnp.float32
NN = (((1,), (0,)), ((), ()))
NT = (((1,), (1,)), ((), ()))
TN = (((0,), (0,)), ((), ()))


def dot(left, right, dims, kind=f32):
    return lax.dot_general(left, right, dims, preferred_element_type=f32).astype(kind)


def swap(piece, hop):
    count = lax.axis_size("row")
    return lax.ppermute(piece, "row", [(i, i ^ hop) for i in range(count)])


def gather_rows(rows, *meanwhile):
    count, me = lax.axis_size("row"), lax.axis_index("row")
    size = rows.shape[0]
    whole = jnp.zeros((count * size,) + rows.shape[1:], rows.dtype)
    for hop in range(1, count):
        whole = lax.dynamic_update_slice_in_dim(whole, swap(rows, hop), (me ^ hop) * size, 0)
    return lax.dynamic_update_slice_in_dim(whole, tie(rows, *meanwhile), me * size, 0)


def dot_scatter(lefts, rights, dims, *meanwhile):
    count, me = lax.axis_size("row"), lax.axis_index("row")
    size = lefts[0].shape[0] // count

    def rows_of(hop, lefts):
        parts = [lax.dynamic_slice_in_dim(left, (me ^ hop) * size, size, 0) for left in lefts]
        return sum(dot(part, right, dims) for part, right in zip(parts, rights))

    coming = [swap(rows_of(hop, lefts).astype(bf16), hop) for hop in reversed(range(1, count))]
    total = rows_of(0, [tie(left, *meanwhile) for left in lefts])
    for piece in coming:
        total = total + piece.astype(f32)
    return total


def send_rows(partial):
    count, me = lax.axis_size("row"), lax.axis_index("row")
    size = partial.shape[0] // count
    return [
        swap(lax.dynamic_slice_in_dim(partial, (me ^ hop) * size, size, 0), hop) for hop in reversed(range(1, count))
    ]


def add_rows(partial, coming, *meanwhile):
    size = partial.shape[0] // lax.axis_size("row")
    mine = lax.dynamic_slice_in_dim(tie(partial, *meanwhile), lax.axis_index("row") * size, size, 0)
    return sum([piece.astype(f32) for piece in coming], mine.astype(f32))


def tie(value, *others):
    return lax.optimization_barrier((value,) + others)[0]


def columns_in(*weights):
    count, me = lax.axis_size("row"), lax.axis_index("row")
    size, wide = weights[0].shape[0], weights[0].shape[1] // count
    whole = jnp.zeros((count * size, wide * len(weights)), bf16)
    for hop in range(count):
        piece = jnp.concatenate(
            [lax.dynamic_slice_in_dim(w, (me ^ hop) * wide, wide, 1).astype(bf16) for w in weights], axis=1
        )
        if hop:
            piece = swap(piece, hop)
        whole = lax.dynamic_update_slice_in_dim(whole, piece, (me ^ hop) * size, 0)
    return whole


def columns_out(block, many=1):
    count, me = lax.axis_size("row"), lax.axis_index("row")
    size, wide = block.shape[0] // count, block.shape[1] // many
    whole = [jnp.zeros((size, wide * count), f32)] * many
    for hop in range(count):
        piece = lax.dynamic_slice_in_dim(block, (me ^ hop) * size, size, 0)
        if hop:
            piece = swap(piece, hop)
        for i in range(many):
            own = piece[:, i * wide : (i + 1) * wide].astype(f32)
            whole[i] = lax.dynamic_update_slice_in_dim(whole[i], own, (me ^ hop) * wide, 1)
    return whole


def sum_rows(small):
    count = lax.axis_size("row")
    total = small
    for hop in range(1, count):
        total = total + swap(small, hop)
    return total


def norm_back(grad_out, unit_rows, scaled, gain_row):
    weighted = grad_out * gain_row
    inner = jnp.mean(weighted * unit_rows, axis=-1, keepdims=True)
    return (scaled * (weighted - unit_rows * inner), jnp.sum(grad_out * unit_rows, axis=0))


def tree_tables(length_row, parent_row, total):
    seg_count = parent_row.shape[0]
    segment_ids = jnp.arange(seg_count, dtype=jnp.int32)
    ends = jnp.cumsum(length_row)
    offsets = ends - length_row
    all_rows = jnp.arange(total, dtype=jnp.int32)
    owned_from = (all_rows[:, None] >= offsets[None, :]).astype(f32)
    onehot_all = owned_from - jnp.concatenate(
        [owned_from[:, 1:], jnp.zeros((total, 1), f32)], axis=1
    )
    parents = jnp.sum(onehot_all * parent_row.astype(f32)[None, :], axis=1)
    segments = jnp.sum(onehot_all * segment_ids.astype(f32)[None, :], axis=1)
    lengths = length_row.astype(f32)
    parent_lengths = jnp.sum((parent_row[:, None] == segment_ids[None, :]) * lengths[None, :], axis=1)
    above = jnp.where(segment_ids > 0, lengths[0], 0.0) + jnp.where(parent_row > 0, parent_lengths, 0.0)
    position = all_rows.astype(f32) + jnp.sum(onehot_all * (above - offsets.astype(f32))[None, :], axis=1)
    on_path = (segments[:, None] == segments[None, :]) | (segments[:, None] == parents[None, :]) | (segments[:, None] == 0.0)
    allowed = on_path & (all_rows[:, None] <= all_rows[None, :])
    bias = jnp.where(allowed, 0.0, masked_fill).astype(bf16)
    frequency = jnp.exp(
        jnp.arange(HEAD_DIM // 2, dtype=f32) * (-2.0 * math.log(rope_theta) / HEAD_DIM)
    )
    angles = position[:, None] * frequency[None, :]
    cos_half, sin_half = jnp.cos(angles), jnp.sin(angles)
    cos_wide = jnp.concatenate([cos_half, cos_half], axis=1)
    sin_wide = jnp.concatenate([-sin_half, sin_half], axis=1)
    return (bias, cos_wide, sin_wide)


def turn(vector, cos_part, sin_part):
    return vector * cos_part + pltpu.roll(vector, HEAD_DIM // 2, 1) * sin_part


def project_kernel(tokens_ref, weights_ref, query_ref, key_ref, value_ref, squares_ref):
    part = query_ref.shape[1]
    tokens = tokens_ref[...]
    for i, out_ref in enumerate((query_ref, key_ref)):
        product = dot(tokens, weights_ref[:, i * part : (i + 1) * part], NN)
        out_ref[...] = product
        square = jnp.sum(product * product, axis=1, keepdims=True)
        squares_ref[i : i + 1, :] = jnp.broadcast_to(square, (square.shape[0], HEAD_DIM)).T[0:1]
    value_ref[...] = dot(tokens, weights_ref[:, 2 * part :], NN, bf16)


def project(tokens, weights, part):
    total, width = tokens.shape
    size = 256
    rows = pl.BlockSpec((size, part), lambda i: (i, 0))
    wide = jax.ShapeDtypeStruct((total, part), f32)
    return pl.pallas_call(
        project_kernel,
        grid=(total // size,),
        in_specs=[
            pl.BlockSpec((size, width), lambda i: (i, 0)),
            pl.BlockSpec((width, 3 * part), lambda i: (0, 0)),
        ],
        out_specs=[rows, rows, rows, pl.BlockSpec((2, size), lambda i: (0, i))],
        out_shape=[
            wide,
            wide,
            jax.ShapeDtypeStruct((total, part), bf16),
            jax.ShapeDtypeStruct((2, total), f32),
        ],
        compiler_params=pltpu.CompilerParams(vmem_limit_bytes=48 * 2**20),
        cost_estimate=pl.CostEstimate(
            flops=6 * total * width * part, bytes_accessed=2 * width * (total + 3 * part) + 10 * total * part, transcendentals=0
        ),
    )(tokens, weights)


def attend_kernel(
    block,
    scale,
    query_pre_ref,
    key_pre_ref,
    value_ref,
    scales_ref,
    gains_ref,
    cos_ref,
    sin_ref,
    bias_ref,
    query_ref,
    key_ref,
    context_ref,
    lse_ref,
):
    total = key_ref.shape[0]
    cos_part, sin_part = cos_ref[...], sin_ref[...]
    query_ref[...] = turn(query_pre_ref[...] * scales_ref[:, 0:1] * gains_ref[0:1], cos_part, sin_part).astype(bf16)
    key_ref[...] = turn(key_pre_ref[...] * scales_ref[:, 1:2] * gains_ref[1:2], cos_part, sin_part).astype(bf16)
    for first in range(0, total, block):
        last = first + block
        scores = dot(key_ref[:last], query_ref[first:last], NT) * scale
        scores = scores + bias_ref[:last, first:last].astype(f32)
        top = jnp.max(scores, axis=0, keepdims=True)
        probs = jnp.exp(scores - top)
        mass = jnp.sum(probs, axis=0, keepdims=True)
        probs_low = (probs * (1.0 / mass)).astype(bf16)
        turned = dot(value_ref[:last], probs_low, TN)
        context_ref[first:last, :] = turned.T.astype(bf16)
        lse_ref[:, first:last] = jnp.broadcast_to(top + jnp.log(mass), (8, block))


def head_specs(total):
    part = pl.BlockSpec((total, HEAD_DIM), lambda h: (0, h))
    whole = pl.BlockSpec((total, HEAD_DIM), lambda h: (0, 0))
    gains = pl.BlockSpec((2, HEAD_DIM), lambda h: (0, h))
    scales = pl.BlockSpec((total, 2), lambda h: (0, 0))
    bias = pl.BlockSpec((total, total), lambda h: (0, 0))
    lse = pl.BlockSpec((8, total), lambda h: (h, 0))
    return part, whole, gains, scales, bias, lse


def attend(query_pre, key_pre, value, scales, gains, cos_wide, sin_wide, bias):
    total, width = query_pre.shape
    heads = width // HEAD_DIM
    part, whole, gain, scale, square, lse = head_specs(total)
    low = jax.ShapeDtypeStruct((total, width), bf16)
    return pl.pallas_call(
        functools.partial(attend_kernel, 256, 1.0 / math.sqrt(HEAD_DIM)),
        grid=(heads,),
        in_specs=[part, part, part, scale, gain, whole, whole, square],
        out_specs=[part, part, part, lse],
        out_shape=[low, low, low, jax.ShapeDtypeStruct((8 * heads, total), f32)],
        compiler_params=pltpu.CompilerParams(vmem_limit_bytes=56 * 2**20),
        cost_estimate=pl.CostEstimate(
            flops=4 * total * total * width, bytes_accessed=16 * total * width, transcendentals=total * total * heads
        ),
    )(query_pre, key_pre, value, scales, gains, cos_wide, sin_wide, bias)


def attend_back_kernel(
    block,
    scale,
    query_ref,
    key_ref,
    value_ref,
    bias_ref,
    lse_ref,
    grad_ref,
    query_pre_ref,
    key_pre_ref,
    scales_ref,
    gains_ref,
    cos_ref,
    sin_ref,
    grad_query_ref,
    grad_key_ref,
    grad_value_ref,
    inner_query_ref,
    inner_key_ref,
    grad_gains_ref,
    key_sum,
    value_sum,
):
    total = key_ref.shape[0]

    @pl.when(pl.program_id(0) == 0)
    def _():
        inner_query_ref[...] = jnp.zeros_like(inner_query_ref)
        inner_key_ref[...] = jnp.zeros_like(inner_key_ref)

    key_sum[...] = jnp.zeros_like(key_sum)
    value_sum[...] = jnp.zeros_like(value_sum)
    for first in range(0, total, block):
        last = first + block
        scores = dot(key_ref[:last], query_ref[first:last], NT) * scale
        scores = scores + bias_ref[:last, first:last].astype(f32)
        probs = jnp.exp(scores - lse_ref[0:1, first:last])
        grad_probs = dot(value_ref[:last], grad_ref[first:last], NT)
        inner = jnp.sum(probs * grad_probs, axis=0, keepdims=True)
        grad_scores = (probs * (grad_probs - inner)).astype(bf16)
        turned = dot(key_ref[:last], grad_scores, TN)
        grad_query_ref[first:last, :] = turned.T
        key_sum[:last, :] += dot(grad_scores, query_ref[first:last], NN)
        value_sum[:last, :] += dot(probs.astype(bf16), grad_ref[first:last], NN)
    grad_value_ref[...] = value_sum[...].astype(bf16)
    cos_part, sin_part = cos_ref[...], -sin_ref[...]
    for row, (grad, out_ref, pre_ref, inner_ref) in enumerate(
        (
            (grad_query_ref[...], grad_query_ref, query_pre_ref, inner_query_ref),
            (key_sum[...], grad_key_ref, key_pre_ref, inner_key_ref),
        )
    ):
        grad = turn(grad * scale, cos_part, sin_part)
        by_unit = grad * (pre_ref[...] * scales_ref[:, row : row + 1])
        inner_ref[...] += by_unit * gains_ref[row : row + 1]
        grad_gains_ref[row : row + 1, :] = jnp.sum(by_unit, axis=0, keepdims=True)
        out_ref[...] = grad


def attend_back(query, key, value, bias, lse, grad_context, query_pre, key_pre, scales, gains, cos_wide, sin_wide):
    total, width = query.shape
    heads = width // HEAD_DIM
    part, whole, gain, scale, square, lse_spec = head_specs(total)
    wide = jax.ShapeDtypeStruct((total, width), f32)
    narrow = jax.ShapeDtypeStruct((total, HEAD_DIM), f32)
    return pl.pallas_call(
        functools.partial(attend_back_kernel, 256, 1.0 / math.sqrt(HEAD_DIM)),
        grid=(heads,),
        in_specs=[part, part, part, square, lse_spec, part, part, part, scale, gain, whole, whole],
        out_specs=[part, part, part, whole, whole, gain],
        out_shape=[
            wide,
            wide,
            jax.ShapeDtypeStruct((total, width), bf16),
            narrow,
            narrow,
            jax.ShapeDtypeStruct((2, width), f32),
        ],
        scratch_shapes=[pltpu.VMEM((total, HEAD_DIM), f32)] * 2,
        compiler_params=pltpu.CompilerParams(vmem_limit_bytes=58 * 2**20),
        cost_estimate=pl.CostEstimate(
            flops=10 * total * total * width, bytes_accessed=30 * total * width, transcendentals=total * total * heads
        ),
    )(query, key, value, bias, lse, grad_context, query_pre, key_pre, scales, gains, cos_wide, sin_wide)


def sums_kernel(tokens_ref, grads_ref, side_ref, out_ref):
    wide = grads_ref.shape[1]
    out_ref[:, :wide] = dot(tokens_ref[...], grads_ref[...], TN, bf16)
    out_ref[:, wide:] = side_ref[...]


def sums_beside(tokens, grads, side):
    total, rows = tokens.shape
    wide, extra = grads.shape[1], side.shape[1]
    size = 256
    return pl.pallas_call(
        sums_kernel,
        grid=(rows // size,),
        in_specs=[
            pl.BlockSpec((total, size), lambda i: (0, i)),
            pl.BlockSpec((total, wide), lambda i: (0, 0)),
            pl.BlockSpec((size, extra), lambda i: (i, 0)),
        ],
        out_specs=pl.BlockSpec((size, wide + extra), lambda i: (i, 0)),
        out_shape=jax.ShapeDtypeStruct((rows, wide + extra), bf16),
        compiler_params=pltpu.CompilerParams(vmem_limit_bytes=40 * 2**20),
        cost_estimate=pl.CostEstimate(
            flops=2 * total * rows * wide, bytes_accessed=2 * rows * (total + wide + 2 * extra), transcendentals=0
        ),
    )(tokens, grads, side)


def landed(ref, sem):
    pltpu.make_async_copy(ref, ref, sem).wait()


def line_order(z):
    far, inner = z // 2, ((z + 1) // 2) % 2
    blocks = []
    for end, middle in ((3, 0), (2, 2), (1, 3), (0, 1)):
        first = end + inner * (middle - end)
        blocks.append(first + far * (3 - 2 * first))
    near = 1 + far
    chips = [near + inner * (blocks[0] - near), blocks[1], blocks[2]]
    slots = [3 + inner * (-2 - far), 2 + inner * (far - 2), far + inner * (2 - far)]
    return far, inner, blocks, chips, slots


def other(index, hop):
    return (index, index + 1 - 2 * (index % 2), (index + 2) % 4, 3 - index)[hop]


def final_kernel(
    tokens_hbm,
    grads_hbm,
    weights_hbm,
    output_hbm,
    hidden_hbm,
    up_hbm,
    gains_hbm,
    query_out,
    key_out,
    value_out,
    output_out,
    inputs_out,
    up_out,
    gains_out,
    tokens,
    grads,
    weights,
    hidden,
    core_out,
    core_in,
    mine,
    line_in,
    side,
    side_in,
    side_mine,
    side_line_in,
    tokens_send,
    tokens_in,
    rows_send,
    rows_in,
    up_in,
    gains,
    gains_in,
    gains_line,
    load_sem,
    row_send_sem,
    row_recv_sem,
    core_send_sem,
    core_recv_sem,
    line_send_sem,
    line_recv_sem,
    leaf_send_sem,
    leaf_recv_sem,
):
    leaf, row = lax.axis_index("leaf"), lax.axis_index("row")
    z, core = leaf // 2, leaf % 2
    far, inner, blocks, chips, slots = line_order(z)
    wide, own = grads.shape[1], query_out.shape[0]
    part, size = wide // 3, mine.shape[1]
    rows = tokens_in.shape[1]
    hops = (3, 1, 2)

    loads = [
        pltpu.make_async_copy(tokens_hbm, tokens, load_sem.at[0]),
        pltpu.make_async_copy(grads_hbm, grads, load_sem.at[1]),
        pltpu.make_async_copy(weights_hbm.at[:, pl.ds(0, wide)], weights, load_sem.at[2]),
        pltpu.make_async_copy(hidden_hbm, hidden, load_sem.at[3]),
        pltpu.make_async_copy(output_hbm.at[:, row], side.at[pl.ds(2 * row, 2)], load_sem.at[4]),
        pltpu.make_async_copy(gains_hbm.at[row], gains, load_sem.at[6]),
    ]
    for load in loads:
        load.start()
    barrier = pltpu.get_barrier_semaphore()
    for hop in hops:
        pl.semaphore_signal(barrier, inc=1, device_id={"row": other(row, hop)}, device_id_type=MESH)
    for step in range(1, 8):
        pl.semaphore_signal(barrier, inc=1, device_id={"leaf": (leaf + step) % 8}, device_id_type=MESH)
    pl.semaphore_wait(barrier, 10)

    sent = []

    def row_copy(source, target, kind, hop):
        copy = pltpu.make_async_remote_copy(
            source,
            target,
            row_send_sem.at[kind, hop - 1],
            row_recv_sem.at[kind, hop - 1],
            device_id={"row": other(row, hop)},
            device_id_type=MESH,
        )
        copy.start()
        sent.append(copy)

    def core_copy(source, target, kind, i):
        copy = pltpu.make_async_remote_copy(
            source,
            target,
            core_send_sem.at[kind, i],
            core_recv_sem.at[kind, i],
            device_id={"leaf": 2 * z + 1 - core},
            device_id_type=MESH,
        )
        copy.start()
        sent.append(copy)

    def line_copy(source, target, kind, i):
        return pltpu.make_async_remote_copy(
            source,
            target.at[slots[i]],
            line_send_sem.at[kind, i],
            line_recv_sem.at[kind, slots[i]],
            device_id={"leaf": 2 * chips[i] + core},
            device_id_type=MESH,
        )

    for hop in hops:
        row_copy(gains_hbm.at[other(row, hop)], gains_in.at[hop - 1], 4, hop)
    for hop in hops:
        row_copy(output_hbm.at[:, other(row, hop)], side.at[pl.ds(2 * row, 2)], 0, hop)

    loads[0].wait()
    loads[1].wait()

    def product(block):
        return dot(tokens[:, pl.ds(pl.multiple_of(block * size, size), size)], grads[...], TN)

    def across(i):
        core_out[i] = product(2 * blocks[i] + 1 - core).astype(bf16)
        core_copy(core_out.at[i], core_in.at[i], 0, i)

    across(0)
    across(1)

    def pair(i):
        mine[i] = (product(2 * blocks[i] + core) + core_in[i].astype(f32)).astype(bf16)

    for i in range(4):
        landed(core_in.at[i], core_recv_sem.at[0, i])
        pair(i)
        if i < 2:
            copy = line_copy(mine.at[i], line_in, 0, i)
            copy.start()
            sent.append(copy)
            across(i + 2)
        if i == 2:
            last = line_copy(mine.at[2], line_in, 0, 2)
            sent.append(last)

            @pl.when(inner == 0)
            def _():
                last.start()

    loads[5].wait()
    for hop in hops:
        landed(gains_in.at[hop - 1], row_recv_sem.at[4, hop - 1])
        gains[...] += gains_in[hop - 1]
    for step in range(1, 8):
        copy = pltpu.make_async_remote_copy(
            gains.at[(leaf + step) % 8],
            gains_line.at[step - 1],
            leaf_send_sem.at[step - 1],
            leaf_recv_sem.at[step - 1],
            device_id={"leaf": (leaf + step) % 8},
            device_id_type=MESH,
        )
        copy.start()
        sent.append(copy)

    loads[2].wait()

    def tokens_part(hop, store):
        lines = grads[pl.ds(pl.multiple_of((other(row, hop)) * rows, rows), rows), :]

        def step(j, carry):
            columns = pl.ds(pl.multiple_of(j * part, part), part)
            store(columns, dot(lines, weights[columns, :], NT))
            return carry

        lax.fori_loop(0, weights.shape[0] // part, step, 0)

    for hop in hops:

        def store(columns, values):
            tokens_send[hop - 1, :, columns] = values.astype(bf16)

        tokens_part(hop, store)
        row_copy(tokens_send.at[hop - 1], tokens_in.at[hop - 1], 1, hop)

    loads[4].wait()
    for hop in hops:
        landed(side.at[pl.ds(2 * (other(row, hop)), 2)], row_recv_sem.at[0, hop - 1])
    for i in range(4):
        core_copy(side.at[2 * blocks[i] + 1 - core], side_in.at[i], 1, i)

    for hop in hops:
        row_copy(up_hbm.at[pl.ds((other(row, hop)) * own, own)], up_in.at[row], 2, hop)
    keep = pltpu.make_async_copy(up_hbm.at[pl.ds(row * own, own)], up_in.at[row], load_sem.at[5])
    keep.start()

    @pl.when(inner == 1)
    def _():
        landed(line_in.at[3], line_recv_sem.at[0, 3])
        mine[2] = (mine[2].astype(f32) + line_in[3].astype(f32)).astype(bf16)
        last.start()

    for i in range(4):
        landed(side_in.at[i], core_recv_sem.at[1, i])
        side_mine[i] = (side[2 * blocks[i] + core].astype(f32) + side_in[i].astype(f32)).astype(bf16)

    loads[3].wait()

    def own_store(columns, values):
        hidden[:, columns] += values

    tokens_part(0, own_store)
    gains_out[...] = gains[leaf]
    for step in range(1, 8):
        landed(gains_line.at[step - 1], leaf_recv_sem.at[step - 1])
        gains_out[...] += gains_line[step - 1]

    def near(kind, came, kept):
        for slot in range(2):

            @pl.when(inner + (1 - far) * slot + far * (1 - slot) > 0)
            def _():
                landed(came.at[slot], line_recv_sem.at[kind, slot])
                kept[3] = (kept[3].astype(f32) + came[slot].astype(f32)).astype(bf16)

    def beyond(kind, came, kept):
        landed(came.at[2], line_recv_sem.at[kind, 2])
        kept[3] = (kept[3].astype(f32) + came[2].astype(f32)).astype(bf16)

    near(0, line_in, mine)
    for i in range(2):
        copy = line_copy(side_mine.at[i], side_line_in, 1, i)
        copy.start()
        sent.append(copy)
    side_last = line_copy(side_mine.at[2], side_line_in, 1, 2)
    sent.append(side_last)

    @pl.when(inner == 0)
    def _():
        side_last.start()

    beyond(0, line_in, mine)
    rows_send[...] = mine[3]
    for hop in hops:
        row_copy(rows_send.at[pl.ds(other(row, hop) * own, own)], rows_in.at[hop - 1], 3, hop)

    @pl.when(inner == 1)
    def _():
        landed(side_line_in.at[3], line_recv_sem.at[1, 3])
        side_mine[2] = (side_mine[2].astype(f32) + side_line_in[3].astype(f32)).astype(bf16)
        side_last.start()

    for hop in hops:
        landed(tokens_in.at[hop - 1], row_recv_sem.at[1, hop - 1])
        hidden[...] += tokens_in[hop - 1].astype(f32)
    inputs_out[...] = hidden[...].astype(bf16)

    keep.wait()
    for hop in hops:
        landed(up_in.at[other(row, hop)], row_recv_sem.at[2, hop - 1])
    for source in range(4):
        up_out[:, source * up_in.shape[2] : (source + 1) * up_in.shape[2]] = up_in[source].astype(f32)

    def give(source, values):
        columns = pl.ds(pl.multiple_of(source * part, part), part)
        for i, out in enumerate((query_out, key_out, value_out)):
            out[:, columns] = values[:, i * part : (i + 1) * part].astype(f32)

    give(row, rows_send[pl.ds(pl.multiple_of(row * own, own), own), :])
    near(1, side_line_in, side_mine)
    beyond(1, side_line_in, side_mine)
    output_out[...] = side_mine[3].astype(f32)
    for hop in hops:
        landed(rows_in.at[hop - 1], row_recv_sem.at[3, hop - 1])
        give(other(row, hop), rows_in[hop - 1])
    for copy in sent:
        copy.wait_send()


def finish(tokens, grads, weights, output_part, hidden, up_shard, gain_part):
    total, width = tokens.shape
    wide = grads.shape[1]
    own = output_part.shape[2]
    size, rows, units = 4 * own, hidden.shape[0], up_shard.shape[1]
    matrix = jax.ShapeDtypeStruct((own, width), f32)
    dma = pltpu.SemaphoreType.DMA
    return pl.pallas_call(
        final_kernel,
        in_specs=[pl.BlockSpec(memory_space=pl.ANY)] * 7,
        out_specs=[pl.BlockSpec(memory_space=pltpu.VMEM)] * 7,
        out_shape=[
            matrix,
            matrix,
            matrix,
            matrix,
            jax.ShapeDtypeStruct((rows, width), bf16),
            jax.ShapeDtypeStruct((own, 4 * units), f32),
            jax.ShapeDtypeStruct((8, HEAD_DIM), f32),
        ],
        scratch_shapes=[
            pltpu.VMEM((total, width), bf16),
            pltpu.VMEM((total, wide), bf16),
            pltpu.VMEM((width, wide), bf16),
            pltpu.VMEM((rows, width), f32),
            pltpu.VMEM((4, size, wide), bf16),
            pltpu.VMEM((4, size, wide), bf16),
            pltpu.VMEM((4, size, wide), bf16),
            pltpu.VMEM((4, size, wide), bf16),
            pltpu.VMEM((8, own, width), bf16),
            pltpu.VMEM((4, own, width), bf16),
            pltpu.VMEM((4, own, width), bf16),
            pltpu.VMEM((4, own, width), bf16),
            pltpu.VMEM((3, rows, width), bf16),
            pltpu.VMEM((3, rows, width), bf16),
            pltpu.VMEM((size, wide), bf16),
            pltpu.VMEM((3, own, wide), bf16),
            pltpu.VMEM((4, own, units), bf16),
            pltpu.VMEM((8, 8, HEAD_DIM), f32),
            pltpu.VMEM((3, 8, 8, HEAD_DIM), f32),
            pltpu.VMEM((7, 8, HEAD_DIM), f32),
            dma((7,)),
            dma((5, 3)),
            dma((5, 3)),
            dma((2, 4)),
            dma((2, 4)),
            dma((2, 3)),
            dma((2, 4)),
            dma((7,)),
            dma((7,)),
        ],
        compiler_params=pltpu.CompilerParams(
            collective_id=1, has_side_effects=True, vmem_limit_bytes=60 * 2**20
        ),
        cost_estimate=pl.CostEstimate(
            flops=4 * total * width * wide, bytes_accessed=100 * 2**20, transcendentals=0
        ),
    )(tokens, grads, weights, output_part, hidden, up_shard, gain_part)


def front_kernel(
    tokens_hbm,
    query_hbm,
    key_hbm,
    value_hbm,
    output_hbm,
    gate_hbm,
    up_hbm,
    down_hbm,
    gains_hbm,
    cos_hbm,
    sin_hbm,
    bias_hbm,
    attn_out,
    gate_out,
    up_out,
    first_out,
    second_out,
    gate_pre_out,
    up_pre_out,
    activated_out,
    tokens_out,
    query_pre_out,
    key_pre_out,
    value_out,
    scales_out,
    query_out,
    key_out,
    context_out,
    lse_out,
    output_out,
    unit_out,
    unit_scale_out,
    hidden_out,
    hidden_all_out,
    gains_out,
    block,
    attn_mat,
    gate_block,
    up_block,
    down_block,
    tokens,
    query_pre,
    key_pre,
    value,
    query,
    key,
    context,
    lse,
    bias,
    cos_part,
    sin_part,
    scale_columns,
    output_in,
    output_mat,
    rows_send,
    rows_in,
    half_in,
    attn,
    unit_scale,
    hidden,
    hidden_all,
    squares,
    squares_in,
    scale_rows,
    gains_leaf,
    gains_all,
    gains,
    load_sem,
    save_sem,
    row_send_sem,
    row_recv_sem,
    leaf_send_sem,
    leaf_recv_sem,
    core_send_sem,
    core_recv_sem,
    line_send_sem,
    line_recv_sem,
):
    leaf, row = lax.axis_index("leaf"), lax.axis_index("row")
    z, core = leaf // 2, leaf % 2
    far, inner = z // 2, ((z + 1) // 2) % 2
    own, width = query_hbm.shape
    part, size = width // 4, 4 * own
    rows, wide = tokens_hbm.shape[0], 3 * part
    units = gate_block.shape[1]
    heads = part // HEAD_DIM
    scale = 1.0 / math.sqrt(HEAD_DIM)
    hops = (3, 1, 2)
    sent, saved = [], []

    def lines(index, count):
        return pl.ds(pl.multiple_of(index * count, count), count)

    def load(source, target, i):
        copy = pltpu.make_async_copy(source, target, load_sem.at[i])
        copy.start()
        return copy

    def save(source, target):
        copy = pltpu.make_async_copy(source, target, save_sem.at[len(saved)])
        copy.start()
        saved.append(copy)

    mine = lines(row, own)
    load_weights = [
        load(source, attn.at[pl.ds(i * own, own)], (0, 1, 15, 16)[i])
        for i, source in enumerate((query_hbm, key_hbm, value_hbm, output_hbm))
    ]
    load_gains = load(gains_hbm, gains_leaf.at[row], 2)
    load_gate = load(gate_hbm.at[:, lines(row, units)], gate_block.at[mine], 3)
    load_tokens = load(tokens_hbm, tokens.at[lines(row, rows)], 4)
    load_up = load(up_hbm.at[:, lines(row, units)], up_block.at[mine], 5)
    load_down = load(down_hbm.at[:, lines(row, units)], down_block.at[mine], 6)
    load_tables = [load(cos_hbm, cos_part, 7), load(sin_hbm, sin_part, 8), load(bias_hbm, bias, 9)]

    barrier = pltpu.get_barrier_semaphore()
    for hop in hops:
        pl.semaphore_signal(barrier, inc=1, device_id={"row": other(row, hop)}, device_id_type=MESH)
    for step in range(1, 8):
        pl.semaphore_signal(barrier, inc=1, device_id={"leaf": (leaf + step) % 8}, device_id_type=MESH)
    pl.semaphore_wait(barrier, 10)

    def row_copy(source, target, kind, hop):
        copy = pltpu.make_async_remote_copy(
            source,
            target,
            row_send_sem.at[kind, hop - 1],
            row_recv_sem.at[kind, hop - 1],
            device_id={"row": other(row, hop)},
            device_id_type=MESH,
        )
        copy.start()
        sent.append(copy)

    def row_landed(target, kind):
        for hop in hops:
            landed(target(other(row, hop), hop), row_recv_sem.at[kind, hop - 1])

    def leaf_copy(source, target, send_sem, recv_sem, to):
        return pltpu.make_async_remote_copy(
            source, target, send_sem, recv_sem, device_id={"leaf": to}, device_id_type=MESH
        )

    for copy in load_weights:
        copy.wait()
    for hop in hops:
        for i in range(3):
            some = attn[i * own : (i + 1) * own, lines(other(row, hop), part)]
            rows_send[hop - 1, :own, i * part : (i + 1) * part] = some.astype(bf16)
        row_copy(rows_send.at[hop - 1, pl.ds(0, own), pl.ds(0, wide)], block.at[mine, pl.ds(0, wide)], 0, hop)
    packs = sent[:]
    sent.clear()
    for i in range(3):
        block[mine, i * part : (i + 1) * part] = attn[i * own : (i + 1) * own, lines(row, part)].astype(bf16)
    for i in range(4):
        block[i * own : (i + 1) * own, wide:] = attn[3 * own :, i * part : (i + 1) * part].astype(bf16)
    for hop in hops:
        row_copy(gains_hbm, gains_leaf.at[row], 1, hop)
    for hop in hops:
        row_copy(gate_hbm.at[:, lines(other(row, hop), units)], gate_block.at[mine], 2, hop)
    for hop in hops:
        row_copy(tokens_hbm, tokens.at[lines(row, rows)], 3, hop)
    for hop in hops:
        row_copy(up_hbm.at[:, lines(other(row, hop), units)], up_block.at[mine], 4, hop)
    for hop in hops:
        row_copy(down_hbm.at[:, lines(other(row, hop), units)], down_block.at[mine], 5, hop)

    sizes = (size, size, size, size // 2, size // 2)

    def spread(kind, source, whole, stage=0):
        place = whole.at[lines(leaf, sizes[kind])]
        across = leaf_copy(
            source, place, line_send_sem.at[kind, 2], line_recv_sem.at[kind, 2], 2 * other(z, 2) + core
        )
        if stage < 2:
            across.start()
            sent.append(across)
        if stage == 1:
            return None
        forth = leaf_copy(source, place, line_send_sem.at[kind, 0], line_recv_sem.at[kind, 0], 2 * z + 2 + core)
        back = leaf_copy(source, place, line_send_sem.at[kind, 1], line_recv_sem.at[kind, 1], 2 * z - 2 + core)

        @pl.when(z < 3)
        def _():
            forth.start()

        @pl.when(z > 0)
        def _():
            back.start()

        beside = leaf_copy(source, place, core_send_sem.at[kind, 3], core_recv_sem.at[kind, 3], 2 * z + 1 - core)
        beside.start()
        sent.append(beside)
        save(source, place)

        def done():
            @pl.when(z < 3)
            def _():
                forth.wait_send()

            @pl.when(z > 0)
            def _():
                back.wait_send()

        return done

    def arrival(step):
        inner_slot, inner_chip = ((2, other(z, 2)), (0, z - 1), (1, z + 1))[step]
        end_slot, end_chip = ((1 - far, 1 + far), (2, other(z, 2)), (3, 3 - z))[step]
        return end_slot + inner * (inner_slot - end_slot), end_chip + inner * (inner_chip - end_chip)

    def pass_on(kind, whole, step):
        slot, chip = arrival(step)
        place = whole.at[lines(2 * chip + core, sizes[kind])]
        landed(place, line_recv_sem.at[kind, slot])
        beside = leaf_copy(place, place, core_send_sem.at[kind, step], core_recv_sem.at[kind, step], 2 * z + 1 - core)
        beside.start()
        sent.append(beside)
        if step == 0:
            onward = leaf_copy(place, place, line_send_sem.at[kind, 3], line_recv_sem.at[kind, 3], 6 * far + core)

            @pl.when(inner == 1)
            def _():
                onward.start()

            def done():
                @pl.when(inner == 1)
                def _():
                    onward.wait_send()

            return done

    def gathered(kind, whole):
        landed(whole.at[lines(2 * z + 1 - core, sizes[kind])], core_recv_sem.at[kind, 3])
        for step in range(3):
            chip = arrival(step)[1]
            landed(whole.at[lines(2 * chip + 1 - core, sizes[kind])], core_recv_sem.at[kind, step])

    row_landed(lambda source, hop: block.at[lines(source, own), pl.ds(0, wide)], 0)
    done = [spread(0, block, attn_mat)]

    load_gains.wait()
    row_landed(lambda source, hop: gains_leaf.at[source], 1)
    for step in range(1, 8):
        copy = leaf_copy(
            gains_leaf, gains_all.at[leaf], leaf_send_sem.at[step - 1], leaf_recv_sem.at[step - 1], (leaf + step) % 8
        )
        copy.start()
        sent.append(copy)
    gains_all[leaf] = gains_leaf[...]

    load_gate.wait()
    row_landed(lambda source, hop: gate_block.at[lines(source, own)], 2)
    done.append(pass_on(0, attn_mat, 0))
    pass_on(0, attn_mat, 1)
    done.append(spread(1, gate_block, gate_out))
    pass_on(0, attn_mat, 2)
    gathered(0, attn_mat)
    saved[0].wait()

    load_tokens.wait()
    row_landed(lambda source, hop: tokens.at[lines(source, rows)], 3)

    def project_step(j, carry):
        at = lines(j, rows)
        some = tokens[at, :]
        for i, out in enumerate((query_pre, key_pre)):
            product = dot(some, attn_mat[:, i * part : (i + 1) * part], NN)
            out[at, :] = product
            square = jnp.sum(product * product, axis=1, keepdims=True)
            squares[i : i + 1, at] = jnp.broadcast_to(square, (rows, HEAD_DIM)).T[0:1]
        value[at, :] = dot(some, attn_mat[:, 2 * part : wide], NN, bf16)
        return carry

    squares[...] = jnp.zeros_like(squares)
    lax.fori_loop(0, 4, project_step, 0)
    for hop in hops:
        row_copy(squares, squares_in.at[hop - 1], 7, hop)
    for hop in hops:
        row_copy(
            attn_mat.at[lines(other(row, hop), 2 * size), pl.ds(wide, part)], output_in.at[row], 6, hop
        )
    swapped = len(sent)
    keep = load(attn_mat.at[lines(row, 2 * size), pl.ds(wide, part)], output_in.at[row], 10)
    load_up.wait()
    row_landed(lambda source, hop: up_block.at[lines(source, own)], 4)
    done.append(spread(2, up_block, up_out))
    save(attn_mat, attn_out)
    save(tokens, tokens_out)
    save(query_pre, query_pre_out)
    save(key_pre, key_pre_out)
    save(value, value_out)
    for step in range(1, 8):
        landed(gains_all.at[(leaf - step + 8) % 8], leaf_recv_sem.at[step - 1])
    for source in range(8):
        for pair in range(2):
            first = (2 * source + pair) * HEAD_DIM
            gains[:, first : first + HEAD_DIM] = gains_all[source, 2 * pair] + gains_all[source, 2 * pair + 1]
    save(gains, gains_out)
    for table in load_tables:
        table.wait()
    row_landed(lambda source, hop: squares_in.at[hop - 1], 7)
    scales = lax.rsqrt((squares[...] + squares_in[0] + squares_in[1] + squares_in[2]) / width + epsilon)
    scale_rows[...] = scales
    save(scale_rows, scales_out)
    for i in range(2):
        scale_columns[i] = jnp.broadcast_to(scales[i : i + 1], (HEAD_DIM, 4 * rows)).T

    def head_step(h, carry):
        at = lines(h, HEAD_DIM)
        at_gain = lines(row * heads + h, HEAD_DIM)
        for i, (pre, out) in enumerate(((query_pre, query), (key_pre, key))):
            scaled = pre[:, at] * scale_columns[i] * gains[i : i + 1, at_gain]
            out[:, at] = turn(scaled, cos_part[...], sin_part[...]).astype(bf16)
        for first in range(0, 4 * rows, rows):
            last = first + rows
            scores = dot(key[:last, at], query[first:last, at], NT) * scale
            scores = scores + bias[:last, first:last].astype(f32)
            top = jnp.max(scores, axis=0, keepdims=True)
            probs = jnp.exp(scores - top)
            mass = jnp.sum(probs, axis=0, keepdims=True)
            probs_low = (probs * (1.0 / mass)).astype(bf16)
            turned = dot(value[:last, at], probs_low, TN)
            context[first:last, at] = turned.T.astype(bf16)
            lse[lines(h, 8), first:last] = jnp.broadcast_to(top + jnp.log(mass), (8, rows))
        return carry

    lax.fori_loop(0, heads, head_step, 0)
    done.append(pass_on(1, gate_out, 0))
    save(query, query_out)
    save(key, key_out)
    save(context, context_out)
    save(lse, lse_out)

    keep.wait()
    row_landed(lambda source, hop: output_in.at[source], 6)
    for i in range(2):
        for source in range(4):
            for j in range(4):
                output_mat[i * size + source * own : i * size + (source + 1) * own, j * part : (j + 1) * part] = (
                    output_in[source, i * size + j * own : i * size + (j + 1) * own, :]
                )
    save(output_mat, output_out)

    def output_part(hop, store):
        some = context[lines(other(row, hop), rows), :]
        for j in range(4):
            columns = slice(j * part, (j + 1) * part)
            store(columns, dot(some, output_mat[:, columns], NN))

    for copy in packs:
        copy.wait_send()
    half = rows // 2
    top, bottom = pl.ds(0, half), pl.ds(half, half)
    for hop in hops:

        def store(columns, values):
            rows_send[hop - 1, :, columns] = values.astype(bf16)

        output_part(hop, store)
        if hop == 3:
            row_copy(rows_send.at[2, top], half_in.at[0], 8, 1)
            row_copy(rows_send.at[2, bottom], half_in.at[1], 8, 2)
        else:
            early = (top, bottom)[hop - 1]
            row_copy(rows_send.at[hop - 1, early], rows_in.at[hop - 1, early], 10, hop)
    for hop in (1, 2):
        late = (bottom, top)[hop - 1]
        landed(half_in.at[2 - hop], row_recv_sem.at[8, 2 - hop])
        rows_send[hop - 1, late] = (rows_send[hop - 1, late].astype(f32) + half_in[2 - hop].astype(f32)).astype(bf16)
        row_copy(rows_send.at[hop - 1, late], rows_in.at[hop - 1, late], 11, hop)

    def own_store(columns, values):
        attn[:, columns] = values

    output_part(0, own_store)

    pass_on(1, gate_out, 1)
    done.append(pass_on(2, up_out, 0))
    for hop in (1, 2):
        early, late = ((top, bottom), (bottom, top))[hop - 1]
        landed(rows_in.at[hop - 1, early], row_recv_sem.at[10, hop - 1])
        landed(rows_in.at[hop - 1, late], row_recv_sem.at[11, hop - 1])
        attn[...] += rows_in[hop - 1].astype(f32)
    mean = jnp.sum(attn[...] * attn[...], axis=1, keepdims=True) / width
    factor = lax.rsqrt(mean + epsilon)
    unit_scale[...] = jnp.broadcast_to(factor, unit_scale.shape)
    attn[...] = attn[...] * factor
    hidden[...] = tokens[lines(row, rows), :].astype(f32) + attn[...] * gains[2:3, :]
    hidden_all[lines(row, rows), :] = hidden[...].astype(bf16)
    for hop in (1, 2):
        place = hidden_all.at[lines(row, rows)]
        row_copy(place, place, 9, hop)
    save(attn, unit_out)
    save(unit_scale, unit_scale_out)
    save(hidden, hidden_out)
    for hop in (1, 2):
        landed(hidden_all.at[lines(other(row, hop), rows)], row_recv_sem.at[9, hop - 1])
        place = hidden_all.at[lines(2 * other(row, hop) + hop - 1, half)]
        row_copy(place, place, 12, 3 - hop)
    for hop in (1, 2):
        landed(hidden_all.at[lines(2 * other(row, 3) + 2 - hop, half)], row_recv_sem.at[12, hop - 1])
    save(hidden_all, hidden_all_out)
    pass_on(1, gate_out, 2)
    pass_on(2, up_out, 1)
    load_down.wait()
    row_landed(lambda source, hop: down_block.at[lines(source, own)], 5)
    downs = (first_out, second_out)
    down_parts = [down_block.at[pl.ds(h * size // 2, size // 2)] for h in range(2)]
    for h in range(2):
        spread(3 + h, down_parts[h], downs[h], 1)
    for h in range(2):
        done.append(spread(3 + h, down_parts[h], downs[h], 2))
    pass_on(2, up_out, 2)
    gathered(1, gate_out)
    gathered(2, up_out)

    for copy in sent[:swapped]:
        copy.wait_send()
    for finish_sends in done[:2]:
        finish_sends()
    for copy in saved[1:]:
        copy.wait()
    saved.clear()

    def quarter(j):
        columns = pl.ds(j * part, part)
        return [
            load(source.at[:, columns], attn_mat.at[:, pl.ds((2 * i + j % 2) * part, part)], 11 + 2 * i + j % 2)
            for i, source in enumerate((gate_out, up_out))
        ]

    coming = quarter(0)
    for j in range(4):
        for copy in coming:
            copy.wait()
        if j < 3:
            coming = quarter(j + 1)
        for copy in saved:
            copy.wait()
        saved.clear()

        slot = j % 2

        def units_step(i, carry):
            at = lines(i, rows)
            some = hidden_all[at, :]
            gate = dot(some, attn_mat[:, slot * part : (slot + 1) * part], NN)
            up = dot(some, attn_mat[:, (2 + slot) * part : (3 + slot) * part], NN)
            query_pre[at, :] = gate
            key_pre[at, :] = up
            value[at, :] = (gate * jax.nn.sigmoid(gate) * up).astype(bf16)
            return carry

        lax.fori_loop(0, 4, units_step, 0)
        columns = pl.ds(j * part, part)
        save(query_pre, gate_pre_out.at[:, columns])
        save(key_pre, up_pre_out.at[:, columns])
        save(value, activated_out.at[:, columns])
        if j == 1:
            done.append(pass_on(3, first_out, 0))
        if j == 2:
            done.append(pass_on(4, second_out, 0))
            pass_on(3, first_out, 1)
    pass_on(3, first_out, 2)
    pass_on(4, second_out, 1)
    pass_on(4, second_out, 2)
    gathered(3, first_out)
    gathered(4, second_out)

    for finish_sends in done[2:]:
        finish_sends()
    for copy in sent[swapped:]:
        copy.wait_send()
    for copy in saved:
        copy.wait()


def front(tokens, weights, gate, up, down, gain_tile, cos_wide, sin_wide, bias):
    rows, width = tokens.shape
    total, part, own = 4 * rows, width // 4, gate.shape[0]
    wide, units, size = 3 * part, gate.shape[1] // 4, 4 * own
    heads = part // HEAD_DIM
    shape = jax.ShapeDtypeStruct
    outs = [
        shape((width, width), bf16),
        shape((width, units), bf16),
        shape((width, units), bf16),
        shape((width // 2, units), bf16),
        shape((width // 2, units), bf16),
        shape((total, units), f32),
        shape((total, units), f32),
        shape((total, units), bf16),
        shape((total, width), bf16),
        shape((total, part), f32),
        shape((total, part), f32),
        shape((total, part), bf16),
        shape((8, total), f32),
        shape((total, part), bf16),
        shape((total, part), bf16),
        shape((total, part), bf16),
        shape((8 * heads, total), f32),
        shape((part, width), bf16),
        shape((rows, width), f32),
        shape((rows, HEAD_DIM), f32),
        shape((rows, width), f32),
        shape((total, width), bf16),
        shape((8, width), f32),
    ]
    vmem, dma = pltpu.VMEM, pltpu.SemaphoreType.DMA
    return pl.pallas_call(
        front_kernel,
        in_specs=[pl.BlockSpec(memory_space=pl.ANY)] * 12,
        out_specs=[pl.BlockSpec(memory_space=pl.ANY)] * len(outs),
        out_shape=outs,
        scratch_shapes=[
            vmem((size, width), bf16),
            vmem((width, width), bf16),
            vmem((size, units), bf16),
            vmem((size, units), bf16),
            vmem((size, units), bf16),
            vmem((total, width), bf16),
            vmem((total, part), f32),
            vmem((total, part), f32),
            vmem((total, part), bf16),
            vmem((total, part), bf16),
            vmem((total, part), bf16),
            vmem((total, part), bf16),
            vmem((8 * heads, total), f32),
            vmem((total, total), bf16),
            vmem((total, HEAD_DIM), f32),
            vmem((total, HEAD_DIM), f32),
            vmem((2, total, HEAD_DIM), f32),
            vmem((4, part, part), bf16),
            vmem((part, width), bf16),
            vmem((3, rows, width), bf16),
            vmem((2, rows, width), bf16),
            vmem((2, rows // 2, width), bf16),
            vmem((rows, width), f32),
            vmem((rows, HEAD_DIM), f32),
            vmem((rows, width), f32),
            vmem((total, width), bf16),
            vmem((8, total), f32),
            vmem((3, 8, total), f32),
            vmem((8, total), f32),
            vmem((4, 8, HEAD_DIM), f32),
            vmem((8, 4, 8, HEAD_DIM), f32),
            vmem((8, width), f32),
            dma((17,)),
            dma((32,)),
            dma((13, 3)),
            dma((13, 3)),
            dma((7,)),
            dma((7,)),
            dma((5, 4)),
            dma((5, 4)),
            dma((5, 4)),
            dma((5, 4)),
        ],
        compiler_params=pltpu.CompilerParams(
            collective_id=2, has_side_effects=True, vmem_limit_bytes=62 * 2**20
        ),
        cost_estimate=pl.CostEstimate(
            flops=10 * total * width * part, bytes_accessed=100 * 2**20, transcendentals=0
        ),
    )(tokens, *weights, gate, up, down, gain_tile, cos_wide, sin_wide, bias)


def body(
    inputs,
    cotangent,
    seg_lengths,
    seg_parents,
    w_query,
    w_key,
    w_value,
    w_output,
    gain_query,
    gain_key,
    gain_attn,
    w_gate,
    w_up,
    w_down,
    gain_mlp,
):
    trees, rows_dev, width = inputs.shape
    count, leaves, me = lax.axis_size("row"), lax.axis_size("leaf"), lax.axis_index("row")
    tree_len = rows_dev * count
    part = width // count
    own = w_query.shape[0]
    group = count * own // 2
    units = w_gate.shape[1] // count
    tokens = inputs.reshape(rows_dev, width)

    def leaf_gather(block):
        return lax.all_gather(block, "leaf", axis=0, tiled=True)

    def leaf_scatter(block):
        return lax.psum_scatter(block, "leaf", scatter_dimension=0, tiled=True)

    bias, cos_wide, sin_wide = tree_tables(seg_lengths[0], seg_parents[0], tree_len)
    fast = leaves == 8 and count == 4
    if fast:
        gain_own = jnp.stack([gain_query, gain_key, gain_attn, gain_mlp]).astype(bf16).astype(f32)
        gain_tile = lax.dynamic_update_slice(jnp.zeros((8, HEAD_DIM), f32), gain_own, (0, (me % 2) * own))
        (
            attn_mat,
            gate_mat,
            up_mat,
            down_first,
            down_second,
            gate_pre,
            up_pre,
            activated,
            all_tokens,
            query_pre,
            key_pre,
            value,
            scales,
            query,
            key,
            context,
            lse,
            output_mat,
            attn_unit,
            attn_scale,
            hidden,
            hidden_all,
            gains_all,
        ) = front(
            tokens,
            (w_query, w_key, w_value, w_output),
            w_gate.astype(bf16),
            w_up.astype(bf16),
            w_down.astype(bf16),
            gain_tile,
            cos_wide,
            sin_wide,
            bias,
        )
        scales, attn_scale = scales[:2], attn_scale[:, :1]
        down_halves = [down_first, down_second]
        query_scale, key_scale = scales[0][:, None], scales[1][:, None]
        attn_gain, mlp_gain = gains_all[2], gains_all[3]
        head_gains = lax.dynamic_slice_in_dim(gains_all[:2], me * part, part, 1)
    else:
        qkv_block = columns_in(w_query, w_key, w_value)
        gains_own = jnp.stack([gain_query, gain_key, gain_attn, gain_mlp]).astype(bf16).reshape(1, 4 * own)
        gains_leaf = gather_rows(gains_own).reshape(count * own, 4)
        attn_block = jnp.concatenate(
            [
                qkv_block,
                w_output.astype(bf16).reshape(count * own, part),
                jnp.pad(gains_leaf, ((0, 0), (0, HEAD_DIM - 4))),
            ],
            axis=1,
        )
        attn_mat = leaf_gather(attn_block)
        qkv_mat = attn_mat[:, : 3 * part]
        output_rows = attn_mat[:, 3 * part : 4 * part].reshape(count, leaves // count, own, width)
        gains_all = attn_mat[:, 4 * part : 4 * part + 4].reshape(leaves, count, 4, own)
        gains_all = jnp.moveaxis(gains_all, 2, 0).reshape(4, width).astype(f32)
        gate_block = columns_in(tie(w_gate, qkv_block))
        up_block = columns_in(tie(w_up, qkv_block))
        down_block = columns_in(tie(w_down, qkv_block))
        all_tokens = gather_rows(tie(tokens, gate_block, up_block, down_block))

        query_pre, key_pre, value, squares = project(all_tokens, attn_mat, part)
        gate_mat = leaf_gather(gate_block)
        up_mat = leaf_gather(up_block)
        down_halves = [leaf_gather(down_block[h * group : (h + 1) * group]) for h in range(2)]

        squares = sum_rows(squares)
        scales = lax.rsqrt(squares / width + epsilon)
        query_scale, key_scale = scales[0][:, None], scales[1][:, None]
        attn_gain, mlp_gain = gains_all[2], gains_all[3]
        head_gains = lax.dynamic_slice_in_dim(gains_all[:2], me * part, part, 1)
        output_rows = tie(output_rows, scales)
        output_mat = jnp.zeros((leaves // count, count, own, width), bf16)
        for hop in range(count):
            piece = lax.dynamic_index_in_dim(output_rows, me ^ hop, 0, keepdims=False)
            if hop:
                piece = swap(piece, hop)
            output_mat = lax.dynamic_update_index_in_dim(output_mat, piece, me ^ hop, 1)
        output_mat = output_mat.reshape(part, width)
        query, key, context, lse = attend(
            query_pre, key_pre, value, scales.T, head_gains, cos_wide, sin_wide, bias
        )
        attn_pre = dot_scatter([context], [output_mat], NN)
        attn_scale = lax.rsqrt(jnp.mean(attn_pre * attn_pre, axis=-1, keepdims=True) + epsilon)
        attn_unit = attn_pre * attn_scale
        hidden = tokens.astype(f32) + attn_unit * attn_gain
        hidden_all = gather_rows(hidden.astype(bf16))

    if not fast:
        gate_pre = dot(hidden_all, gate_mat, NN)
        up_pre = dot(hidden_all, up_mat, NN)
        activated = (gate_pre * jax.nn.sigmoid(gate_pre) * up_pre).astype(bf16)
    sigmoid_gate = jax.nn.sigmoid(gate_pre)
    mlp_halves = [dot_scatter([activated], [down_halves[h]], NT) for h in range(2)]
    grad_final = cotangent.reshape(rows_dev, width).astype(f32)
    halves = range(2)

    def split(rows):
        rows = rows.reshape(rows.shape[:-1] + (leaves, 2, group))
        return [rows[..., h, :].reshape(rows.shape[:-3] + (width // 2,)) for h in halves]

    weighted = tie(split(grad_final * mlp_gain), hidden_all)
    square = sum(jnp.sum(m * m, axis=-1, keepdims=True) for m in mlp_halves) / width
    cross = sum(jnp.sum(m * w, axis=-1, keepdims=True) for m, w in zip(mlp_halves, weighted)) / width
    mlp_scale = lax.rsqrt(square + epsilon)
    grad_mlp = [
        (mlp_scale * (w - m * (mlp_scale * mlp_scale * cross))).astype(bf16) for m, w in zip(mlp_halves, weighted)
    ]
    grad_mlp_halves = [gather_rows(grad_mlp[h]) for h in halves]
    down_sums = [dot(grad_mlp_halves[h], activated, TN, bf16) for h in range(2)]
    down_shards = [leaf_scatter(down_sums[h]) for h in range(2)]
    grad_act = dot(tie(grad_mlp_halves[0], down_sums[0]), down_halves[0], NN)
    grad_act = grad_act + dot(tie(grad_mlp_halves[1], down_sums[1]), down_halves[1], NN)
    grad_gate = (grad_act * up_pre * sigmoid_gate * (1.0 + gate_pre * (1.0 - sigmoid_gate))).astype(bf16)
    grad_up = (grad_act * gate_pre * sigmoid_gate).astype(bf16)
    wide = width // 2
    gate_sum = dot(hidden_all, grad_gate, TN, bf16)
    parts, coming = [], []
    for h in range(2):
        one = tie(grad_gate, gate_sum, *parts), tie(grad_up, gate_sum, *parts)
        part_h = sum(
            dot(left, right[h * wide : (h + 1) * wide], NT) for left, right in zip(one, (gate_mat, up_mat))
        ).astype(bf16)
        parts.append(part_h)
        coming.append(send_rows(part_h))
    grad_hidden = grad_final + jnp.concatenate(
        [add_rows(part_h, pieces) for part_h, pieces in zip(parts, coming)], axis=1
    )
    gate_sum = tie(gate_sum, *down_sums)
    gate_shard = leaf_scatter(gate_sum)

    grad_attn, grad_attn_gain = norm_back(grad_hidden, attn_unit, attn_scale, attn_gain)
    grad_attn_low = grad_attn.astype(bf16)
    up_sum = dot(hidden_all, tie(grad_up, grad_attn_low), TN, bf16)
    grad_attn_all = gather_rows(tie(grad_attn_low, *down_shards), up_sum)
    grad_context = dot(grad_attn_all, output_mat, NT, bf16)
    up_shard = leaf_scatter(tie(up_sum, gate_sum))
    grad_context = tie(grad_context, gate_shard)
    grad_query, grad_key, grad_value, inner_query, inner_key, grad_head_gains = attend_back(
        query, key, value, bias, lse, grad_context, query_pre, key_pre, scales.T, head_gains, cos_wide, sin_wide
    )
    inner = sum_rows(jnp.stack([jnp.sum(inner_query, axis=1), jnp.sum(inner_key, axis=1)])) / width
    output_part = dot(context, tie(grad_attn_all, inner), TN, bf16).reshape(leaves // count, count, own, width)
    grad_query_low = (
        query_scale * (grad_query * head_gains[0] - query_pre * (query_scale * inner[0][:, None]))
    ).astype(bf16)
    grad_key_low = (
        key_scale * (grad_key * head_gains[1] - key_pre * (key_scale * inner[1][:, None]))
    ).astype(bf16)
    grad_qkv = jnp.concatenate([grad_query_low, grad_key_low, grad_value], axis=1)
    gate_out = columns_out(tie(gate_shard, inner_query))
    down_out = columns_out(tie(jnp.concatenate(down_shards), inner_query))
    mlp_halves = tie(mlp_halves, inner_query)
    mlp_unit = jnp.stack([m.reshape(rows_dev, leaves, group) for m in mlp_halves], axis=2).reshape(rows_dev, width)
    mlp_unit = mlp_unit * mlp_scale
    outputs = (hidden + mlp_unit * mlp_gain).astype(bf16).reshape(inputs.shape)
    grad_mlp_gain = jnp.sum(grad_final * mlp_unit, axis=0)

    wide_part = jnp.stack([tie(grad_attn_gain, inner), grad_mlp_gain]).reshape(2, leaves, count, own)
    narrow_part = grad_head_gains.reshape(2, leaves // count, count, own)
    grad_qkv = tie(grad_qkv, gate_out, down_out, outputs)
    if fast:
        gain_part = jnp.zeros((count, leaves, 8, HEAD_DIM), f32)
        gain_part = lax.dynamic_update_slice(
            gain_part, jnp.transpose(narrow_part, (2, 1, 0, 3)), (0, me * (leaves // count), 0, 0)
        )
        gain_part = lax.dynamic_update_slice(gain_part, jnp.transpose(wide_part, (2, 1, 0, 3)), (0, 0, 2, 0))
        *grad_mats, grad_output, grad_tokens, up_out, grad_gains = finish(
            all_tokens, grad_qkv, attn_mat, output_part, grad_hidden, up_shard, gain_part
        )
        grad_inputs, up_out, grad_gains = grad_tokens.reshape(inputs.shape), [up_out], grad_gains[:4, :own]
    else:
        wide_sum = jnp.zeros((2, leaves, own), f32)
        narrow_all = jnp.zeros((2, leaves, own), f32)
        for hop in range(count):
            piece = lax.dynamic_index_in_dim(jnp.concatenate([wide_part, narrow_part], axis=1), me ^ hop, 2, keepdims=False)
            if hop:
                piece = swap(piece, hop)
            wide_sum = wide_sum + piece[:, :leaves]
            narrow_all = lax.dynamic_update_slice_in_dim(
                narrow_all, piece[:, leaves:], (me ^ hop) * (leaves // count), 1
            )
        grad_gains = jnp.concatenate([narrow_all, wide_sum], axis=0)
        stride = 1
        while stride < leaves:
            grad_gains = grad_gains + lax.ppermute(
                grad_gains, "leaf", [(i, i ^ stride) for i in range(leaves)]
            )
            stride *= 2
        grad_gains = lax.dynamic_index_in_dim(grad_gains, lax.axis_index("leaf"), 1, keepdims=False)
        output_turned = jnp.zeros((count, leaves // count, own, width), bf16)
        for hop in range(count):
            piece = lax.dynamic_index_in_dim(output_part, me ^ hop, 1, keepdims=False)
            if hop:
                piece = swap(piece, hop)
            output_turned = lax.dynamic_update_index_in_dim(output_turned, piece, me ^ hop, 0)
        attn_sum = sums_beside(all_tokens, grad_qkv, output_turned.reshape(leaves * count * own, part))
        grad_tokens = grad_hidden + dot_scatter([grad_qkv], [qkv_mat], NT)
        grad_inputs = grad_tokens.astype(bf16).reshape(inputs.shape)
        attn_shard = leaf_scatter(tie(attn_sum, up_shard))
        up_out = columns_out(up_shard)
        grad_mats = columns_out(attn_shard[:, : 3 * part], 3)
        grad_output = attn_shard[:, 3 * part :].reshape(own, width).astype(f32)
    return (
        outputs,
        grad_inputs,
        *grad_mats,
        grad_output,
        grad_gains[0],
        grad_gains[1],
        grad_gains[2],
        *gate_out,
        *up_out,
        *down_out,
        grad_gains[3],
    )


def solution(mesh):
    both = ("leaf", "row")
    token_spec, tree_spec, matrix_spec, gain_spec = P("leaf", "row", None), P("leaf", None), P(both, None), P(both)
    return jax.shard_map(
        body,
        mesh=mesh,
        in_specs=(token_spec,) * 2 + (tree_spec,) * 2 + (matrix_spec,) * 4 + (gain_spec,) * 3 + (matrix_spec,) * 3 + (gain_spec,),
        out_specs=(token_spec,) * 2 + (matrix_spec,) * 4 + (gain_spec,) * 3 + (matrix_spec,) * 3 + (gain_spec,),
        check_vma=False,
    )
```
